32 devices in a mesh: stream: 4 (over z), span: 2 (over x), wall: 4 (over y, core).
Axes of the slice: x: 2, y: 2, z: 4, core: 2. Of those that a mesh axis runs over, the one named last changes fastest.
Arguments:
- adj_init: float32 [17, 48, 32, 256], P(None, 'stream', 'wall', 'span'), may hold values from -1.2 to 1.2
- adj_source: float32 [17, 48, 32, 256], P(None, 'stream', 'wall', 'span'), may hold values from -12 to 12
- velocity: float32 [3, 48, 32, 256], P(None, 'stream', 'wall', 'span'), may hold values from -4 to 4
- sound: float32 [48, 32, 256], P('stream', 'wall', 'span'), may hold values from 0.5 to 2
- face_couple: float32 [3, 2, 17, 17], replicated, may hold values from -0.36 to 0.36
- precond_inv: float32 [17, 17], replicated, may hold values from -0.3 to 1.3
- wall_code: int32 [48, 256], replicated, may hold values from 0 to 3
- spall_mask: int32 [48, 256], replicated, may hold values 0 or 1
- wall_table: float32 [4, 17], replicated, may hold values from 0.5 to 2
- spall_gain: float32 [17], replicated, may hold values from 0.5 to 3
Outputs:
- adjoint_out: float32 [17, 48, 32, 256], P(None, 'stream', 'wall', 'span')
- residual_out: float32 [17, 48, 32, 256], P(None, 'stream', 'wall', 'span')
The draws below stay inside these ranges and needn't reach their ends.
All inputs are finite; a program needn't handle non-finite values.
Results may differ from the reference program's by a relative error of at most 0.00015.
Values sent between devices are 32-bit elements; how exact they have to be, the bound alone decides.
No kernel may reach another device: no remote copies, remote signals or barrier semaphores. Data moves between devices by JAX's collectives and lax.ppermute only.
A program may use at most 128 MiB of HBM per device.

```python
import math
import jax
import jax.numpy as jnp
from jax import lax

NV = 17
KINDS = 4
SWEEPS = 2
NX = 48
NW = 32
NS = 256


def draw_precond_inv(key, part):
    first_key, second_key = jax.random.split(key)
    row_ids = jnp.arange(NV)
    identity = (row_ids[:, None] == row_ids[None, :]).astype(jnp.float32)
    diagonal_part = jax.random.uniform(first_key, (NV, NV), jnp.float32, 0.7, 1.3)
    off_part = jnp.clip(0.08 * jax.random.normal(second_key, (NV, NV), jnp.float32), -0.3, 0.3)
    return identity * diagonal_part + (1.0 - identity) * off_part


def touch_ends(entries, stream_key, low, high):
    longest = entries.shape.index(max(entries.shape))
    spots = []
    for shift in (0, 1):
        where = [jax.random.randint(jax.random.fold_in(stream_key, axis), (), 0, length) for axis, length in enumerate(entries.shape)]
        where[longest] = (where[longest] + shift) % entries.shape[longest]
        spots.append(tuple(where))
    return entries.at[spots[0]].set(low).at[spots[1]].set(high)


def levels(rng, dims, pieces, smallest, largest):
    factor_of = 1.0
    for axis_at, parts in pieces:
        heights = jax.random.uniform(jax.random.fold_in(jax.random.fold_in(rng, 6), axis_at), (parts,), jnp.float32, smallest / len(pieces), largest / len(pieces))
        factor_of = factor_of * jnp.repeat(jnp.exp(heights), dims[axis_at] // parts).reshape((-1,) + (1,) * (len(dims) - 1 - axis_at))
    return factor_of


def centred(rng, shape, width, bound, pieces=(), kind=jnp.bfloat16):
    gain = levels(rng, shape, pieces, -0.22, 0.18) if pieces else 1.0
    values = jax.random.normal(rng, shape, jnp.float32) * width * gain
    return jnp.minimum(jnp.maximum(values, -bound), bound).astype(kind)


def setup_inputs(seed: int = 0) -> dict:
    splits = jax.random.split(jax.random.key(seed), 11)
    adj_init = centred(splits[0], (NV, NX, NW, NS), 0.2, 1.2, ((1, 4), (2, 4), (3, 2)), jnp.float32)
    adj_source = centred(splits[1], (NV, NX, NW, NS), 2.0, 12.0, ((1, 4), (2, 4), (3, 2)), jnp.float32)
    velocity = centred(splits[2], (3, NX, NW, NS), 1.0, 4.0, ((1, 4), (2, 4), (3, 2)), jnp.float32)
    sound = jnp.clip(jnp.exp(math.log(2.0) - 1.3862944 * jax.random.uniform(splits[3], (NX, NW, NS), jnp.float32) ** levels(splits[3], (NX, NW, NS), ((0, 4), (1, 4), (2, 2)), -0.2, 0.2)), 0.5, 2.0)
    face_couple = centred(splits[4], (3, 2, NV, NV), 0.06, 0.36, (), jnp.float32)
    precond_inv = draw_precond_inv(jax.random.fold_in(splits[10], 71), 0)
    wall_code = touch_ends(jax.random.randint(splits[6], (NX, NS), 0, 4), jax.random.fold_in(splits[6], 1), 0, 3).astype(jnp.int32)
    spall_mask = touch_ends((jax.random.randint(splits[7], (NX, NS), 0, 4) < 1).astype(jnp.int32), jax.random.fold_in(splits[7], 1), 0, 1)
    wall_table = jnp.clip(jnp.exp(jax.random.uniform(splits[8], (KINDS, NV), jnp.float32, math.log(0.5), math.log(2.0))), 0.5, 2.0)
    spall_gain = jnp.clip(jnp.exp(jax.random.uniform(splits[9], (NV,), jnp.float32, math.log(0.5), math.log(3.0))), 0.5, 3.0)
    return dict(adj_init=adj_init, adj_source=adj_source, velocity=velocity, sound=sound, face_couple=face_couple, precond_inv=precond_inv, wall_code=wall_code, spall_mask=spall_mask, wall_table=wall_table, spall_gain=spall_gain)


def shifted(field, direction, facing):
    if direction == 2:
        return jnp.roll(field, 1 if facing == 0 else -1, axis=3)
    widths = [(0, 0), (0, 0), (0, 0), (0, 0)]
    widths[direction + 1] = (1, 1)
    padded = jnp.pad(field, widths)
    if direction == 0:
        return padded[:, :-2] if facing == 0 else padded[:, 2:]
    return padded[:, :, :-2] if facing == 0 else padded[:, :, 2:]


def make_wall_coef(wall_code, spall_mask, wall_table, spall_gain):
    kinds_ids = jnp.arange(wall_table.shape[0], dtype=jnp.int32)
    onehot = (wall_code[None] == kinds_ids[:, None, None]).astype(jnp.float32)
    table_part = jnp.einsum('ki,krc->irc', wall_table, onehot, precision=lax.Precision.HIGHEST)
    return table_part + spall_gain[:, None, None] * spall_mask.astype(jnp.float32)[None]


def reference(adj_init, adj_source, velocity, sound, face_couple, precond_inv, wall_code, spall_mask, wall_table, spall_gain):
    radius = jnp.abs(velocity) + sound[None]
    wall_coef = make_wall_coef(wall_code, spall_mask, wall_table, spall_gain)
    adjoint = adj_init
    residual = adj_source
    for sweep_index in range(SWEEPS):
        rate_sum = jnp.ones_like(radius[0])
        flow_sum = jnp.zeros_like(adjoint)
        for direction in range(3):
            for facing in range(2):
                face_rate = 0.5 * (radius[direction] + shifted(radius, direction, facing)[direction])
                coupled = jnp.einsum('ji,jxyz->ixyz', face_couple[direction, facing], shifted(adjoint, direction, facing), precision=lax.Precision.HIGHEST)
                flow_sum = flow_sum + face_rate[None] * coupled
                rate_sum = rate_sum + face_rate
        residual = adj_source - rate_sum[None] * adjoint - flow_sum
        wall_term = radius[1][:, 0, :][None] * wall_coef * adjoint[:, :, 0, :]
        residual = residual.at[:, :, 0, :].add(-wall_term)
        update = jnp.einsum('ij,jxyz->ixyz', precond_inv, residual, precision=lax.Precision.HIGHEST)
        adjoint = adjoint + update / rate_sum[None]
    return adjoint, residual
```

```python
import functools

import jax
import jax.numpy as jnp
import numpy as np
from jax import lax
from jax.experimental import pallas as pl
from jax.experimental.pallas import tpu as pltpu
from jax.sharding import PartitionSpec as P

AXES = ("stream", "span", "wall")
F32 = jnp.float32
BF16 = jnp.bfloat16
HIGHEST = lax.Precision.HIGHEST


class Dims:
    def __init__(self, shape):
        self.V, self.X, self.W, self.Z = shape
        self.G = self.V + 1
        while self.G * self.W % 16:
            self.G += 1
        self.B = self.G * self.W
        self.rows = self.V * self.X * self.W
        self.wall_rows = self.X * self.G + 8
        self.wall_k = -(-self.G // 8) * 8
        self.per = self.Z // (2 * self.X)
        self.span_groups = -(-(self.V + 1) // self.per)

    def block(self, group, x):
        return pl.ds((group * self.X + x) * self.W, self.W)

    def plane(self, ref, x):
        return jnp.concatenate([ref[self.block(v, x), :] for v in range(self.V)], axis=0)

    def store_plane(self, ref, x, value):
        for v in range(self.V):
            ref[self.block(v, x), :] = value[v * self.W : (v + 1) * self.W]

    def each(self, factor):
        return jnp.concatenate([factor] * self.V, axis=0)


def lanes(d, rows):
    return lax.broadcasted_iota(jnp.int32, (rows, d.Z), 1)


def row_ids(d):
    return lax.broadcasted_iota(jnp.int32, (d.W, d.Z), 0)


def radius_at(d, vel, snd, direction, x):
    return jnp.abs(vel[d.block(direction, x), :]) + snd[d.block(0, x), :]


def split3(value):
    high = value.astype(BF16)
    low = (value - high.astype(F32)).astype(BF16)
    return jnp.concatenate([high, low, high], axis=0)


def padded_plane(d, value):
    extra = d.B - value.shape[0]
    if not extra:
        return value
    return jnp.concatenate([value, jnp.zeros((extra, value.shape[1]), F32)], axis=0)


def dot(a, b):
    return jnp.dot(a, b, preferred_element_type=F32)


def pack_faces(d, block_of, radius_of, rows_of, even_s, even_w, s_a, s_b, w_a, w_b, z_out):
    V, X, W, Z, G = d.V, d.X, d.W, d.Z, d.G
    zero = jnp.zeros((W, Z), F32)
    for g in range(G):
        if g < V:
            first, last = block_of(g, 0), block_of(g, X - 1)
        elif g == V and radius_of is not None:
            first, last = radius_of(0, 0), radius_of(0, X - 1)
        else:
            first = last = zero
        s_a[g * W : (g + 1) * W, :] = jnp.where(even_s, last, first)
        s_b[g * W : (g + 1) * W, :] = jnp.where(even_s, first, last)
    tail = jnp.zeros((G - V, Z), F32)
    for x in range(X):
        first, last = rows_of(x, 0), rows_of(x, W - 1)
        w_a[x * G : x * G + V, :] = jnp.where(even_w, last, first)
        w_b[x * G : x * G + V, :] = jnp.where(even_w, first, last)
        w_a[x * G + V : (x + 1) * G, :] = tail
        w_b[x * G + V : (x + 1) * G, :] = tail
        if radius_of is not None:
            radius = radius_of(1, x)
            first, last = radius[:1], radius[W - 1 :]
            w_a[x * G + V : x * G + V + 1, :] = jnp.where(even_w, last, first)
            w_b[x * G + V : x * G + V + 1, :] = jnp.where(even_w, first, last)
    w_a[X * G :, :] = jnp.zeros((8, Z), F32)
    w_b[X * G :, :] = jnp.zeros((8, Z), F32)
    pair = lanes(d, W) // 2
    groups = [zero] * d.span_groups
    for x in range(X):
        for v in range(V + 1):
            if v < V:
                value = block_of(v, x)
            elif radius_of is not None:
                value = radius_of(2, x)
            else:
                continue
            spot = X * (v % d.per) + x
            moved = pltpu.roll(value, (2 * spot + 1) % Z, 1)
            groups[v // d.per] = jnp.where(pair == spot, moved, groups[v // d.per])
    for q in range(d.span_groups):
        z_out[q * W : (q + 1) * W, :] = groups[q]


def parity(axis):
    return lax.rem(lax.axis_index(axis), 2) == 0


def pack_kernel(d, adj, vel, snd, s_a, s_b, w_a, w_b, z_out):
    pack_faces(
        d,
        lambda v, x: adj[d.block(v, x), :],
        functools.partial(radius_at, d, vel, snd),
        lambda x, w: adj[pl.ds(x * d.W + w, d.V, stride=d.X * d.W), :],
        parity("stream"),
        parity("wall"),
        s_a,
        s_b,
        w_a,
        w_b,
        z_out,
    )


def make_matrices(d, couple, precond, mk, mw, pk):
    V, W, B = d.V, d.W, d.B
    K = d.wall_k
    row = lax.broadcasted_iota(jnp.int32, (B, 3 * B), 0)
    col = lax.broadcasted_iota(jnp.int32, (B, 3 * B), 1)
    shift = lax.rem(col, W) - lax.rem(row, W)
    same, lower, upper = shift == 0, shift == -1, shift == 1
    spread = lax.broadcasted_iota(jnp.int32, (B, V), 0) // W
    spread = (spread == lax.broadcasted_iota(jnp.int32, (B, V), 1)).astype(BF16)
    down = lax.broadcasted_iota(jnp.int32, (2 * V, 3 * B), 0)
    across = lax.broadcasted_iota(jnp.int32, (2 * V, 3 * B), 1)
    wide_high = (lax.rem(across, B) // W == down) & (across < 2 * B) & (down < V)
    wide_low = (lax.rem(across, B) // W == down - V) & (across >= 2 * B)
    wide = (wide_high | wide_low).astype(BF16)

    def halves(m, contract):
        high = m.astype(BF16)
        low = (m - high.astype(F32)).astype(BF16)
        dims = (((1,), (contract,)), ((), ()))
        parts = [lax.dot_general(spread, p, dims, preferred_element_type=F32) for p in (high, low)]
        return jnp.concatenate(parts, axis=1).astype(BF16)

    def spread_out(parts, mask):
        return jnp.where(mask, dot(parts, wide), 0.0).astype(BF16)

    couples = [halves(couple[n], 1) for n in range(6)]
    for n in range(6):
        mk[n * B : (n + 1) * B, :] = spread_out(couples[n], {2: lower, 3: upper}.get(n, same))
    pk[...] = spread_out(halves(precond[...], 0), same)
    down = lax.broadcasted_iota(jnp.int32, (2 * V, 6 * K), 0)
    across = lax.broadcasted_iota(jnp.int32, (2 * V, 6 * K), 1)
    wide_high = (lax.rem(across, K) == down) & (across < 4 * K) & (down < V)
    wide_low = (lax.rem(across, K) == down - V) & (across >= 4 * K)
    wide = (wide_high | wide_low).astype(BF16)
    row = lax.rem(lax.broadcasted_iota(jnp.int32, (B, 6 * K), 0), W)
    side = lax.rem(lax.broadcasted_iota(jnp.int32, (B, 6 * K), 1) // K, 2)
    low_side = jnp.where((row == 0) & (side == 0), dot(couples[2], wide), 0.0)
    high_side = jnp.where((row == W - 1) & (side == 1), dot(couples[3], wide), 0.0)
    mw[...] = (low_side + high_side).astype(BF16)


def make_wall(d, codes, mask, table, gain, wall_out):
    X, Z = d.X, d.Z
    place = lax.axis_index("stream")
    lane0 = pl.multiple_of(lax.axis_index("span") * Z, Z)
    kinds = table.shape[0]

    def window(ref):
        value = ref[:X, pl.ds(lane0, Z)]
        for s in range(1, lax.axis_size("stream")):
            value = jnp.where(place == s, ref[s * X : (s + 1) * X, pl.ds(lane0, Z)], value)
        return value

    code, spall = window(codes), window(mask).astype(F32)
    pieces = []
    for x in range(X):
        here = code[x : x + 1]
        pieces.append(
            jnp.concatenate(
                [(here == k).astype(F32) for k in range(kinds)] + [spall[x : x + 1]], axis=0
            )
        )
    hot = jnp.concatenate(pieces, axis=1)
    full = jnp.concatenate([table[...], gain[...]], axis=0)
    wall_out[...] = lax.dot_general(
        full, hot, (((0,), (0,)), ((), ())), precision=HIGHEST, preferred_element_type=F32
    )


def sweep_local(d, adj, src, vel, snd, mk, wall_coef, rates_of, out, rs_out):
    V, X, W, Z, B = d.V, d.X, d.W, d.Z, d.B
    n = V * W
    lane, row = lanes(d, W), row_ids(d)
    wall_flag = (lax.axis_index("wall") == 0).astype(F32)
    radius = [[radius_at(d, vel, snd, k, x) for x in range(X)] for k in range(3)]
    step = 2
    products = {}

    def product(x, k):
        chunk, offset = products[x]
        return chunk[k * B : k * B + n, offset * Z : (offset + 1) * Z]

    def finish(x):
        a = d.plane(adj, x)
        total = 1.0
        terms = []
        half = [0.5 * radius[k][x] for k in range(3)]
        for k, neighbour in ((0, x - 1), (1, x + 1)):
            rate = half[0]
            if 0 <= neighbour < X:
                rate = rate + 0.5 * radius[0][neighbour]
                terms.append((rate, product(neighbour, k)))
            total = total + rate
        for k, edge, turn in ((2, 0, 1), (3, W - 1, W - 1)):
            near = jnp.where(row == edge, 0.0, pltpu.roll(half[1], turn, 0))
            rate = half[1] + near
            terms.append((rate, product(x, k)))
            total = total + rate
        for k, edge, turn in ((4, 0, 1), (5, Z - 1, Z - 1)):
            near = jnp.where(lane == edge, 0.0, pltpu.roll(half[2], turn, 1))
            total = total + half[2] + near
            rate = jnp.where(lane == edge, 0.0, half[2] + near)
            terms.append((rate, pltpu.roll(product(x, k), turn, 1)))
        if rates_of is None:
            rs_out[d.block(0, x), :] = total
        else:
            total = rates_of[d.block(0, x), :]
        result = d.plane(src, x) - d.each(total) * a
        for rate, value in terms:
            result = result - d.each(rate) * value
        d.store_plane(out, x, result)
        spot = pl.ds(x * W, V, stride=X * W)
        factor = wall_flag * radius[1][x][:1]
        coef = wall_coef[:, x * Z : (x + 1) * Z]
        out[spot, :] = out[spot, :] - factor * coef * adj[spot, :]

    done = 0
    for start in range(0, X, step):
        here = list(range(start, min(X, start + step)))
        right = jnp.concatenate([padded_plane(d, d.plane(adj, x)) for x in here], axis=1)
        chunk = dot(mk[...], split3(right))
        for offset, x in enumerate(here):
            products[x] = (chunk, offset)
        while done < X and (done + 1 in products or (done + 1 == X and done in products)):
            finish(done)
            done += 1


def first_local_kernel(
    d, adj, src, vel, snd, couple, precond, codes, mask, table, gain, out, rs, mk, mw, pk, wall_coef
):
    make_matrices(d, couple, precond, mk, mw, pk)
    make_wall(d, codes, mask, table, gain, wall_coef)
    sweep_local(d, adj, src, vel, snd, mk, wall_coef, None, out, rs)


def later_local_kernel(d, adj, src, vel, snd, rs, mk, wall_coef, out):
    sweep_local(d, adj, src, vel, snd, mk, wall_coef, rs, out, None)


def halo_terms(d, s0, s1, w0, w1, zl, zr, mk, mw):
    V, X, W, Z, G, B = d.V, d.X, d.W, d.Z, d.G, d.B
    n = V * W
    even_s, even_w = parity("stream"), parity("wall")
    si, wi = lax.axis_index("stream"), lax.axis_index("wall")
    has = lambda flag: flag.astype(F32)
    s_low, s_high = has(si > 0), has(si < lax.axis_size("stream") - 1)
    w_low, w_high = has(wi > 0), has(wi < lax.axis_size("wall") - 1)
    low = jnp.where(even_s, s1[...], s0[...]) * s_low
    high = jnp.where(even_s, s0[...], s1[...]) * s_high
    stream = (dot(mk[:B], split3(low))[:n], dot(mk[B : 2 * B], split3(high))[:n])
    stream_radius = (low[n : n + W], high[n : n + W])

    def wall_rows(x):
        rows = pl.ds(x * G, d.wall_k)
        a, b = w0[rows, :], w1[rows, :]
        return jnp.where(even_w, b, a) * w_low, jnp.where(even_w, a, b) * w_high

    def wall(x):
        return jnp.concatenate(wall_rows(x), axis=0)

    row = row_ids(d)

    def wall_radius(x):
        rows = pl.ds(x * G + V, 1)
        a, b = w0[rows, :], w1[rows, :]
        first = jnp.where(even_w, b, a) * w_low
        last = jnp.where(even_w, a, b) * w_high
        return jnp.where(row == 0, first, jnp.where(row == W - 1, last, 0.0))

    even = lax.rem(lanes(d, W), 2) == 0
    pieces = []
    for v in range(V + 1):
        q = pl.ds((v // d.per) * W, W)
        value = jnp.where(even, zl[q, :], zr[q, :])
        turn = (Z - 2 * X * (v % d.per)) % Z
        pieces.append(pltpu.roll(value, turn, 1) if turn else value)
    span_radius = jnp.where(even, pieces[V], pltpu.roll(pieces[V], Z - 2, 1))
    pieces += [jnp.zeros((W, Z), F32)] * (G - V - 1)
    both = dot(mk[4 * B : 6 * B], split3(jnp.concatenate(pieces, axis=0)))
    even = lax.rem(lanes(d, n), 2) == 0
    span = jnp.where(even, both[:n], pltpu.roll(both[B : B + n], Z - 2, 1))
    at = lambda value, x: pltpu.roll(value, (Z - 2 * x) % Z, 1) if x else value
    return (
        stream,
        stream_radius,
        wall,
        wall_radius,
        lambda x: at(span, x),
        lambda x: at(span_radius, x),
    )


def finish_sweep(d, partial, adj, rs_of, halo_rates, corrections, halo, mw, pk, put):
    V, X, W, Z = d.V, d.X, d.W, d.Z
    n = V * W
    stream, _, wall, _, span, _ = halo
    for start in range(0, X, 2):
        here = list(range(start, min(X, start + 2)))
        from_wall = dot(mw[...], split3(jnp.concatenate([wall(x) for x in here], axis=1)))
        residuals = []
        for k, x in enumerate(here):
            low, high, rate_wall, rate_span = halo_rates(x)
            res = d.plane(partial, x)
            if corrections is not None:
                res = res - d.each(corrections(x)) * d.plane(adj, x)
            res = res - d.each(rate_wall) * from_wall[:n, k * Z : (k + 1) * Z]
            res = res - d.each(rate_span) * span(x)
            if low is not None:
                res = res - d.each(low) * stream[0]
            if high is not None:
                res = res - d.each(high) * stream[1]
            residuals.append(res)
        right = jnp.concatenate([padded_plane(d, r) for r in residuals], axis=1)
        update = dot(pk[...], split3(right))
        for k, x in enumerate(here):
            inverse = 1.0 / rs_of(x)
            new = d.plane(adj, x) + update[:n, k * Z : (k + 1) * Z] * d.each(inverse)
            put(x, new, residuals[k])


def first_halo_kernel(
    d, partial, adj, rs, vel, snd, s0, s1, w0, w1, zl, zr, mk, mw, pk,
    new_adj, rs_full, rates, s_a, s_b, w_a, w_b, z_out,
):
    X, W, Z = d.X, d.W, d.Z
    halo = halo_terms(d, s0, s1, w0, w1, zl, zr, mk, mw)
    _, stream_radius, _, wall_radius, _, span_radius = halo
    lane, row = lanes(d, W), row_ids(d)
    edge_lane = (lane == 0) | (lane == Z - 1)
    edge_row = (row == 0) | (row == W - 1)
    kept = {}
    for x in range(X):
        from_wall = 0.5 * wall_radius(x)
        from_span = jnp.where(edge_lane, 0.5 * span_radius(x), 0.0)
        rate_wall = jnp.where(edge_row, 0.5 * radius_at(d, vel, snd, 1, x) + from_wall, 0.0)
        rate_span = jnp.where(edge_lane, 0.5 * radius_at(d, vel, snd, 2, x) + from_span, 0.0)
        correction = from_wall + from_span
        low = high = None
        if x == 0:
            correction = correction + 0.5 * stream_radius[0]
            low = 0.5 * (radius_at(d, vel, snd, 0, x) + stream_radius[0])
            rates[d.block(2, 0), :] = low
        if x == X - 1:
            correction = correction + 0.5 * stream_radius[1]
            high = 0.5 * (radius_at(d, vel, snd, 0, x) + stream_radius[1])
            rates[d.block(2, 1 % X) if X > 1 else pl.ds((2 * X + 1) * W, W), :] = high
        rates[d.block(0, x), :] = rate_wall
        rates[d.block(1, x), :] = rate_span
        total = rs[d.block(0, x), :] + correction
        rs_full[d.block(0, x), :] = total
        kept[x] = (correction, total, (low, high, rate_wall, rate_span))

    def put(x, new, _):
        d.store_plane(new_adj, x, new)

    finish_sweep(
        d, partial, adj, lambda x: kept[x][1], lambda x: kept[x][2], lambda x: kept[x][0],
        halo, mw, pk, put,
    )
    pack_faces(
        d,
        lambda v, x: new_adj[d.block(v, x), :],
        None,
        lambda x, w: new_adj[pl.ds(x * W + w, d.V, stride=X * W), :],
        parity("stream"),
        parity("wall"),
        s_a, s_b, w_a, w_b, z_out,
    )


def last_halo_kernel(
    d, partial, adj, rs_full, rates, s0, s1, w0, w1, zl, zr, mk, mw, pk, new_adj, residual
):
    X, W = d.X, d.W
    halo = halo_terms(d, s0, s1, w0, w1, zl, zr, mk, mw)

    def halo_rates(x):
        low = rates[pl.ds(2 * X * W, W), :] if x == 0 else None
        high = rates[pl.ds((2 * X + 1) * W, W), :] if x == X - 1 else None
        return low, high, rates[d.block(0, x), :], rates[d.block(1, x), :]

    def put(x, new, res):
        d.store_plane(new_adj, x, new)
        d.store_plane(residual, x, res)

    finish_sweep(
        d, partial, adj, lambda x: rs_full[d.block(0, x), :], halo_rates, None, halo, mw, pk, put
    )


def exchange_pairs(sizes, axis, odd, spare):
    ids = np.arange(int(np.prod(sizes))).reshape(sizes)
    pairs = []
    for at in np.ndindex(*sizes):
        to = list(at)
        step = 1 if (at[axis] - odd) % 2 == 0 else -1
        if at[axis] >= odd and 0 <= at[axis] + step < sizes[axis]:
            to[axis] += step
        elif (at[spare] ^ 1) < sizes[spare]:
            to[spare] ^= 1
        else:
            continue
        pairs.append((int(ids[at]), int(ids[tuple(to)])))
    return pairs


def swap_lines(sizes, s_a, s_b, w_a, w_b, z):
    move = lambda value, pairs: lax.ppermute(value, AXES, pairs)
    s0 = move(s_a, exchange_pairs(sizes, 0, 0, 2))
    s1 = move(s_b, exchange_pairs(sizes, 0, 1, 2))
    w1 = move(w_b, exchange_pairs(sizes, 2, 1, 1))
    w0 = move(w_a, exchange_pairs(sizes, 2, 0, 1))
    peers = sizes[1]
    if peers == 1:
        zl = zr = z
    elif peers == 2:
        zl = zr = lax.ppermute(z, "span", [(0, 1), (1, 0)])
    else:
        up = [(i, (i + 1) % peers) for i in range(peers)]
        zl = lax.ppermute(z, "span", up)
        zr = lax.ppermute(z, "span", [(j, i) for i, j in up])
    return s0, s1, w0, w1, zl, zr


def call(kernel, d, outs, flops, args, in_vmem=True, out_vmem=True):
    name = kernel.__name__
    if out_vmem:
        shapes = tuple(pltpu.VMEM(s, t) for s, t in outs)
    else:
        shapes = tuple(jax.ShapeDtypeStruct(s, t) for s, t in outs)
    if in_vmem:
        args = [pltpu.with_memory_space_constraint(a, pltpu.VMEM) for a in args]
    moved = sum(int(np.prod(a.shape)) * a.dtype.itemsize for a in args)
    return pl.pallas_call(
        functools.partial(kernel, d),
        out_shape=shapes,
        in_specs=[pl.BlockSpec(memory_space=pltpu.VMEM)] * len(args),
        out_specs=tuple(pl.BlockSpec(memory_space=pltpu.VMEM) for _ in outs),
        compiler_params=pltpu.CompilerParams(vmem_limit_bytes=24 * 2**20),
        cost_estimate=pl.CostEstimate(flops=flops, bytes_accessed=moved, transcendentals=0),
        name=name,
    )(*args)


def on_device(sizes, adj, source, velocity, sound, couple, precond, codes, mask, table, gain):
    shape = adj.shape
    d = Dims(shape)
    X, W, Z, B = d.X, d.W, d.Z, d.B
    adj = adj.reshape(d.rows, Z)
    source = source.reshape(d.rows, Z)
    velocity = velocity.reshape(3 * X * W, Z)
    sound = sound.reshape(X * W, Z)
    couple = couple.reshape((6,) + couple.shape[2:])
    gain = gain.reshape(1, -1)
    vmem = lambda a: pltpu.with_memory_space_constraint(a, pltpu.VMEM)

    faces = [((B, Z), F32)] * 2 + [((d.wall_rows, Z), F32)] * 2 + [((d.span_groups * W, Z), F32)]
    field, scalar = ((d.rows, Z), F32), ((X * W, Z), F32)
    packets = call(pack_kernel, d, faces, 0, [adj, velocity, sound])
    got = swap_lines(sizes, *packets)
    partial, rs, mk, mw, pk, wall_coef = call(
        first_local_kernel,
        d,
        [
            field,
            scalar,
            ((6 * B, 3 * B), BF16),
            ((B, 6 * d.wall_k), BF16),
            ((B, 3 * B), BF16),
            ((d.V, X * Z), F32),
        ],
        10**9,
        [adj, source, velocity, sound, couple, precond, codes, mask, table, gain],
    )
    adj1, rs_full, rates, *packets = call(
        first_halo_kernel,
        d,
        [field, scalar, ((2 * (X + 1) * W, Z), F32)] + faces,
        10**8,
        [partial, adj, rs, velocity, sound, *got, mk, mw, pk],
    )
    got = swap_lines(sizes, *packets)
    (partial,) = call(
        later_local_kernel, d, [field], 10**9, [adj1, source, velocity, sound, rs_full, mk, wall_coef]
    )
    adj2, residual = call(
        last_halo_kernel,
        d,
        [field, field],
        10**8,
        [partial, adj1, rs_full, rates, *got, mk, mw, pk],
        out_vmem=False,
    )
    return adj2.reshape(shape), residual.reshape(shape)


def solution(mesh):
    sizes = tuple(mesh.shape[a] for a in AXES)
    field = P(None, "stream", "wall", "span")
    return jax.shard_map(
        functools.partial(on_device, sizes),
        mesh=mesh,
        in_specs=(field, field, field, P("stream", "wall", "span")) + (P(),) * 6,
        out_specs=(field, field),
        check_vma=False,
    )
```

```python
import functools

import jax
import jax.numpy as jnp
import numpy as np
from jax import lax
from jax.experimental import pallas as pl
from jax.experimental.pallas import tpu as pltpu
from jax.sharding import PartitionSpec as P

AXES = ("stream", "span", "wall")
F32 = jnp.float32
BF16 = jnp.bfloat16
HIGHEST = lax.Precision.HIGHEST
STORE = 6


class Dims:
    def __init__(self, shape):
        self.V, self.X, self.W, self.Z = shape
        self.G = self.V + 1
        while self.G * self.W % 16:
            self.G += 1
        self.B = self.G * self.W
        self.n = self.V * self.W
        self.rows = self.n * self.X
        self.wall_rows = self.X * self.G + 8
        self.wall_k = -(-self.G // 8) * 8
        self.per = self.Z // (2 * self.X)
        self.span_groups = -(-(self.V + 1) // self.per)

    def block(self, group, x):
        return pl.ds((group * self.X + x) * self.W, self.W)

    def plane(self, ref, x):
        return jnp.concatenate([ref[self.block(v, x), :] for v in range(self.V)], axis=0)

    def store_plane(self, ref, x, value):
        for v in range(self.V):
            ref[self.block(v, x), :] = value[v * self.W : (v + 1) * self.W]

    def plane3(self, ref, x):
        return ref[:, x * self.W : (x + 1) * self.W, :].reshape(self.n, self.Z)

    def planes_at(self, start, count):
        return (slice(None), pl.ds(start * self.W, count * self.W), slice(None))

    def each(self, factor):
        return jnp.concatenate([factor] * self.V, axis=0)


def lanes(d, rows):
    return lax.broadcasted_iota(jnp.int32, (rows, d.Z), 1)


def row_ids(d):
    return lax.broadcasted_iota(jnp.int32, (d.W, d.Z), 0)


def radius_at(d, vel, snd, direction, x):
    return jnp.abs(vel[d.block(direction, x), :]) + snd[d.block(0, x), :]


def split3(value):
    high = value.astype(BF16)
    low = (value - high.astype(F32)).astype(BF16)
    return jnp.concatenate([high, low, high], axis=0)


def padded_plane(d, value):
    extra = d.B - value.shape[0]
    if not extra:
        return value
    return jnp.concatenate([value, jnp.zeros((extra, value.shape[1]), F32)], axis=0)


def dot(a, b):
    return jnp.dot(a, b, preferred_element_type=F32)


def pack_faces(
    d, block_of, radius_of, rows_of, even_s, even_w, s_a, s_b, w_a, w_b, z_out
):
    V, X, W, Z, G = d.V, d.X, d.W, d.Z, d.G
    zero = jnp.zeros((W, Z), F32)
    pair = lanes(d, W) // 2
    groups = [zero] * d.span_groups

    def span_columns(v, x, value):
        spot = X * (v % d.per) + x
        moved = pltpu.roll(value, (2 * spot + 1) % Z, 1)
        groups[v // d.per] = jnp.where(pair == spot, moved, groups[v // d.per])

    for g in range(G):
        if g < V:
            first, last = block_of(g, 0), block_of(g, X - 1)
            for x in range(X):
                span_columns(g, x, block_of(g, x))
        elif g == V and radius_of is not None:
            first, last = radius_of(0, 0), radius_of(0, X - 1)
            for x in range(X):
                span_columns(V, x, radius_of(2, x))
        else:
            first = last = zero
        s_a[g * W : (g + 1) * W, :] = jnp.where(even_s, last, first)
        s_b[g * W : (g + 1) * W, :] = jnp.where(even_s, first, last)
    for q in range(d.span_groups):
        z_out[q * W : (q + 1) * W, :] = groups[q]
    tail = jnp.zeros((G - V, Z), F32)
    for x in range(X):
        first, last = rows_of(x, 0), rows_of(x, W - 1)
        w_a[x * G : x * G + V, :] = jnp.where(even_w, last, first)
        w_b[x * G : x * G + V, :] = jnp.where(even_w, first, last)
        if radius_of is None or G - V > 1:
            w_a[x * G + V : (x + 1) * G, :] = tail
            w_b[x * G + V : (x + 1) * G, :] = tail
        if radius_of is not None:
            radius = radius_of(1, x)
            first, last = radius[:1], radius[W - 1 :]
            w_a[x * G + V : x * G + V + 1, :] = jnp.where(even_w, last, first)
            w_b[x * G + V : x * G + V + 1, :] = jnp.where(even_w, first, last)
    w_a[X * G :, :] = jnp.zeros((8, Z), F32)
    w_b[X * G :, :] = jnp.zeros((8, Z), F32)


def parity(axis):
    return lax.rem(lax.axis_index(axis), 2) == 0


def pack_kernel(d, *refs):
    count = (len(refs) - 6) // 2
    held, kept = refs[:count], refs[count : 2 * count]
    s_a, s_b, w_a, w_b, z_out, sems = refs[2 * count :]
    adj, vel, snd = kept[:3]
    copies = [pltpu.make_async_copy(held[k], kept[k], sems.at[k]) for k in range(count)]
    for copy in copies:
        copy.start()
    for copy in copies:
        copy.wait()
    pack_faces(
        d,
        lambda v, x: adj[d.block(v, x), :],
        functools.partial(radius_at, d, vel, snd),
        lambda x, w: adj[pl.ds(x * d.W + w, d.V, stride=d.X * d.W), :],
        parity("stream"),
        parity("wall"),
        s_a,
        s_b,
        w_a,
        w_b,
        z_out,
    )


def make_matrices(d, couple, precond, mk, mw, pk):
    V, W, B, n, K = d.V, d.W, d.B, d.n, d.wall_k
    stack = -(-V // 8) * 8

    def expand(m, contract, high_mask, low_mask):
        high = m.astype(BF16)
        low = (m - high.astype(F32)).astype(BF16)
        dims = (((contract,), (0,)), ((), ()))
        wide = lax.dot_general(high, high_mask, dims, preferred_element_type=F32)
        wide = wide + lax.dot_general(low, low_mask, dims, preferred_element_type=F32)
        extra = jnp.zeros((stack - V, wide.shape[1]), F32)
        return jnp.concatenate([wide, extra], axis=0) if stack > V else wide

    down = lax.broadcasted_iota(jnp.int32, (V, 3 * B), 0)
    across = lax.broadcasted_iota(jnp.int32, (V, 3 * B), 1)
    match = lax.rem(across, B) // W == down
    high_mask, low_mask = (match & (across < 2 * B)), (match & (across >= 2 * B))
    high_mask, low_mask = high_mask.astype(BF16), low_mask.astype(BF16)
    blocks = [(couple[k // 2, k % 2], 0) for k in range(6)] + [(precond[...], 1)]
    wide = [expand(m, contract, high_mask, low_mask) for m, contract in blocks]
    wide = jnp.concatenate(wide, axis=0).astype(BF16)
    lane = lax.broadcasted_iota(jnp.int32, (W, 7 * stack), 1)
    spread = [(lane == k * stack + v).astype(F32) for k in range(7) for v in range(V)]
    full = dot(jnp.concatenate(spread, axis=0).astype(BF16), wide)
    row = lax.broadcasted_iota(jnp.int32, (W, 3 * B), 0)
    col = lax.rem(lax.broadcasted_iota(jnp.int32, (W, 3 * B), 1), W)
    same, lower, upper = [(col - row == k).astype(F32) for k in (0, -1, 1)]
    for k in range(7):
        mask = {2: lower, 3: upper}.get(k, same)
        block = full[k * n : (k + 1) * n].reshape(V, W, 3 * B) * mask[None]
        block = block.reshape(n, 3 * B).astype(BF16)
        if k < 6:
            mk[k * n : (k + 1) * n, :] = block
        else:
            pk[...] = block
    down = lax.broadcasted_iota(jnp.int32, (V, 6 * K), 0)
    across = lax.broadcasted_iota(jnp.int32, (V, 6 * K), 1)
    match = lax.rem(across, K) == down
    side = lax.rem(across // K, 2)
    wide = [
        expand(
            couple[1, k],
            0,
            (match & (side == k) & (across < 4 * K)).astype(BF16),
            (match & (side == k) & (across >= 4 * K)).astype(BF16),
        )
        for k in range(2)
    ]
    wide = jnp.concatenate(wide, axis=0).astype(BF16)
    lane = lax.broadcasted_iota(jnp.int32, (W, 2 * stack), 1)
    row = lax.broadcasted_iota(jnp.int32, (W, 2 * stack), 0)
    spread = [
        (((lane == v) & (row == 0)) | ((lane == stack + v) & (row == W - 1))).astype(F32)
        for v in range(V)
    ]
    mw[...] = dot(jnp.concatenate(spread, axis=0).astype(BF16), wide).astype(BF16)


def make_wall(d, codes, mask, table, gain, wall_out):
    X, Z = d.X, d.Z
    place = lax.axis_index("stream")
    lane0 = pl.multiple_of(lax.axis_index("span") * Z, Z)
    kinds = table.shape[0]

    def window(ref):
        value = ref[:X, pl.ds(lane0, Z)]
        for s in range(1, lax.axis_size("stream")):
            value = jnp.where(place == s, ref[s * X : (s + 1) * X, pl.ds(lane0, Z)], value)
        return value

    code, spall = window(codes), window(mask).astype(F32)
    pieces = []
    for x in range(X):
        here = code[x : x + 1]
        pieces.append(
            jnp.concatenate(
                [(here == k).astype(F32) for k in range(kinds)] + [spall[x : x + 1]], axis=0
            )
        )
    hot = jnp.concatenate(pieces, axis=1)
    full = jnp.concatenate([table[...], gain[...]], axis=0)
    wall_out[...] = lax.dot_general(
        full, hot, (((0,), (0,)), ((), ())), precision=HIGHEST, preferred_element_type=F32
    )


def sweep_local(d, adj, src, vel, snd, mk, wall_coef, rates_of, out, rs_out):
    V, X, W, Z, n = d.V, d.X, d.W, d.Z, d.n
    lane, row = lanes(d, W), row_ids(d)
    wall_flag = (lax.axis_index("wall") == 0).astype(F32)
    radius = [[radius_at(d, vel, snd, k, x) for x in range(X)] for k in range(3)]
    step = 2
    products = {}

    def product(x, k):
        chunk, offset = products[x]
        return chunk[k * n : (k + 1) * n, offset * Z : (offset + 1) * Z]

    def finish(x):
        a = d.plane(adj, x)
        total = 1.0
        terms = []
        half = [0.5 * radius[k][x] for k in range(3)]
        for k, neighbour in ((0, x - 1), (1, x + 1)):
            rate = half[0]
            if 0 <= neighbour < X:
                rate = rate + 0.5 * radius[0][neighbour]
                terms.append((rate, product(neighbour, k)))
            total = total + rate
        for k, edge, turn in ((2, 0, 1), (3, W - 1, W - 1)):
            near = jnp.where(row == edge, 0.0, pltpu.roll(half[1], turn, 0))
            rate = half[1] + near
            terms.append((rate, product(x, k)))
            total = total + rate
        for k, edge, turn in ((4, 0, 1), (5, Z - 1, Z - 1)):
            near = jnp.where(lane == edge, 0.0, pltpu.roll(half[2], turn, 1))
            total = total + half[2] + near
            rate = jnp.where(lane == edge, 0.0, half[2] + near)
            terms.append((rate, pltpu.roll(product(x, k), turn, 1)))
        if rates_of is None:
            rs_out[d.block(0, x), :] = total
        else:
            total = rates_of[d.block(0, x), :]
        result = d.plane3(src, x) - d.each(total) * a
        for rate, value in terms:
            result = result - d.each(rate) * value
        d.store_plane(out, x, result)
        spot = pl.ds(x * W, V, stride=X * W)
        factor = wall_flag * radius[1][x][:1]
        coef = wall_coef[:, x * Z : (x + 1) * Z]
        out[spot, :] = out[spot, :] - factor * coef * adj[spot, :]

    done = 0
    for start in range(0, X, step):
        here = list(range(start, min(X, start + step)))
        right = jnp.concatenate([padded_plane(d, d.plane(adj, x)) for x in here], axis=1)
        chunk = dot(mk[...], split3(right))
        for offset, x in enumerate(here):
            products[x] = (chunk, offset)
        while done < X and (done + 1 in products or (done + 1 == X and done in products)):
            finish(done)
            done += 1


def first_local_kernel(
    d, adj, src, vel, snd, couple, precond, codes, mask, table, gain,
    out, rs, mk, mw, pk, wall_coef,
):
    make_matrices(d, couple, precond, mk, mw, pk)
    make_wall(d, codes, mask, table, gain, wall_coef)
    sweep_local(d, adj, src, vel, snd, mk, wall_coef, None, out, rs)


def later_local_kernel(d, adj, src, vel, snd, rs, mk, wall_coef, out):
    sweep_local(d, adj, src, vel, snd, mk, wall_coef, rs, out, None)


def halo_terms(d, s0, s1, w0, w1, zl, zr, mk, mw):
    V, X, W, Z, G, n = d.V, d.X, d.W, d.Z, d.G, d.n
    even_s, even_w = parity("stream"), parity("wall")
    si, wi = lax.axis_index("stream"), lax.axis_index("wall")
    has = lambda flag: flag.astype(F32)
    s_low, s_high = has(si > 0), has(si < lax.axis_size("stream") - 1)
    w_low, w_high = has(wi > 0), has(wi < lax.axis_size("wall") - 1)
    low = jnp.where(even_s, s1[...], s0[...]) * s_low
    high = jnp.where(even_s, s0[...], s1[...]) * s_high
    both = dot(mk[: 2 * n], split3(jnp.concatenate([low, high], axis=1)))
    stream = both[:n, :Z], both[n:, Z:]
    stream_radius = (low[n : n + W], high[n : n + W])

    def wall_rows(x):
        rows = pl.ds(x * G, d.wall_k)
        a, b = w0[rows, :], w1[rows, :]
        return jnp.where(even_w, b, a) * w_low, jnp.where(even_w, a, b) * w_high

    def wall(x):
        return jnp.concatenate(wall_rows(x), axis=0)

    row = row_ids(d)

    def wall_radius(x):
        rows = pl.ds(x * G + V, 1)
        a, b = w0[rows, :], w1[rows, :]
        first = jnp.where(even_w, b, a) * w_low
        last = jnp.where(even_w, a, b) * w_high
        return jnp.where(row == 0, first, jnp.where(row == W - 1, last, 0.0))

    even = lax.rem(lanes(d, W), 2) == 0
    pieces = []
    for v in range(V + 1):
        q = pl.ds((v // d.per) * W, W)
        value = jnp.where(even, zl[q, :], zr[q, :])
        turn = (Z - 2 * X * (v % d.per)) % Z
        pieces.append(pltpu.roll(value, turn, 1) if turn else value)
    span_radius = jnp.where(even, pieces[V], pltpu.roll(pieces[V], Z - 2, 1))
    pieces += [jnp.zeros((W, Z), F32)] * (G - V - 1)
    both = dot(mk[4 * n :], split3(jnp.concatenate(pieces, axis=0)))
    even = lax.rem(lanes(d, n), 2) == 0
    span = jnp.where(even, both[:n], pltpu.roll(both[n:], Z - 2, 1))
    at = lambda value, x: pltpu.roll(value, (Z - 2 * x) % Z, 1) if x else value
    return (
        stream,
        stream_radius,
        wall,
        wall_radius,
        lambda x: at(span, x),
        lambda x: at(span_radius, x),
    )


def finish_sweep(d, partial, adj, rs_of, halo_rates, corrections, halo, mw, pk, put):
    V, X, W, Z = d.V, d.X, d.W, d.Z
    n = V * W
    stream, _, wall, _, span, _ = halo
    for start in range(0, X, 2):
        here = list(range(start, min(X, start + 2)))
        from_wall = dot(mw[...], split3(jnp.concatenate([wall(x) for x in here], axis=1)))
        residuals = []
        for k, x in enumerate(here):
            low, high, rate_wall, rate_span = halo_rates(x)
            res = d.plane(partial, x)
            if corrections is not None:
                res = res - d.each(corrections(x)) * d.plane(adj, x)
            res = res - d.each(rate_wall) * from_wall[:n, k * Z : (k + 1) * Z]
            res = res - d.each(rate_span) * span(x)
            if low is not None:
                res = res - d.each(low) * stream[0]
            if high is not None:
                res = res - d.each(high) * stream[1]
            residuals.append(res)
        right = jnp.concatenate([padded_plane(d, r) for r in residuals], axis=1)
        update = dot(pk[...], split3(right))
        for k, x in enumerate(here):
            inverse = 1.0 / rs_of(x)
            new = d.plane(adj, x) + update[:n, k * Z : (k + 1) * Z] * d.each(inverse)
            put(x, new, residuals[k])


def first_halo_kernel(
    d, partial, adj, rs, vel, snd, s0, s1, w0, w1, zl, zr, mk, mw, pk,
    new_adj, rs_full, rates, s_a, s_b, w_a, w_b, z_out,
):
    X, W, Z = d.X, d.W, d.Z
    halo = halo_terms(d, s0, s1, w0, w1, zl, zr, mk, mw)
    _, stream_radius, _, wall_radius, _, span_radius = halo
    lane, row = lanes(d, W), row_ids(d)
    edge_lane = (lane == 0) | (lane == Z - 1)
    edge_row = (row == 0) | (row == W - 1)
    kept = {}
    for x in range(X):
        from_wall = 0.5 * wall_radius(x)
        from_span = jnp.where(edge_lane, 0.5 * span_radius(x), 0.0)
        rate_wall = jnp.where(edge_row, 0.5 * radius_at(d, vel, snd, 1, x) + from_wall, 0.0)
        rate_span = jnp.where(edge_lane, 0.5 * radius_at(d, vel, snd, 2, x) + from_span, 0.0)
        correction = from_wall + from_span
        low = high = None
        if x == 0:
            correction = correction + 0.5 * stream_radius[0]
            low = 0.5 * (radius_at(d, vel, snd, 0, x) + stream_radius[0])
            rates[d.block(2, 0), :] = low
        if x == X - 1:
            correction = correction + 0.5 * stream_radius[1]
            high = 0.5 * (radius_at(d, vel, snd, 0, x) + stream_radius[1])
            rates[d.block(2, 1 % X) if X > 1 else pl.ds((2 * X + 1) * W, W), :] = high
        rates[d.block(0, x), :] = rate_wall
        rates[d.block(1, x), :] = rate_span
        total = rs[d.block(0, x), :] + correction
        rs_full[d.block(0, x), :] = total
        kept[x] = (correction, total, (low, high, rate_wall, rate_span))

    def put(x, new, _):
        d.store_plane(new_adj, x, new)

    finish_sweep(
        d, partial, adj, lambda x: kept[x][1], lambda x: kept[x][2], lambda x: kept[x][0],
        halo, mw, pk, put,
    )
    pack_faces(
        d,
        lambda v, x: new_adj[d.block(v, x), :],
        None,
        lambda x, w: new_adj[pl.ds(x * W + w, d.V, stride=X * W), :],
        parity("stream"),
        parity("wall"),
        s_a, s_b, w_a, w_b, z_out,
    )


def last_halo_kernel(
    d, partial, adj, rs_full, rates, s0, s1, w0, w1, zl, zr, mk, mw, pk,
    new_adj, residual, new_adj_here, residual_here, sems,
):
    X, W, Z = d.X, d.W, d.Z
    halo = halo_terms(d, s0, s1, w0, w1, zl, zr, mk, mw)

    def halo_rates(x):
        low = rates[pl.ds(2 * X * W, W), :] if x == 0 else None
        high = rates[pl.ds((2 * X + 1) * W, W), :] if x == X - 1 else None
        return low, high, rates[d.block(0, x), :], rates[d.block(1, x), :]

    copies = []

    def put(x, new, res):
        here = d.planes_at(x, 1)
        new_adj_here[here] = new.reshape(d.V, W, Z)
        residual_here[here] = res.reshape(d.V, W, Z)
        if (x + 1) % STORE == 0 or x == X - 1:
            start = x - x % STORE
            part = d.planes_at(start, x + 1 - start)
            for k, (a, b) in enumerate(((new_adj_here, new_adj), (residual_here, residual))):
                copy = pltpu.make_async_copy(a.at[part], b.at[part], sems.at[k, start // STORE])
                copy.start()
                copies.append(copy)

    finish_sweep(
        d, partial, adj, lambda x: rs_full[d.block(0, x), :], halo_rates, None, halo, mw, pk, put
    )
    for copy in copies:
        copy.wait()


def exchange_pairs(sizes, axis, odd, spare):
    ids = np.arange(int(np.prod(sizes))).reshape(sizes)
    pairs = []
    for at in np.ndindex(*sizes):
        to = list(at)
        step = 1 if (at[axis] - odd) % 2 == 0 else -1
        if at[axis] >= odd and 0 <= at[axis] + step < sizes[axis]:
            to[axis] += step
        elif (at[spare] ^ 1) < sizes[spare]:
            to[spare] ^= 1
        else:
            continue
        pairs.append((int(ids[at]), int(ids[tuple(to)])))
    return pairs


def swap_lines(sizes, s_a, s_b, w_a, w_b, z):
    move = lambda value, pairs: lax.ppermute(value, AXES, pairs)
    s0 = move(s_a, exchange_pairs(sizes, 0, 0, 2))
    s1 = move(s_b, exchange_pairs(sizes, 0, 1, 2))
    w1 = move(w_b, exchange_pairs(sizes, 2, 1, 1))
    w0 = move(w_a, exchange_pairs(sizes, 2, 0, 1))
    peers = sizes[1]
    if peers == 1:
        zl = zr = z
    elif peers == 2:
        zl = zr = lax.ppermute(z, "span", [(0, 1), (1, 0)])
    else:
        up = [(i, (i + 1) % peers) for i in range(peers)]
        zl = lax.ppermute(z, "span", up)
        zr = lax.ppermute(z, "span", [(j, i) for i, j in up])
    return s0, s1, w0, w1, zl, zr


def call(kernel, d, outs, flops, args, held=(), scratch=(), out_held=False):
    space = lambda k: pltpu.HBM if k in held else pltpu.VMEM
    out_space = pltpu.HBM if out_held else pltpu.VMEM
    args = [pltpu.with_memory_space_constraint(a, space(k)) for k, a in enumerate(args)]
    moved = sum(int(np.prod(a.shape)) * a.dtype.itemsize for a in args)
    return pl.pallas_call(
        functools.partial(kernel, d),
        out_shape=tuple(out_space(s, t) for s, t in outs),
        in_specs=[pl.BlockSpec(memory_space=space(k)) for k in range(len(args))],
        out_specs=tuple(pl.BlockSpec(memory_space=out_space) for _ in outs),
        scratch_shapes=scratch,
        compiler_params=pltpu.CompilerParams(vmem_limit_bytes=24 * 2**20),
        cost_estimate=pl.CostEstimate(flops=flops, bytes_accessed=moved, transcendentals=0),
        name=kernel.__name__,
    )(*args)


def on_device(sizes, adj, source, velocity, sound, couple, precond, codes, mask, table, gain):
    shape = adj.shape
    d = Dims(shape)
    V, X, W, Z, B, n = d.V, d.X, d.W, d.Z, d.B, d.n
    inputs = [
        adj.reshape(d.rows, Z),
        velocity.reshape(3 * X * W, Z),
        sound.reshape(X * W, Z),
        precond,
        codes,
        mask,
        table,
        gain.reshape(1, -1),
    ]
    source = source.reshape(V, X * W, Z)
    faces = [((B, Z), F32)] * 2 + [((d.wall_rows, Z), F32)] * 2 + [((d.span_groups * W, Z), F32)]
    field, scalar = ((d.rows, Z), F32), ((X * W, Z), F32)
    planes = ((V, X * W, Z), F32)
    stores = -(-X // STORE)
    sems = lambda *counts: pltpu.SemaphoreType.DMA(counts)
    *kept, s_a, s_b, w_a, w_b, z = call(
        pack_kernel,
        d,
        [(a.shape, a.dtype) for a in inputs] + faces,
        0,
        inputs,
        held=range(len(inputs)),
        scratch=[sems(len(inputs))],
    )
    adj, velocity, sound = kept[:3]
    got = swap_lines(sizes, s_a, s_b, w_a, w_b, z)
    partial, rs, mk, mw, pk, wall_coef = call(
        first_local_kernel,
        d,
        [
            field,
            scalar,
            ((6 * n, 3 * B), BF16),
            ((n, 6 * d.wall_k), BF16),
            ((n, 3 * B), BF16),
            ((V, X * Z), F32),
        ],
        10**9,
        [adj, source, velocity, sound, couple] + kept[3:],
    )
    adj1, rs_full, rates, *packets = call(
        first_halo_kernel,
        d,
        [field, scalar, ((2 * (X + 1) * W, Z), F32)] + faces,
        10**8,
        [partial, adj, rs, velocity, sound, *got, mk, mw, pk],
    )
    got = swap_lines(sizes, *packets)
    (partial,) = call(
        later_local_kernel,
        d,
        [field],
        10**9,
        [adj1, source, velocity, sound, rs_full, mk, wall_coef],
    )
    adj2, residual = call(
        last_halo_kernel,
        d,
        [planes, planes],
        10**8,
        [partial, adj1, rs_full, rates, *got, mk, mw, pk],
        scratch=[pltpu.VMEM(*planes), pltpu.VMEM(*planes), sems(2, stores)],
        out_held=True,
    )
    return adj2.reshape(shape), residual.reshape(shape)


def solution(mesh):
    sizes = tuple(mesh.shape[a] for a in AXES)
    field = P(None, "stream", "wall", "span")
    return jax.shard_map(
        functools.partial(on_device, sizes),
        mesh=mesh,
        in_specs=(field, field, field, P("stream", "wall", "span")) + (P(),) * 6,
        out_specs=(field, field),
        check_vma=False,
    )
```

```python
import functools

import jax
import jax.numpy as jnp
import numpy as np
from jax import lax
from jax.experimental import pallas as pl
from jax.experimental.pallas import tpu as pltpu
from jax.sharding import PartitionSpec as P

AXES = ("stream", "span", "wall")
F32 = jnp.float32
BF16 = jnp.bfloat16
STORE = 4


class Dims:
    def __init__(self, shape):
        self.V, self.X, self.W, self.Z = shape
        self.G = self.V + 1
        while self.G * self.W % 16:
            self.G += 1
        self.B = self.G * self.W
        self.n = self.V * self.W
        self.rows = self.n * self.X
        self.wall_rows = self.X * self.G + 8
        self.wall_k = -(-self.G // 8) * 8
        self.stack = -(-self.V // 8) * 8
        self.per = self.Z // (2 * self.X)
        self.span_groups = -(-(self.V + 1) // self.per)

    def block(self, group, x):
        return pl.ds((group * self.X + x) * self.W, self.W)

    def plane(self, ref, x):
        return jnp.concatenate([ref[self.block(v, x), :] for v in range(self.V)], axis=0)

    def store_plane(self, ref, x, value):
        for v in range(self.V):
            ref[self.block(v, x), :] = value[v * self.W : (v + 1) * self.W]

    def plane3(self, ref, x):
        return ref[:, x * self.W : (x + 1) * self.W, :].reshape(self.n, self.Z)

    def planes_at(self, start, count):
        return (slice(None), pl.ds(start * self.W, count * self.W), slice(None))

    def each(self, factor):
        return jnp.concatenate([factor] * self.V, axis=0)


def lanes(d, rows):
    return lax.broadcasted_iota(jnp.int32, (rows, d.Z), 1)


def row_ids(d):
    return lax.broadcasted_iota(jnp.int32, (d.W, d.Z), 0)


def radius_at(d, vel, snd, direction, x):
    return jnp.abs(vel[d.block(direction, x), :]) + snd[d.block(0, x), :]


def split3(value):
    high = value.astype(BF16)
    low = (value - high.astype(F32)).astype(BF16)
    return jnp.concatenate([high, low, high], axis=0)


def padded_plane(d, value):
    extra = d.B - value.shape[0]
    if not extra:
        return value
    return jnp.concatenate([value, jnp.zeros((extra, value.shape[1]), F32)], axis=0)


def dot(a, b):
    return jnp.dot(a, b, preferred_element_type=F32)


def pack_faces(
    d, block_of, radius_of, rows_of, even_s, even_w, s_a, s_b, w_a, w_b, z_out
):
    V, X, W, Z, G = d.V, d.X, d.W, d.Z, d.G
    zero = jnp.zeros((W, Z), F32)
    pair = lanes(d, W) // 2
    groups = [zero] * d.span_groups

    def span_columns(v, x, value):
        spot = X * (v % d.per) + x
        moved = pltpu.roll(value, (2 * spot + 1) % Z, 1)
        groups[v // d.per] = jnp.where(pair == spot, moved, groups[v // d.per])

    for g in range(G):
        if g < V:
            first, last = block_of(g, 0), block_of(g, X - 1)
            for x in range(X):
                span_columns(g, x, block_of(g, x))
        elif g == V and radius_of is not None:
            first, last = radius_of(0, 0), radius_of(0, X - 1)
            for x in range(X):
                span_columns(V, x, radius_of(2, x))
        else:
            first = last = zero
        s_a[g * W : (g + 1) * W, :] = jnp.where(even_s, last, first)
        s_b[g * W : (g + 1) * W, :] = jnp.where(even_s, first, last)
    for q in range(d.span_groups):
        z_out[q * W : (q + 1) * W, :] = groups[q]
    tail = jnp.zeros((G - V, Z), F32)
    for x in range(X):
        first, last = rows_of(x, 0), rows_of(x, W - 1)
        w_a[x * G : x * G + V, :] = jnp.where(even_w, last, first)
        w_b[x * G : x * G + V, :] = jnp.where(even_w, first, last)
        if radius_of is None or G - V > 1:
            w_a[x * G + V : (x + 1) * G, :] = tail
            w_b[x * G + V : (x + 1) * G, :] = tail
        if radius_of is not None:
            radius = radius_of(1, x)
            first, last = radius[:1], radius[W - 1 :]
            w_a[x * G + V : x * G + V + 1, :] = jnp.where(even_w, last, first)
            w_b[x * G + V : x * G + V + 1, :] = jnp.where(even_w, first, last)
    w_a[X * G :, :] = jnp.zeros((8, Z), F32)
    w_b[X * G :, :] = jnp.zeros((8, Z), F32)


def parity(axis):
    return lax.rem(lax.axis_index(axis), 2) == 0


def pack_kernel(d, *refs):
    count = (len(refs) - 6) // 2
    held, kept = refs[:count], refs[count : 2 * count]
    s_a, s_b, w_a, w_b, z_out, sems = refs[2 * count :]
    adj, vel, snd = kept[:3]
    copies = [pltpu.make_async_copy(held[k], kept[k], sems.at[k]) for k in range(count)]
    for copy in copies:
        copy.start()
    for copy in copies:
        copy.wait()
    pack_faces(
        d,
        lambda v, x: adj[d.block(v, x), :],
        functools.partial(radius_at, d, vel, snd),
        lambda x, w: adj[pl.ds(x * d.W + w, d.V, stride=d.X * d.W), :],
        parity("stream"),
        parity("wall"),
        s_a,
        s_b,
        w_a,
        w_b,
        z_out,
    )


def make_matrices(d, couple, precond, mk, mw, pk, wide, wide_wall):
    V, W, B, n, K, S = d.V, d.W, d.B, d.n, d.wall_k, d.stack
    gap = jnp.zeros((V, S - V), F32)
    blocks = [couple[k // 2, k % 2] for k in range(6)] + [precond[...].T]
    blocks = [piece for m in blocks for piece in ((m, gap) if S > V else (m,))]
    blocks = jnp.concatenate(blocks, axis=1)
    high = blocks.astype(BF16).astype(F32)
    gap = jnp.zeros((S - V, 7 * S), F32)
    pieces = (high, gap, blocks - high, gap) if S > V else (high, blocks - high)
    blocks = jnp.concatenate(pieces, axis=0).astype(BF16)
    dims = (((0,), (0,)), ((), ()))

    def spread(some, width, keep):
        row = lax.broadcasted_iota(jnp.int32, (2 * S, 3 * width), 0)
        col = lax.broadcasted_iota(jnp.int32, (2 * S, 3 * width), 1)
        part = keep(lax.rem(col, width), jnp.where(row < S, row, row - S))
        part = part & ((row < S) == (col < 2 * width))
        return lax.dot_general(some, part.astype(BF16), dims, preferred_element_type=F32)

    wide[...] = spread(blocks, B, lambda col, v: col // W == v)
    for side in range(2):
        some = blocks[:, (2 + side) * S : (3 + side) * S]
        wide_wall[side * S : (side + 1) * S, :] = spread(some, 2 * K, lambda col, v: col - side * K == v)
    row = lax.broadcasted_iota(jnp.int32, (W, 3 * B), 0)
    col = lax.rem(lax.broadcasted_iota(jnp.int32, (W, 3 * B), 1), W)
    same, lower, upper = [(col - row == k).astype(F32) for k in (0, -1, 1)]

    def rows(k):
        mask = {2: lower, 3: upper}.get(k, same)
        return [wide[pl.ds(k * S + v, 1), :] * mask for v in range(V)]

    for k in range(0, 6, 2):
        both = jnp.concatenate(rows(k) + rows(k + 1), axis=0)
        mk[k * n : (k + 2) * n, :] = both.astype(BF16)
    pk[...] = jnp.concatenate(rows(6), axis=0).astype(BF16)
    row = lax.broadcasted_iota(jnp.int32, (W, 6 * K), 0)
    first, last = (row == 0).astype(F32), (row == W - 1).astype(F32)
    pieces = [
        wide_wall[pl.ds(v, 1), :] * first + wide_wall[pl.ds(S + v, 1), :] * last for v in range(V)
    ]
    mw[...] = jnp.concatenate(pieces, axis=0).astype(BF16)


def make_wall(d, codes, mask, table, gain, wall_out):
    X, Z, V, S = d.X, d.Z, d.V, d.stack
    place = lax.axis_index("stream")
    lane0 = pl.multiple_of(lax.axis_index("span") * Z, Z)
    kinds = table.shape[0]

    def window(ref):
        value = ref[:X, pl.ds(lane0, Z)]
        for s in range(1, lax.axis_size("stream")):
            value = jnp.where(place == s, ref[s * X : (s + 1) * X, pl.ds(lane0, Z)], value)
        return value

    code, spall = window(codes), window(mask).astype(F32)
    column = lambda values: jnp.broadcast_to(values.T, (V, Z))
    columns = [column(table[k : k + 1, :]) for k in range(kinds)]
    gains = column(gain[...])
    for x in range(X):
        here = jnp.broadcast_to(code[x : x + 1], (V, Z))
        coef = columns[kinds - 1]
        for k in range(kinds - 1):
            coef = jnp.where(here == k, columns[k], coef)
        wall_out[x * S : x * S + V, :] = coef + gains * spall[x : x + 1]


def sweep_local(d, adj, src, vel, snd, mk, wall_coef, rates_of, out, rs_out):
    V, X, W, Z, n = d.V, d.X, d.W, d.Z, d.n
    lane, row = lanes(d, W), row_ids(d)
    wall_flag = (lax.axis_index("wall") == 0).astype(F32)
    radius = [[radius_at(d, vel, snd, k, x) for x in range(X)] for k in range(3)]
    step = 2
    products = {}

    def product(x, k):
        chunk, offset = products[x]
        return chunk[k * n : (k + 1) * n, offset * Z : (offset + 1) * Z]

    def finish(x):
        a = d.plane(adj, x)
        total = 1.0
        terms = []
        half = [0.5 * radius[k][x] for k in range(3)]
        for k, neighbour in ((0, x - 1), (1, x + 1)):
            rate = half[0]
            if 0 <= neighbour < X:
                rate = rate + 0.5 * radius[0][neighbour]
                terms.append((rate, product(neighbour, k)))
            total = total + rate
        for k, edge, turn in ((2, 0, 1), (3, W - 1, W - 1)):
            near = jnp.where(row == edge, 0.0, pltpu.roll(half[1], turn, 0))
            rate = half[1] + near
            terms.append((rate, product(x, k)))
            total = total + rate
        for k, edge, turn in ((4, 0, 1), (5, Z - 1, Z - 1)):
            near = jnp.where(lane == edge, 0.0, pltpu.roll(half[2], turn, 1))
            total = total + half[2] + near
            rate = jnp.where(lane == edge, 0.0, half[2] + near)
            terms.append((rate, pltpu.roll(product(x, k), turn, 1)))
        if rates_of is None:
            rs_out[d.block(0, x), :] = total
        else:
            total = rates_of[d.block(0, x), :]
        result = d.plane3(src, x) - d.each(total) * a
        for rate, value in terms:
            result = result - d.each(rate) * value
        d.store_plane(out, x, result)
        spot = pl.ds(x * W, V, stride=X * W)
        factor = wall_flag * radius[1][x][:1]
        coef = wall_coef[x * d.stack : x * d.stack + V, :]
        out[spot, :] = out[spot, :] - factor * coef * adj[spot, :]

    done = 0
    for start in range(0, X, step):
        here = list(range(start, min(X, start + step)))
        right = jnp.concatenate([padded_plane(d, d.plane(adj, x)) for x in here], axis=1)
        chunk = dot(mk[...], split3(right))
        for offset, x in enumerate(here):
            products[x] = (chunk, offset)
        while done < X and (done + 1 in products or (done + 1 == X and done in products)):
            finish(done)
            done += 1


def first_local_kernel(
    d, adj, src, vel, snd, couple, precond, codes, mask, table, gain,
    out, rs, mk, mw, pk, wall_coef, wide, wide_wall,
):
    make_matrices(d, couple, precond, mk, mw, pk, wide, wide_wall)
    make_wall(d, codes, mask, table, gain, wall_coef)
    sweep_local(d, adj, src, vel, snd, mk, wall_coef, None, out, rs)


def later_local_kernel(d, adj, src, vel, snd, rs, mk, wall_coef, out):
    sweep_local(d, adj, src, vel, snd, mk, wall_coef, rs, out, None)


def halo_terms(d, s0, s1, w0, w1, zl, zr, mk, mw):
    V, X, W, Z, G, n = d.V, d.X, d.W, d.Z, d.G, d.n
    even_s, even_w = parity("stream"), parity("wall")
    si, wi = lax.axis_index("stream"), lax.axis_index("wall")
    has = lambda flag: flag.astype(F32)
    s_low, s_high = has(si > 0), has(si < lax.axis_size("stream") - 1)
    w_low, w_high = has(wi > 0), has(wi < lax.axis_size("wall") - 1)
    low = jnp.where(even_s, s1[...], s0[...]) * s_low
    high = jnp.where(even_s, s0[...], s1[...]) * s_high
    both = dot(mk[: 2 * n], split3(jnp.concatenate([low, high], axis=1)))
    stream = both[:n, :Z], both[n:, Z:]
    stream_radius = (low[n : n + W], high[n : n + W])

    def wall_rows(x):
        rows = pl.ds(x * G, d.wall_k)
        a, b = w0[rows, :], w1[rows, :]
        return jnp.where(even_w, b, a) * w_low, jnp.where(even_w, a, b) * w_high

    def wall(x):
        return jnp.concatenate(wall_rows(x), axis=0)

    row = row_ids(d)

    def wall_radius(x):
        rows = pl.ds(x * G + V, 1)
        a, b = w0[rows, :], w1[rows, :]
        first = jnp.where(even_w, b, a) * w_low
        last = jnp.where(even_w, a, b) * w_high
        return jnp.where(row == 0, first, jnp.where(row == W - 1, last, 0.0))

    even = lax.rem(lanes(d, W), 2) == 0
    pieces = []
    for v in range(V + 1):
        q = pl.ds((v // d.per) * W, W)
        value = jnp.where(even, zl[q, :], zr[q, :])
        turn = (Z - 2 * X * (v % d.per)) % Z
        pieces.append(pltpu.roll(value, turn, 1) if turn else value)
    span_radius = jnp.where(even, pieces[V], pltpu.roll(pieces[V], Z - 2, 1))
    pieces += [jnp.zeros((W, Z), F32)] * (G - V - 1)
    both = dot(mk[4 * n :], split3(jnp.concatenate(pieces, axis=0)))
    even = lax.rem(lanes(d, n), 2) == 0
    span = jnp.where(even, both[:n], pltpu.roll(both[n:], Z - 2, 1))
    at = lambda value, x: pltpu.roll(value, (Z - 2 * x) % Z, 1) if x else value
    return (
        stream,
        stream_radius,
        wall,
        wall_radius,
        lambda x: at(span, x),
        lambda x: at(span_radius, x),
    )


def finish_sweep(d, partial, adj, rs_of, halo_rates, corrections, halo, mw, pk, put):
    X, Z = d.X, d.Z
    stream, _, wall, _, span, _ = halo
    walls = {}
    for start in range(0, X, 2):
        here = list(range(start, min(X, start + 2)))
        value = dot(mw[...], split3(jnp.concatenate([wall(x) for x in here], axis=1)))
        for k, x in enumerate(here):
            walls[x] = value[:, k * Z : (k + 1) * Z]

    def residual(x):
        low, high, rate_wall, rate_span = halo_rates(x)
        res = d.plane(partial, x)
        if corrections is not None:
            res = res - d.each(corrections(x)) * d.plane(adj, x)
        res = res - d.each(rate_wall) * walls[x]
        res = res - d.each(rate_span) * span(x)
        if low is not None:
            res = res - d.each(low) * stream[0]
        if high is not None:
            res = res - d.each(high) * stream[1]
        return res

    def updated(here, residuals, update):
        for k, x in enumerate(here):
            inverse = 1.0 / rs_of(x)
            new = d.plane(adj, x) + update[:, k * Z : (k + 1) * Z] * d.each(inverse)
            put(x, new, residuals[k])

    waiting = None
    for start in range(0, X, 2):
        here = list(range(start, min(X, start + 2)))
        residuals = [residual(x) for x in here]
        right = jnp.concatenate([padded_plane(d, r) for r in residuals], axis=1)
        update = dot(pk[...], split3(right))
        if waiting:
            updated(*waiting)
        waiting = here, residuals, update
    updated(*waiting)


def first_halo_kernel(
    d, partial, adj, rs, vel, snd, s0, s1, w0, w1, zl, zr, mk, mw, pk,
    new_adj, rs_full, rates, s_a, s_b, w_a, w_b, z_out,
):
    X, W, Z = d.X, d.W, d.Z
    halo = halo_terms(d, s0, s1, w0, w1, zl, zr, mk, mw)
    _, stream_radius, _, wall_radius, _, span_radius = halo
    lane, row = lanes(d, W), row_ids(d)
    edge_lane = (lane == 0) | (lane == Z - 1)
    edge_row = (row == 0) | (row == W - 1)
    kept = {}
    for x in range(X):
        from_wall = 0.5 * wall_radius(x)
        from_span = jnp.where(edge_lane, 0.5 * span_radius(x), 0.0)
        rate_wall = jnp.where(edge_row, 0.5 * radius_at(d, vel, snd, 1, x) + from_wall, 0.0)
        rate_span = jnp.where(edge_lane, 0.5 * radius_at(d, vel, snd, 2, x) + from_span, 0.0)
        correction = from_wall + from_span
        low = high = None
        if x == 0:
            correction = correction + 0.5 * stream_radius[0]
            low = 0.5 * (radius_at(d, vel, snd, 0, x) + stream_radius[0])
            rates[d.block(2, 0), :] = low
        if x == X - 1:
            correction = correction + 0.5 * stream_radius[1]
            high = 0.5 * (radius_at(d, vel, snd, 0, x) + stream_radius[1])
            rates[d.block(2, 1 % X) if X > 1 else pl.ds((2 * X + 1) * W, W), :] = high
        rates[d.block(0, x), :] = rate_wall
        rates[d.block(1, x), :] = rate_span
        total = rs[d.block(0, x), :] + correction
        rs_full[d.block(0, x), :] = total
        kept[x] = (correction, total, (low, high, rate_wall, rate_span))

    def put(x, new, _):
        d.store_plane(new_adj, x, new)

    finish_sweep(
        d, partial, adj, lambda x: kept[x][1], lambda x: kept[x][2], lambda x: kept[x][0],
        halo, mw, pk, put,
    )
    pack_faces(
        d,
        lambda v, x: new_adj[d.block(v, x), :],
        None,
        lambda x, w: new_adj[pl.ds(x * W + w, d.V, stride=X * W), :],
        parity("stream"),
        parity("wall"),
        s_a, s_b, w_a, w_b, z_out,
    )


def last_halo_kernel(
    d, partial, adj, rs_full, rates, s0, s1, w0, w1, zl, zr, mk, mw, pk,
    new_adj, residual, new_adj_here, residual_here, sems,
):
    X, W, Z = d.X, d.W, d.Z
    halo = halo_terms(d, s0, s1, w0, w1, zl, zr, mk, mw)

    def halo_rates(x):
        low = rates[pl.ds(2 * X * W, W), :] if x == 0 else None
        high = rates[pl.ds((2 * X + 1) * W, W), :] if x == X - 1 else None
        return low, high, rates[d.block(0, x), :], rates[d.block(1, x), :]

    copies = []

    def put(x, new, res):
        here = d.planes_at(x, 1)
        new_adj_here[here] = new.reshape(d.V, W, Z)
        residual_here[here] = res.reshape(d.V, W, Z)
        if (x + 1) % STORE == 0 or x == X - 1:
            start = x - x % STORE
            part = d.planes_at(start, x + 1 - start)
            for k, (a, b) in enumerate(((new_adj_here, new_adj), (residual_here, residual))):
                copy = pltpu.make_async_copy(a.at[part], b.at[part], sems.at[k, start // STORE])
                copy.start()
                copies.append(copy)

    finish_sweep(
        d, partial, adj, lambda x: rs_full[d.block(0, x), :], halo_rates, None, halo, mw, pk, put
    )
    for copy in copies:
        copy.wait()


def exchange_pairs(sizes, axis, odd, spare):
    ids = np.arange(int(np.prod(sizes))).reshape(sizes)
    pairs = []
    for at in np.ndindex(*sizes):
        to = list(at)
        step = 1 if (at[axis] - odd) % 2 == 0 else -1
        if at[axis] >= odd and 0 <= at[axis] + step < sizes[axis]:
            to[axis] += step
        elif (at[spare] ^ 1) < sizes[spare]:
            to[spare] ^= 1
        else:
            continue
        pairs.append((int(ids[at]), int(ids[tuple(to)])))
    return pairs


def swap_lines(sizes, s_a, s_b, w_a, w_b, z):
    move = lambda value, pairs: lax.ppermute(value, AXES, pairs)
    s0 = move(s_a, exchange_pairs(sizes, 0, 0, 2))
    s1 = move(s_b, exchange_pairs(sizes, 0, 1, 2))
    w1 = move(w_b, exchange_pairs(sizes, 2, 1, 1))
    w0 = move(w_a, exchange_pairs(sizes, 2, 0, 1))
    peers = sizes[1]
    if peers == 1:
        zl = zr = z
    elif peers == 2:
        zl = zr = lax.ppermute(z, "span", [(0, 1), (1, 0)])
    else:
        up = [(i, (i + 1) % peers) for i in range(peers)]
        zl = lax.ppermute(z, "span", up)
        zr = lax.ppermute(z, "span", [(j, i) for i, j in up])
    return s0, s1, w0, w1, zl, zr


def call(kernel, d, outs, flops, args, held=(), scratch=(), out_held=False):
    space = lambda k: pltpu.HBM if k in held else pltpu.VMEM
    out_space = pltpu.HBM if out_held else pltpu.VMEM
    args = [pltpu.with_memory_space_constraint(a, space(k)) for k, a in enumerate(args)]
    moved = sum(int(np.prod(a.shape)) * a.dtype.itemsize for a in args)
    return pl.pallas_call(
        functools.partial(kernel, d),
        out_shape=tuple(out_space(s, t) for s, t in outs),
        in_specs=[pl.BlockSpec(memory_space=space(k)) for k in range(len(args))],
        out_specs=tuple(pl.BlockSpec(memory_space=out_space) for _ in outs),
        scratch_shapes=scratch,
        compiler_params=pltpu.CompilerParams(vmem_limit_bytes=24 * 2**20),
        cost_estimate=pl.CostEstimate(flops=flops, bytes_accessed=moved, transcendentals=0),
        name=kernel.__name__,
    )(*args)


def on_device(sizes, adj, source, velocity, sound, couple, precond, codes, mask, table, gain):
    shape = adj.shape
    d = Dims(shape)
    V, X, W, Z, B, n = d.V, d.X, d.W, d.Z, d.B, d.n
    inputs = [
        adj.reshape(d.rows, Z),
        velocity.reshape(3 * X * W, Z),
        sound.reshape(X * W, Z),
        precond,
        codes,
        mask,
        table,
        gain.reshape(1, -1),
    ]
    source = source.reshape(V, X * W, Z)
    faces = [((B, Z), F32)] * 2 + [((d.wall_rows, Z), F32)] * 2 + [((d.span_groups * W, Z), F32)]
    field, scalar = ((d.rows, Z), F32), ((X * W, Z), F32)
    planes = ((V, X * W, Z), F32)
    stores = -(-X // STORE)
    sems = lambda *counts: pltpu.SemaphoreType.DMA(counts)
    *kept, s_a, s_b, w_a, w_b, z = call(
        pack_kernel,
        d,
        [(a.shape, a.dtype) for a in inputs] + faces,
        0,
        inputs,
        held=range(len(inputs)),
        scratch=[sems(len(inputs))],
    )
    adj, velocity, sound = kept[:3]
    got = swap_lines(sizes, s_a, s_b, w_a, w_b, z)
    partial, rs, mk, mw, pk, wall_coef = call(
        first_local_kernel,
        d,
        [
            field,
            scalar,
            ((6 * n, 3 * B), BF16),
            ((n, 6 * d.wall_k), BF16),
            ((n, 3 * B), BF16),
            ((X * d.stack, Z), F32),
        ],
        10**9,
        [adj, source, velocity, sound, couple] + kept[3:],
        scratch=[pltpu.VMEM((7 * d.stack, 3 * B), F32), pltpu.VMEM((2 * d.stack, 6 * d.wall_k), F32)],
    )
    adj1, rs_full, rates, *packets = call(
        first_halo_kernel,
        d,
        [field, scalar, ((2 * (X + 1) * W, Z), F32)] + faces,
        10**8,
        [partial, adj, rs, velocity, sound, *got, mk, mw, pk],
    )
    got = swap_lines(sizes, *packets)
    (partial,) = call(
        later_local_kernel,
        d,
        [field],
        10**9,
        [adj1, source, velocity, sound, rs_full, mk, wall_coef],
    )
    adj2, residual = call(
        last_halo_kernel,
        d,
        [planes, planes],
        10**8,
        [partial, adj1, rs_full, rates, *got, mk, mw, pk],
        scratch=[pltpu.VMEM(*planes), pltpu.VMEM(*planes), sems(2, stores)],
        out_held=True,
    )
    return adj2.reshape(shape), residual.reshape(shape)


def solution(mesh):
    sizes = tuple(mesh.shape[a] for a in AXES)
    field = P(None, "stream", "wall", "span")
    return jax.shard_map(
        functools.partial(on_device, sizes),
        mesh=mesh,
        in_specs=(field, field, field, P("stream", "wall", "span")) + (P(),) * 6,
        out_specs=(field, field),
        check_vma=False,
    )
```

```python
import functools

import jax
import jax.numpy as jnp
import numpy as np
from jax import lax
from jax.experimental import pallas as pl
from jax.experimental.pallas import tpu as pltpu
from jax.sharding import PartitionSpec as P

AXES = ("stream", "span", "wall")
F32 = jnp.float32
BF16 = jnp.bfloat16


class Dims:
    def __init__(self, shape):
        self.V, self.X, self.W, self.Z = shape
        self.G = self.V + 1
        while self.G * self.W % 16:
            self.G += 1
        self.B = self.G * self.W
        self.n = self.V * self.W
        self.rows = self.n * self.X
        self.edges = sorted({0, self.X - 1})
        self.inner = range(1, self.X - 1)
        self.wall_rows = self.X * self.G + 8
        self.wall_k = -(-self.G // 8) * 8
        self.stack = -(-self.V // 8) * 8
        self.per = self.Z // (2 * self.X)
        self.span_groups = -(-(self.V + 1) // self.per)

    def block(self, group, x):
        return pl.ds((group * self.X + x) * self.W, self.W)

    def rows_at(self, x, w):
        return pl.ds(x * self.W + w, self.V, stride=self.X * self.W)

    def plane(self, ref, x):
        return jnp.concatenate([ref[self.block(v, x), :] for v in range(self.V)], axis=0)

    def store_plane(self, ref, x, value):
        for v in range(self.V):
            ref[self.block(v, x), :] = value[v * self.W : (v + 1) * self.W]

    def plane3(self, ref, x):
        return ref[:, x * self.W : (x + 1) * self.W, :].reshape(self.n, self.Z)

    def planes_at(self, start, count):
        return (slice(None), pl.ds(start * self.W, count * self.W), slice(None))

    def each(self, factor):
        return jnp.concatenate([factor] * self.V, axis=0)


def lanes(d, rows):
    return lax.broadcasted_iota(jnp.int32, (rows, d.Z), 1)


def row_ids(d):
    return lax.broadcasted_iota(jnp.int32, (d.W, d.Z), 0)


def radius_at(d, vel, snd, direction, x):
    return jnp.abs(vel[d.block(direction, x), :]) + snd[d.block(0, x), :]


def split3(value):
    high = value.astype(BF16)
    low = (value - high.astype(F32)).astype(BF16)
    return jnp.concatenate([high, low, high], axis=0)


def padded_plane(d, value):
    extra = d.B - value.shape[0]
    if not extra:
        return value
    return jnp.concatenate([value, jnp.zeros((extra, value.shape[1]), F32)], axis=0)


def dot(a, b):
    return jnp.dot(a, b, preferred_element_type=F32)


def pack_stream(d, block_of, radius_of, s_a, s_b):
    W, even = d.W, parity("stream")
    for g in range(d.G):
        if g < d.V:
            first, last = block_of(g, 0), block_of(g, d.X - 1)
        elif g == d.V and radius_of is not None:
            first, last = radius_of(0, 0), radius_of(0, d.X - 1)
        else:
            first = last = jnp.zeros((W, d.Z), F32)
        s_a[g * W : (g + 1) * W, :] = jnp.where(even, last, first)
        s_b[g * W : (g + 1) * W, :] = jnp.where(even, first, last)


def pack_span(d, planes, block_of, radius_of, given, z_out):
    V, X, W, Z = d.V, d.X, d.W, d.Z
    pair = lanes(d, W) // 2
    for q in range(d.span_groups):
        rows = pl.ds(q * W, W)
        group = jnp.zeros((W, Z), F32) if given is None else given[rows, :]
        for v in range(q * d.per, min(V + 1, (q + 1) * d.per)):
            if v == V and radius_of is None:
                continue
            for x in planes:
                value = block_of(v, x) if v < V else radius_of(2, x)
                spot = X * (v % d.per) + x
                group = jnp.where(pair == spot, pltpu.roll(value, (2 * spot + 1) % Z, 1), group)
        z_out[rows, :] = group


def pack_walls(d, planes, adj, radius_of, w_a, w_b):
    V, X, W, Z, G = d.V, d.X, d.W, d.Z, d.G
    even = parity("wall")
    tail = jnp.zeros((G - V, Z), F32)
    for x in planes:
        first, last = adj[d.rows_at(x, 0), :], adj[d.rows_at(x, W - 1), :]
        w_a[x * G : x * G + V, :] = jnp.where(even, last, first)
        w_b[x * G : x * G + V, :] = jnp.where(even, first, last)
        if radius_of is None or G - V > 1:
            w_a[x * G + V : (x + 1) * G, :] = tail
            w_b[x * G + V : (x + 1) * G, :] = tail
        if radius_of is not None:
            radius = radius_of(1, x)
            first, last = radius[:1], radius[W - 1 :]
            w_a[x * G + V : x * G + V + 1, :] = jnp.where(even, last, first)
            w_b[x * G + V : x * G + V + 1, :] = jnp.where(even, first, last)
    if X - 1 in planes:
        w_a[X * G :, :] = jnp.zeros((8, Z), F32)
        w_b[X * G :, :] = jnp.zeros((8, Z), F32)


def parity(axis):
    return lax.rem(lax.axis_index(axis), 2) == 0


def pack_kernel(d, *refs):
    count = (len(refs) - 6) // 2
    held, kept = refs[:count], refs[count : 2 * count]
    s_a, s_b, w_a, w_b, z_out, sems = refs[2 * count :]
    adj, vel, snd = kept[:3]
    copies = [pltpu.make_async_copy(held[k], kept[k], sems.at[k]) for k in range(count)]
    for copy in copies:
        copy.start()
    for copy in copies:
        copy.wait()
    block_of = lambda v, x: adj[d.block(v, x), :]
    radius_of = functools.partial(radius_at, d, vel, snd)
    pack_stream(d, block_of, radius_of, s_a, s_b)
    pack_span(d, range(d.X), block_of, radius_of, None, z_out)
    pack_walls(d, range(d.X), adj, radius_of, w_a, w_b)


def make_matrices(d, couple, precond, mk, mw, pk, wide, wide_wall):
    V, W, B, n, K, S = d.V, d.W, d.B, d.n, d.wall_k, d.stack
    gap = jnp.zeros((V, S - V), F32)
    blocks = [couple[k // 2, k % 2] for k in range(6)] + [precond[...].T]
    blocks = [piece for m in blocks for piece in ((m, gap) if S > V else (m,))]
    blocks = jnp.concatenate(blocks, axis=1)
    high = blocks.astype(BF16).astype(F32)
    gap = jnp.zeros((S - V, 7 * S), F32)
    pieces = (high, gap, blocks - high, gap) if S > V else (high, blocks - high)
    blocks = jnp.concatenate(pieces, axis=0).astype(BF16)
    dims = (((0,), (0,)), ((), ()))

    def spread(some, width, keep):
        row = lax.broadcasted_iota(jnp.int32, (2 * S, 3 * width), 0)
        col = lax.broadcasted_iota(jnp.int32, (2 * S, 3 * width), 1)
        part = keep(lax.rem(col, width), jnp.where(row < S, row, row - S))
        part = part & ((row < S) == (col < 2 * width))
        return lax.dot_general(some, part.astype(BF16), dims, preferred_element_type=F32)

    wide[...] = spread(blocks, B, lambda col, v: col // W == v)
    sides = []
    for side in range(2):
        some = blocks[:, (2 + side) * S : (3 + side) * S]
        sides.append(spread(some, 2 * K, lambda col, v: col - side * K == v))
    wide_wall[...] = jnp.concatenate(sides, axis=0)
    row = lax.broadcasted_iota(jnp.int32, (W, 3 * B), 0)
    col = lax.rem(lax.broadcasted_iota(jnp.int32, (W, 3 * B), 1), W)
    same, lower, upper = [(col - row == k).astype(F32) for k in (0, -1, 1)]

    def rows(k):
        mask = {2: lower, 3: upper}.get(k, same)
        return [wide[pl.ds(k * S + v, 1), :] * mask for v in range(V)]

    for k in range(0, 6, 2):
        both = jnp.concatenate(rows(k) + rows(k + 1), axis=0)
        mk[k * n : (k + 2) * n, :] = both.astype(BF16)
    pk[...] = jnp.concatenate(rows(6), axis=0).astype(BF16)
    row = lax.broadcasted_iota(jnp.int32, (W, 6 * K), 0)
    first, last = (row == 0).astype(F32), (row == W - 1).astype(F32)
    pieces = [
        wide_wall[pl.ds(v, 1), :] * first + wide_wall[pl.ds(S + v, 1), :] * last for v in range(V)
    ]
    mw[...] = jnp.concatenate(pieces, axis=0).astype(BF16)


def make_wall(d, codes, mask, table, gain, wall_out):
    X, Z, V, S = d.X, d.Z, d.V, d.stack
    place = lax.axis_index("stream")
    lane0 = pl.multiple_of(lax.axis_index("span") * Z, Z)
    kinds = table.shape[0]

    def window(ref):
        value = ref[:X, pl.ds(lane0, Z)]
        for s in range(1, lax.axis_size("stream")):
            value = jnp.where(place == s, ref[s * X : (s + 1) * X, pl.ds(lane0, Z)], value)
        return value

    code, spall = window(codes), window(mask).astype(F32)
    column = lambda values: jnp.broadcast_to(values.T, (V, Z))
    columns = [column(table[k : k + 1, :]) for k in range(kinds)]
    gains = column(gain[...])
    for x in range(X):
        here = jnp.broadcast_to(code[x : x + 1], (V, Z))
        coef = columns[kinds - 1]
        for k in range(kinds - 1):
            coef = jnp.where(here == k, columns[k], coef)
        wall_out[x * S : x * S + V, :] = coef + gains * spall[x : x + 1]


def sweep_local(d, adj, src, vel, snd, mk, wall_coef, rates_of, out, rs_out):
    V, X, W, Z, n = d.V, d.X, d.W, d.Z, d.n
    lane, row = lanes(d, W), row_ids(d)
    wall_flag = (lax.axis_index("wall") == 0).astype(F32)
    radius = [[radius_at(d, vel, snd, k, x) for x in range(X)] for k in range(3)]
    step = 2
    products = {}

    def product(x, k):
        chunk, offset = products[x]
        return chunk[k * n : (k + 1) * n, offset * Z : (offset + 1) * Z]

    def finish(x):
        a = d.plane(adj, x)
        total = 1.0
        terms = []
        half = [0.5 * radius[k][x] for k in range(3)]
        for k, neighbour in ((0, x - 1), (1, x + 1)):
            rate = half[0]
            if 0 <= neighbour < X:
                rate = rate + 0.5 * radius[0][neighbour]
                terms.append((rate, product(neighbour, k)))
            total = total + rate
        for k, edge, turn in ((2, 0, 1), (3, W - 1, W - 1)):
            near = jnp.where(row == edge, 0.0, pltpu.roll(half[1], turn, 0))
            rate = half[1] + near
            terms.append((rate, product(x, k)))
            total = total + rate
        for k, edge, turn in ((4, 0, 1), (5, Z - 1, Z - 1)):
            near = jnp.where(lane == edge, 0.0, pltpu.roll(half[2], turn, 1))
            total = total + half[2] + near
            rate = jnp.where(lane == edge, 0.0, half[2] + near)
            terms.append((rate, pltpu.roll(product(x, k), turn, 1)))
        if rates_of is None:
            rs_out[d.block(0, x), :] = total
        else:
            total = rates_of[d.block(0, x), :]
        result = d.plane3(src, x) - d.each(total) * a
        for rate, value in terms:
            result = result - d.each(rate) * value
        d.store_plane(out, x, result)
        spot = d.rows_at(x, 0)
        factor = wall_flag * radius[1][x][:1]
        coef = wall_coef[x * d.stack : x * d.stack + V, :]
        out[spot, :] = out[spot, :] - factor * coef * adj[spot, :]

    done = 0
    for start in range(0, X, step):
        here = list(range(start, min(X, start + step)))
        right = jnp.concatenate([padded_plane(d, d.plane(adj, x)) for x in here], axis=1)
        chunk = dot(mk[...], split3(right))
        for offset, x in enumerate(here):
            products[x] = (chunk, offset)
        while done < X and (done + 1 in products or (done + 1 == X and done in products)):
            finish(done)
            done += 1


def first_local_kernel(
    d, adj, src, vel, snd, couple, precond, codes, mask, table, gain,
    out, rs, mk, mw, pk, wall_coef, wide, wide_wall,
):
    make_matrices(d, couple, precond, mk, mw, pk, wide, wide_wall)
    make_wall(d, codes, mask, table, gain, wall_coef)
    sweep_local(d, adj, src, vel, snd, mk, wall_coef, None, out, rs)


def later_local_kernel(d, adj, src, vel, snd, rs, mk, wall_coef, out):
    sweep_local(d, adj, src, vel, snd, mk, wall_coef, rs, out, None)


def neighbours(axis):
    index = lax.axis_index(axis)
    return (index > 0).astype(F32), (index < lax.axis_size(axis) - 1).astype(F32)


def wall_terms(d, w0, w1, mw):
    X, W, Z, G = d.X, d.W, d.Z, d.G
    even = parity("wall")
    has_low, has_high = neighbours("wall")
    row = row_ids(d)

    def received(start, count):
        a, b = w0[pl.ds(start, count), :], w1[pl.ds(start, count), :]
        return jnp.where(even, b, a) * has_low, jnp.where(even, a, b) * has_high

    products = {}
    for start in range(0, X, 2):
        here = list(range(start, min(X, start + 2)))
        right = [jnp.concatenate(received(x * G, d.wall_k), axis=0) for x in here]
        value = dot(mw[...], split3(jnp.concatenate(right, axis=1)))
        for k, x in enumerate(here):
            products[x] = value[:, k * Z : (k + 1) * Z]

    def radius(x):
        first, last = received(x * G + d.V, 1)
        return jnp.where(row == 0, first, jnp.where(row == W - 1, last, 0.0))

    return products.get, radius


def span_terms(d, zl, zr, mk):
    V, X, W, Z, n = d.V, d.X, d.W, d.Z, d.n
    even = lax.rem(lanes(d, W), 2) == 0
    pieces = []
    for v in range(V + 1):
        q = pl.ds((v // d.per) * W, W)
        value = jnp.where(even, zl[q, :], zr[q, :])
        turn = (Z - 2 * X * (v % d.per)) % Z
        pieces.append(pltpu.roll(value, turn, 1) if turn else value)
    radius = jnp.where(even, pieces[V], pltpu.roll(pieces[V], Z - 2, 1))
    pieces += [jnp.zeros((W, Z), F32)] * (d.G - V - 1)
    both = dot(mk[4 * n :], split3(jnp.concatenate(pieces, axis=0)))
    even = lax.rem(lanes(d, n), 2) == 0
    span = jnp.where(even, both[:n], pltpu.roll(both[n:], Z - 2, 1))
    at = lambda value, x: pltpu.roll(value, (Z - 2 * x) % Z, 1) if x else value
    return lambda x: at(span, x), lambda x: at(radius, x)


def update_planes(d, planes, residual_of, adj, rs_of, pk, put):
    Z = d.Z

    def finish(here, residuals, update):
        for k, x in enumerate(here):
            inverse = 1.0 / rs_of(x)
            new = d.plane(adj, x) + update[:, k * Z : (k + 1) * Z] * d.each(inverse)
            put(x, new, residuals[k])

    waiting = None
    for start in range(0, len(planes), 2):
        here = planes[start : start + 2]
        residuals = [residual_of(x) for x in here]
        right = jnp.concatenate([padded_plane(d, r) for r in residuals], axis=1)
        update = dot(pk[...], split3(right))
        if waiting:
            finish(*waiting)
        waiting = here, residuals, update
    if waiting:
        finish(*waiting)


def first_inner_kernel(
    d, partial, adj, rs, vel, snd, w0, w1, zl, zr, mk, mw, pk,
    new_adj, rs_full, rates, edge, w_a, w_b, z_out,
):
    V, X, W, Z, n = d.V, d.X, d.W, d.Z, d.n
    span, span_radius = span_terms(d, zl, zr, mk)
    wall, wall_radius = wall_terms(d, w0, w1, mw)
    lane, row = lanes(d, W), row_ids(d)
    edge_lane = (lane == 0) | (lane == Z - 1)
    edge_row = (row == 0) | (row == W - 1)
    totals = {}

    def residual_of(x):
        from_wall = 0.5 * wall_radius(x)
        from_span = jnp.where(edge_lane, 0.5 * span_radius(x), 0.0)
        rate_wall = jnp.where(edge_row, 0.5 * radius_at(d, vel, snd, 1, x) + from_wall, 0.0)
        rate_span = jnp.where(edge_lane, 0.5 * radius_at(d, vel, snd, 2, x) + from_span, 0.0)
        correction = from_wall + from_span
        totals[x] = rs[d.block(0, x), :] + correction
        rates[d.block(0, x), :] = rate_wall
        rates[d.block(1, x), :] = rate_span
        rs_full[d.block(0, x), :] = totals[x]
        result = d.plane(partial, x) - d.each(correction) * d.plane(adj, x)
        return result - d.each(rate_wall) * wall(x) - d.each(rate_span) * span(x)

    for k, x in enumerate(d.edges):
        edge[k * n : (k + 1) * n, :] = residual_of(x)
    put = lambda x, new, _: d.store_plane(new_adj, x, new)
    update_planes(d, list(d.inner), residual_of, adj, totals.get, pk, put)
    pack_walls(d, d.inner, new_adj, None, w_a, w_b)
    pack_span(d, d.inner, lambda v, x: new_adj[d.block(v, x), :], None, None, z_out)


def later_inner_kernel(
    d, partial, adj, rs_full, rates, w0, w1, zl, zr, mk, mw, pk, new_adj, residual, edge
):
    W, n = d.W, d.n
    span, _ = span_terms(d, zl, zr, mk)
    wall, _ = wall_terms(d, w0, w1, mw)

    def residual_of(x):
        result = d.plane(partial, x) - d.each(rates[d.block(0, x), :]) * wall(x)
        return result - d.each(rates[d.block(1, x), :]) * span(x)

    def put(x, new, res):
        new_adj[d.planes_at(x, 1)] = new.reshape(d.V, W, d.Z)
        residual[d.planes_at(x, 1)] = res.reshape(d.V, W, d.Z)

    for k, x in enumerate(d.edges):
        edge[k * n : (k + 1) * n, :] = residual_of(x)
    rs_of = lambda x: rs_full[d.block(0, x), :]
    update_planes(d, list(d.inner), residual_of, adj, rs_of, pk, put)


def stream_terms(d, s0, s1, mk):
    n, Z = d.n, d.Z
    even = parity("stream")
    has_low, has_high = neighbours("stream")
    low = jnp.where(even, s1[...], s0[...]) * has_low
    high = jnp.where(even, s0[...], s1[...]) * has_high
    both = dot(mk[: 2 * n], split3(jnp.concatenate([low, high], axis=1)))
    return (both[:n, :Z], both[n:, Z:]), (low[n : n + d.W], high[n : n + d.W])


def first_stream_kernel(
    d, edge, adj, rs, vel, snd, s0, s1, mk, pk, inner, w_in0, w_in1, z_in,
    new_adj, rs_full, w_a, w_b, z_out, rates, s_a, s_b,
):
    X, W, n = d.X, d.W, d.n
    products, received = stream_terms(d, s0, s1, mk)
    totals = {}

    def residual_of(x):
        k = d.edges.index(x)
        result = edge[k * n : (k + 1) * n, :]
        totals[x] = rs[d.block(0, x), :]
        for side, at in enumerate((0, X - 1)):
            if x == at:
                rate = 0.5 * (radius_at(d, vel, snd, 0, x) + received[side])
                rates[side * W : (side + 1) * W, :] = rate
                totals[x] = totals[x] + 0.5 * received[side]
                result = result - d.each(0.5 * received[side]) * d.plane(adj, x)
                result = result - d.each(rate) * products[side]
        rs_full[d.block(0, x), :] = totals[x]
        return result

    planes = {}

    def put(x, new, _):
        d.store_plane(new_adj, x, new)
        planes[x] = new

    update_planes(d, d.edges, residual_of, adj, totals.get, pk, put)
    block_of = lambda v, x: planes[x][v * W : (v + 1) * W]
    pack_stream(d, block_of, None, s_a, s_b)
    pack_span(d, d.edges, block_of, None, z_in, z_out)
    pack_walls(d, d.edges, new_adj, None, w_a, w_b)


def later_stream_kernel(
    d, edge, adj, rs_full, rates, s0, s1, mk, pk, inner_adj, inner_residual,
    new_adj, residual, edge_adj, edge_residual, sems,
):
    X, W, Z, n = d.X, d.W, d.Z, d.n
    copies = []

    def store(source, target, part, here):
        copy = pltpu.make_async_copy(source.at[here], target.at[part], sems.at[len(copies)])
        copy.start()
        copies.append(copy)

    if len(d.inner):
        part = d.planes_at(1, len(d.inner))
        store(inner_residual, residual, part, part)
        store(inner_adj, new_adj, part, part)
    products, _ = stream_terms(d, s0, s1, mk)

    def residual_of(x):
        k = d.edges.index(x)
        result = edge[k * n : (k + 1) * n, :]
        for side, at in enumerate((0, X - 1)):
            if x == at:
                result = result - d.each(rates[side * W : (side + 1) * W, :]) * products[side]
        return result

    def put(x, new, res):
        here = d.planes_at(d.edges.index(x), 1)
        for value, held, target in (
            (res, edge_residual, residual),
            (new, edge_adj, new_adj),
        ):
            held[here] = value.reshape(d.V, W, Z)
            store(held, target, d.planes_at(x, 1), here)

    rs_of = lambda x: rs_full[d.block(0, x), :]
    update_planes(d, d.edges, residual_of, adj, rs_of, pk, put)
    for copy in copies:
        copy.wait()


def exchange_pairs(sizes, axis, odd, spare):
    ids = np.arange(int(np.prod(sizes))).reshape(sizes)
    pairs = []
    for at in np.ndindex(*sizes):
        to = list(at)
        step = 1 if (at[axis] - odd) % 2 == 0 else -1
        if at[axis] >= odd and 0 <= at[axis] + step < sizes[axis]:
            to[axis] += step
        elif (at[spare] ^ 1) < sizes[spare]:
            to[spare] ^= 1
        else:
            continue
        pairs.append((int(ids[at]), int(ids[tuple(to)])))
    return pairs


def swap_lines(sizes, s_a, s_b, w_a, w_b, z):
    move = lambda value, pairs: lax.ppermute(value, AXES, pairs)
    s0 = move(s_a, exchange_pairs(sizes, 0, 0, 2))
    s1 = move(s_b, exchange_pairs(sizes, 0, 1, 2))
    w1 = move(w_b, exchange_pairs(sizes, 2, 1, 1))
    w0 = move(w_a, exchange_pairs(sizes, 2, 0, 1))
    peers = sizes[1]
    if peers == 1:
        zl = zr = z
    elif peers == 2:
        zl = zr = lax.ppermute(z, "span", [(0, 1), (1, 0)])
    else:
        up = [(i, (i + 1) % peers) for i in range(peers)]
        zl = lax.ppermute(z, "span", up)
        zr = lax.ppermute(z, "span", [(j, i) for i, j in up])
    return s0, s1, w0, w1, zl, zr


def call(kernel, d, outs, flops, args, held=(), scratch=(), out_held=False, aliases=None):
    space = lambda k: pltpu.HBM if k in held else pltpu.VMEM
    out_space = pltpu.HBM if out_held else pltpu.VMEM
    args = [pltpu.with_memory_space_constraint(a, space(k)) for k, a in enumerate(args)]
    moved = sum(int(np.prod(a.shape)) * a.dtype.itemsize for a in args)
    return pl.pallas_call(
        functools.partial(kernel, d),
        out_shape=tuple(out_space(s, t) for s, t in outs),
        in_specs=[pl.BlockSpec(memory_space=space(k)) for k in range(len(args))],
        out_specs=tuple(pl.BlockSpec(memory_space=out_space) for _ in outs),
        scratch_shapes=scratch,
        input_output_aliases=aliases or {},
        compiler_params=pltpu.CompilerParams(vmem_limit_bytes=24 * 2**20),
        cost_estimate=pl.CostEstimate(flops=flops, bytes_accessed=moved, transcendentals=0),
        name=kernel.__name__,
    )(*args)


def on_device(sizes, adj, source, velocity, sound, couple, precond, codes, mask, table, gain):
    shape = adj.shape
    d = Dims(shape)
    V, X, W, Z, B, n = d.V, d.X, d.W, d.Z, d.B, d.n
    inputs = [
        adj.reshape(d.rows, Z),
        velocity.reshape(3 * X * W, Z),
        sound.reshape(X * W, Z),
        precond,
        codes,
        mask,
        table,
        gain.reshape(1, -1),
    ]
    source = source.reshape(V, X * W, Z)
    faces = [((B, Z), F32)] * 2 + [((d.wall_rows, Z), F32)] * 2 + [((d.span_groups * W, Z), F32)]
    field, scalar = ((d.rows, Z), F32), ((X * W, Z), F32)
    planes = ((V, X * W, Z), F32)
    sems = lambda *counts: pltpu.SemaphoreType.DMA(counts)
    *kept, s_a, s_b, w_a, w_b, z = call(
        pack_kernel,
        d,
        [(a.shape, a.dtype) for a in inputs] + faces,
        0,
        inputs,
        held=range(len(inputs)),
        scratch=[sems(len(inputs))],
    )
    adj, velocity, sound = kept[:3]
    got = swap_lines(sizes, s_a, s_b, w_a, w_b, z)
    partial, rs, mk, mw, pk, wall_coef = call(
        first_local_kernel,
        d,
        [
            field,
            scalar,
            ((6 * n, 3 * B), BF16),
            ((n, 6 * d.wall_k), BF16),
            ((n, 3 * B), BF16),
            ((X * d.stack, Z), F32),
        ],
        10**9,
        [adj, source, velocity, sound, couple] + kept[3:],
        scratch=[pltpu.VMEM((7 * d.stack, 3 * B), F32), pltpu.VMEM((2 * d.stack, 6 * d.wall_k), F32)],
    )
    s0, s1, w0, w1, zl, zr = got
    edge = ((len(d.edges) * n, Z), F32)
    inner, rs, rates, held, w_a, w_b, z = call(
        first_inner_kernel,
        d,
        [field, scalar, ((2 * X * W, Z), F32), edge] + faces[2:],
        10**8,
        [partial, adj, rs, velocity, sound, w0, w1, zl, zr, mk, mw, pk],
    )
    adj1, rs, w_a, w_b, z, stream_rates, s_a, s_b = call(
        first_stream_kernel,
        d,
        [field, scalar] + faces[2:] + [((2 * W, Z), F32)] + faces[:2],
        10**7,
        [held, adj, rs, velocity, sound, s0, s1, mk, pk, inner, w_a, w_b, z],
        aliases={9: 0, 2: 1, 10: 2, 11: 3, 12: 4},
    )
    s0, s1, w0, w1, zl, zr = swap_lines(sizes, s_a, s_b, w_a, w_b, z)
    (partial,) = call(
        later_local_kernel,
        d,
        [field],
        10**9,
        [adj1, source, velocity, sound, rs, mk, wall_coef],
    )
    inner, inner_residual, held = call(
        later_inner_kernel,
        d,
        [planes, planes, edge],
        10**8,
        [partial, adj1, rs, rates, w0, w1, zl, zr, mk, mw, pk],
    )
    edge = ((V, len(d.edges) * W, Z), F32)
    adj2, residual = call(
        later_stream_kernel,
        d,
        [planes, planes],
        10**7,
        [held, adj1, rs, stream_rates, s0, s1, mk, pk, inner, inner_residual],
        scratch=[pltpu.VMEM(*edge), pltpu.VMEM(*edge), sems(2 + 2 * len(d.edges))],
        out_held=True,
    )
    return adj2.reshape(shape), residual.reshape(shape)


def solution(mesh):
    sizes = tuple(mesh.shape[a] for a in AXES)
    field = P(None, "stream", "wall", "span")
    return jax.shard_map(
        functools.partial(on_device, sizes),
        mesh=mesh,
        in_specs=(field, field, field, P("stream", "wall", "span")) + (P(),) * 6,
        out_specs=(field, field),
        check_vma=False,
    )
```

```python
import functools

import jax
import jax.numpy as jnp
import numpy as np
from jax import lax
from jax.experimental import pallas as pl
from jax.experimental.pallas import tpu as pltpu
from jax.sharding import PartitionSpec as P

AXES = ("stream", "span", "wall")
F32 = jnp.float32
BF16 = jnp.bfloat16


class Dims:
    def __init__(self, shape):
        self.V, self.X, self.W, self.Z = shape
        self.G = self.V + 1
        while self.G * self.W % 16:
            self.G += 1
        self.B = self.G * self.W
        self.n = self.V * self.W
        self.rows = self.n * self.X
        self.edges = sorted({0, self.X - 1})
        self.inner = range(1, self.X - 1)
        self.wall_rows = self.X * self.G + 8
        self.wall_k = -(-self.G // 8) * 8
        self.stack = -(-self.V // 8) * 8
        self.per = self.Z // (2 * self.X)
        self.span_groups = -(-(self.V + 1) // self.per)

    def block(self, group, x):
        return pl.ds((group * self.X + x) * self.W, self.W)

    def rows_at(self, x, w):
        return pl.ds(x * self.W + w, self.V, stride=self.X * self.W)

    def plane(self, ref, x):
        return jnp.concatenate([ref[self.block(v, x), :] for v in range(self.V)], axis=0)

    def store_plane(self, ref, x, value):
        for v in range(self.V):
            ref[self.block(v, x), :] = value[v * self.W : (v + 1) * self.W]

    def plane3(self, ref, x):
        return ref[:, x * self.W : (x + 1) * self.W, :].reshape(self.n, self.Z)

    def planes_at(self, start, count):
        return (slice(None), pl.ds(start * self.W, count * self.W), slice(None))

    def each(self, factor):
        return jnp.concatenate([factor] * self.V, axis=0)


def lanes(d, rows):
    return lax.broadcasted_iota(jnp.int32, (rows, d.Z), 1)


def row_ids(d):
    return lax.broadcasted_iota(jnp.int32, (d.W, d.Z), 0)


def radius_at(d, vel, snd, direction, x):
    return jnp.abs(vel[d.block(direction, x), :]) + snd[d.block(0, x), :]


def split3(value):
    high = value.astype(BF16)
    low = (value - high.astype(F32)).astype(BF16)
    return jnp.concatenate([high, low, high], axis=0)


def padded_plane(d, value):
    extra = d.B - value.shape[0]
    if not extra:
        return value
    return jnp.concatenate([value, jnp.zeros((extra, value.shape[1]), F32)], axis=0)


def dot(a, b):
    return jnp.dot(a, b, preferred_element_type=F32)


def pack_stream(d, block_of, radius_of, s_a, s_b):
    W, even = d.W, parity("stream")
    for g in range(d.G):
        if g < d.V:
            first, last = block_of(g, 0), block_of(g, d.X - 1)
        elif g == d.V and radius_of is not None:
            first, last = radius_of(0, 0), radius_of(0, d.X - 1)
        else:
            first = last = jnp.zeros((W, d.Z), F32)
        s_a[g * W : (g + 1) * W, :] = jnp.where(even, last, first)
        s_b[g * W : (g + 1) * W, :] = jnp.where(even, first, last)


def pack_span(d, planes, block_of, radius_of, given, z_out):
    V, X, W, Z = d.V, d.X, d.W, d.Z
    pair = lanes(d, W) // 2
    for q in range(d.span_groups):
        rows = pl.ds(q * W, W)
        group = jnp.zeros((W, Z), F32) if given is None else given[rows, :]
        for v in range(q * d.per, min(V + 1, (q + 1) * d.per)):
            if v == V and radius_of is None:
                continue
            for x in planes:
                value = block_of(v, x) if v < V else radius_of(2, x)
                spot = X * (v % d.per) + x
                group = jnp.where(pair == spot, pltpu.roll(value, (2 * spot + 1) % Z, 1), group)
        z_out[rows, :] = group


def pack_walls(d, planes, adj, radius_of, w_a, w_b):
    V, X, W, Z, G = d.V, d.X, d.W, d.Z, d.G
    even = parity("wall")
    tail = jnp.zeros((G - V, Z), F32)
    for x in planes:
        first, last = adj[d.rows_at(x, 0), :], adj[d.rows_at(x, W - 1), :]
        w_a[x * G : x * G + V, :] = jnp.where(even, last, first)
        w_b[x * G : x * G + V, :] = jnp.where(even, first, last)
        if radius_of is None or G - V > 1:
            w_a[x * G + V : (x + 1) * G, :] = tail
            w_b[x * G + V : (x + 1) * G, :] = tail
        if radius_of is not None:
            radius = radius_of(1, x)
            first, last = radius[:1], radius[W - 1 :]
            w_a[x * G + V : x * G + V + 1, :] = jnp.where(even, last, first)
            w_b[x * G + V : x * G + V + 1, :] = jnp.where(even, first, last)
    if X - 1 in planes:
        w_a[X * G :, :] = jnp.zeros((8, Z), F32)
        w_b[X * G :, :] = jnp.zeros((8, Z), F32)


def parity(axis):
    return lax.rem(lax.axis_index(axis), 2) == 0


def pack_kernel(d, *refs):
    count = (len(refs) - 6) // 2
    held, kept = refs[:count], refs[count : 2 * count]
    s_a, s_b, w_a, w_b, z_out, sems = refs[2 * count :]
    adj, vel, snd = kept[:3]
    copies = [pltpu.make_async_copy(held[k], kept[k], sems.at[k]) for k in range(count)]
    for copy in copies:
        copy.start()
    for copy in copies:
        copy.wait()
    block_of = lambda v, x: adj[d.block(v, x), :]
    radius_of = functools.partial(radius_at, d, vel, snd)
    pack_stream(d, block_of, radius_of, s_a, s_b)
    pack_span(d, range(d.X), block_of, radius_of, None, z_out)
    pack_walls(d, range(d.X), adj, radius_of, w_a, w_b)


def make_matrices(d, couple, precond, mk, mw, pk, wide, wide_wall):
    V, W, B, n, K, S = d.V, d.W, d.B, d.n, d.wall_k, d.stack
    gap = jnp.zeros((V, S - V), F32)
    blocks = [couple[k // 2, :, k % 2, :] for k in range(6)] + [precond[...].T]
    blocks = [piece for m in blocks for piece in ((m, gap) if S > V else (m,))]
    blocks = jnp.concatenate(blocks, axis=1)
    high = blocks.astype(BF16).astype(F32)
    gap = jnp.zeros((S - V, 7 * S), F32)
    pieces = (high, gap, blocks - high, gap) if S > V else (high, blocks - high)
    blocks = jnp.concatenate(pieces, axis=0).astype(BF16)
    dims = (((0,), (0,)), ((), ()))

    def spread(some, width, keep):
        row = lax.broadcasted_iota(jnp.int32, (2 * S, 3 * width), 0)
        col = lax.broadcasted_iota(jnp.int32, (2 * S, 3 * width), 1)
        part = keep(lax.rem(col, width), jnp.where(row < S, row, row - S))
        part = part & ((row < S) == (col < 2 * width))
        return lax.dot_general(some, part.astype(BF16), dims, preferred_element_type=F32)

    wide[...] = spread(blocks, B, lambda col, v: col // W == v)
    sides = []
    for side in range(2):
        some = blocks[:, (2 + side) * S : (3 + side) * S]
        sides.append(spread(some, 2 * K, lambda col, v: col - side * K == v))
    wide_wall[...] = jnp.concatenate(sides, axis=0)
    row = lax.broadcasted_iota(jnp.int32, (W, 3 * B), 0)
    col = lax.rem(lax.broadcasted_iota(jnp.int32, (W, 3 * B), 1), W)
    same, lower, upper = [(col - row == k).astype(F32) for k in (0, -1, 1)]

    def rows(k):
        mask = {2: lower, 3: upper}.get(k, same)
        return [wide[pl.ds(k * S + v, 1), :] * mask for v in range(V)]

    for k in range(0, 6, 2):
        both = jnp.concatenate(rows(k) + rows(k + 1), axis=0)
        mk[k * n : (k + 2) * n, :] = both.astype(BF16)
    pk[...] = jnp.concatenate(rows(6), axis=0).astype(BF16)
    row = lax.broadcasted_iota(jnp.int32, (W, 6 * K), 0)
    first, last = (row == 0).astype(F32), (row == W - 1).astype(F32)
    pieces = [
        wide_wall[pl.ds(v, 1), :] * first + wide_wall[pl.ds(S + v, 1), :] * last for v in range(V)
    ]
    mw[...] = jnp.concatenate(pieces, axis=0).astype(BF16)


def make_wall(d, codes, mask, table, gain, wall_out):
    X, Z, V, S = d.X, d.Z, d.V, d.stack
    place = lax.axis_index("stream")
    lane0 = pl.multiple_of(lax.axis_index("span") * Z, Z)
    kinds = table.shape[0]

    def window(ref):
        value = ref[:X, pl.ds(lane0, Z)]
        for s in range(1, lax.axis_size("stream")):
            value = jnp.where(place == s, ref[s * X : (s + 1) * X, pl.ds(lane0, Z)], value)
        return value

    code, spall = window(codes), window(mask).astype(F32)
    column = lambda values: jnp.broadcast_to(values.T, (V, Z))
    columns = [column(table[k : k + 1, :]) for k in range(kinds)]
    gains = column(gain[...])
    for x in range(X):
        here = jnp.broadcast_to(code[x : x + 1], (V, Z))
        coef = columns[kinds - 1]
        for k in range(kinds - 1):
            coef = jnp.where(here == k, columns[k], coef)
        wall_out[x * S : x * S + V, :] = coef + gains * spall[x : x + 1]


def sweep_local(d, adj, src, vel, snd, mk, wall_coef, rates_of, out, rs_out):
    V, X, W, Z, n = d.V, d.X, d.W, d.Z, d.n
    lane, row = lanes(d, W), row_ids(d)
    wall_flag = (lax.axis_index("wall") == 0).astype(F32)
    radius = [[radius_at(d, vel, snd, k, x) for x in range(X)] for k in range(3)]
    step = 2
    products = {}

    def product(x, k):
        chunk, offset = products[x]
        return chunk[k * n : (k + 1) * n, offset * Z : (offset + 1) * Z]

    def finish(x):
        a = d.plane(adj, x)
        total = 1.0
        terms = []
        half = [0.5 * radius[k][x] for k in range(3)]
        for k, neighbour in ((0, x - 1), (1, x + 1)):
            rate = half[0]
            if 0 <= neighbour < X:
                rate = rate + 0.5 * radius[0][neighbour]
                terms.append((rate, product(neighbour, k)))
            total = total + rate
        for k, edge, turn in ((2, 0, 1), (3, W - 1, W - 1)):
            near = jnp.where(row == edge, 0.0, pltpu.roll(half[1], turn, 0))
            rate = half[1] + near
            terms.append((rate, product(x, k)))
            total = total + rate
        for k, edge, turn in ((4, 0, 1), (5, Z - 1, Z - 1)):
            near = jnp.where(lane == edge, 0.0, pltpu.roll(half[2], turn, 1))
            total = total + half[2] + near
            rate = jnp.where(lane == edge, 0.0, half[2] + near)
            terms.append((rate, pltpu.roll(product(x, k), turn, 1)))
        if rates_of is None:
            rs_out[d.block(0, x), :] = total
        else:
            total = rates_of[d.block(0, x), :]
        result = d.plane3(src, x) - d.each(total) * a
        for rate, value in terms:
            result = result - d.each(rate) * value
        d.store_plane(out, x, result)
        spot = d.rows_at(x, 0)
        factor = wall_flag * radius[1][x][:1]
        coef = wall_coef[x * d.stack : x * d.stack + V, :]
        out[spot, :] = out[spot, :] - factor * coef * adj[spot, :]

    done = 0
    for start in range(0, X, step):
        here = list(range(start, min(X, start + step)))
        right = jnp.concatenate([padded_plane(d, d.plane(adj, x)) for x in here], axis=1)
        chunk = dot(mk[...], split3(right))
        for offset, x in enumerate(here):
            products[x] = (chunk, offset)
        while done < X and (done + 1 in products or (done + 1 == X and done in products)):
            finish(done)
            done += 1


def early():
    return 2 * lax.axis_index("stream") < lax.axis_size("stream")


def early_kernel(d, couple, precond, codes, mask, table, gain, *refs):
    mk, mw, pk, wall_coef = refs[5:9]
    wide, wide_wall = refs[-2:]

    @pl.when(early())
    def _():
        make_matrices(d, couple, precond, mk, mw, pk, wide, wide_wall)
        make_wall(d, codes, mask, table, gain, wall_coef)


def first_local_kernel(
    d, adj, src, vel, snd, couple, precond, codes, mask, table, gain, _mk, _mw, _pk, _wall_coef,
    out, rs, mk, mw, pk, wall_coef, wide, wide_wall,
):
    @pl.when(jnp.logical_not(early()))
    def _():
        make_matrices(d, couple, precond, mk, mw, pk, wide, wide_wall)
        make_wall(d, codes, mask, table, gain, wall_coef)

    sweep_local(d, adj, src, vel, snd, mk, wall_coef, None, out, rs)


def later_local_kernel(d, adj, src, vel, snd, rs, mk, wall_coef, out):
    sweep_local(d, adj, src, vel, snd, mk, wall_coef, rs, out, None)


def neighbours(axis):
    index = lax.axis_index(axis)
    return (index > 0).astype(F32), (index < lax.axis_size(axis) - 1).astype(F32)


def wall_terms(d, w0, w1, mw):
    X, W, Z, G = d.X, d.W, d.Z, d.G
    even = parity("wall")
    has_low, has_high = neighbours("wall")
    row = row_ids(d)

    def received(start, count):
        a, b = w0[pl.ds(start, count), :], w1[pl.ds(start, count), :]
        return jnp.where(even, b, a) * has_low, jnp.where(even, a, b) * has_high

    products = {}
    for start in range(0, X, 2):
        here = list(range(start, min(X, start + 2)))
        right = [jnp.concatenate(received(x * G, d.wall_k), axis=0) for x in here]
        value = dot(mw[...], split3(jnp.concatenate(right, axis=1)))
        for k, x in enumerate(here):
            products[x] = value[:, k * Z : (k + 1) * Z]

    def radius(x):
        first, last = received(x * G + d.V, 1)
        return jnp.where(row == 0, first, jnp.where(row == W - 1, last, 0.0))

    return products.get, radius


def span_terms(d, zl, zr, mk):
    V, X, W, Z, n = d.V, d.X, d.W, d.Z, d.n
    even = lax.rem(lanes(d, W), 2) == 0
    pieces = []
    for v in range(V + 1):
        q = pl.ds((v // d.per) * W, W)
        value = jnp.where(even, zl[q, :], zr[q, :])
        turn = (Z - 2 * X * (v % d.per)) % Z
        pieces.append(pltpu.roll(value, turn, 1) if turn else value)
    radius = jnp.where(even, pieces[V], pltpu.roll(pieces[V], Z - 2, 1))
    pieces += [jnp.zeros((W, Z), F32)] * (d.G - V - 1)
    both = dot(mk[4 * n :], split3(jnp.concatenate(pieces, axis=0)))
    even = lax.rem(lanes(d, n), 2) == 0
    span = jnp.where(even, both[:n], pltpu.roll(both[n:], Z - 2, 1))
    at = lambda value, x: pltpu.roll(value, (Z - 2 * x) % Z, 1) if x else value
    return lambda x: at(span, x), lambda x: at(radius, x)


def update_planes(d, planes, residual_of, adj, rs_of, pk, put):
    Z = d.Z

    def finish(here, residuals, update):
        for k, x in enumerate(here):
            inverse = 1.0 / rs_of(x)
            new = d.plane(adj, x) + update[:, k * Z : (k + 1) * Z] * d.each(inverse)
            put(x, new, residuals[k])

    waiting = None
    for start in range(0, len(planes), 2):
        here = planes[start : start + 2]
        residuals = [residual_of(x) for x in here]
        right = jnp.concatenate([padded_plane(d, r) for r in residuals], axis=1)
        update = dot(pk[...], split3(right))
        if waiting:
            finish(*waiting)
        waiting = here, residuals, update
    if waiting:
        finish(*waiting)


def first_inner_kernel(
    d, partial, adj, rs, vel, snd, w0, w1, zl, zr, mk, mw, pk,
    new_adj, rs_full, rates, edge, w_a, w_b, z_out,
):
    V, X, W, Z, n = d.V, d.X, d.W, d.Z, d.n
    span, span_radius = span_terms(d, zl, zr, mk)
    wall, wall_radius = wall_terms(d, w0, w1, mw)
    lane, row = lanes(d, W), row_ids(d)
    edge_lane = (lane == 0) | (lane == Z - 1)
    edge_row = (row == 0) | (row == W - 1)
    totals = {}

    def residual_of(x):
        from_wall = 0.5 * wall_radius(x)
        from_span = jnp.where(edge_lane, 0.5 * span_radius(x), 0.0)
        rate_wall = jnp.where(edge_row, 0.5 * radius_at(d, vel, snd, 1, x) + from_wall, 0.0)
        rate_span = jnp.where(edge_lane, 0.5 * radius_at(d, vel, snd, 2, x) + from_span, 0.0)
        correction = from_wall + from_span
        totals[x] = rs[d.block(0, x), :] + correction
        rates[d.block(0, x), :] = rate_wall
        rates[d.block(1, x), :] = rate_span
        rs_full[d.block(0, x), :] = totals[x]
        result = d.plane(partial, x) - d.each(correction) * d.plane(adj, x)
        return result - d.each(rate_wall) * wall(x) - d.each(rate_span) * span(x)

    for k, x in enumerate(d.edges):
        edge[k * n : (k + 1) * n, :] = residual_of(x)
    put = lambda x, new, _: d.store_plane(new_adj, x, new)
    update_planes(d, list(d.inner), residual_of, adj, totals.get, pk, put)
    pack_walls(d, d.inner, new_adj, None, w_a, w_b)
    pack_span(d, d.inner, lambda v, x: new_adj[d.block(v, x), :], None, None, z_out)


def later_inner_kernel(
    d, partial, adj, rs_full, rates, w0, w1, zl, zr, mk, mw, pk, new_adj, residual, edge
):
    W, n = d.W, d.n
    span, _ = span_terms(d, zl, zr, mk)
    wall, _ = wall_terms(d, w0, w1, mw)

    def residual_of(x):
        result = d.plane(partial, x) - d.each(rates[d.block(0, x), :]) * wall(x)
        return result - d.each(rates[d.block(1, x), :]) * span(x)

    def put(x, new, res):
        new_adj[d.planes_at(x, 1)] = new.reshape(d.V, W, d.Z)
        residual[d.planes_at(x, 1)] = res.reshape(d.V, W, d.Z)

    for k, x in enumerate(d.edges):
        edge[k * n : (k + 1) * n, :] = residual_of(x)
    rs_of = lambda x: rs_full[d.block(0, x), :]
    update_planes(d, list(d.inner), residual_of, adj, rs_of, pk, put)


def stream_terms(d, s0, s1, mk):
    n, Z = d.n, d.Z
    even = parity("stream")
    has_low, has_high = neighbours("stream")
    low = jnp.where(even, s1[...], s0[...]) * has_low
    high = jnp.where(even, s0[...], s1[...]) * has_high
    both = dot(mk[: 2 * n], split3(jnp.concatenate([low, high], axis=1)))
    return (both[:n, :Z], both[n:, Z:]), (low[n : n + d.W], high[n : n + d.W])


def first_stream_kernel(
    d, edge, adj, rs, vel, snd, s0, s1, mk, pk, inner, w_in0, w_in1, z_in,
    new_adj, rs_full, w_a, w_b, z_out, rates, s_a, s_b,
):
    X, W, n = d.X, d.W, d.n
    products, received = stream_terms(d, s0, s1, mk)
    totals = {}

    def residual_of(x):
        k = d.edges.index(x)
        result = edge[k * n : (k + 1) * n, :]
        totals[x] = rs[d.block(0, x), :]
        for side, at in enumerate((0, X - 1)):
            if x == at:
                rate = 0.5 * (radius_at(d, vel, snd, 0, x) + received[side])
                rates[side * W : (side + 1) * W, :] = rate
                totals[x] = totals[x] + 0.5 * received[side]
                result = result - d.each(0.5 * received[side]) * d.plane(adj, x)
                result = result - d.each(rate) * products[side]
        rs_full[d.block(0, x), :] = totals[x]
        return result

    planes = {}

    def put(x, new, _):
        d.store_plane(new_adj, x, new)
        planes[x] = new

    update_planes(d, d.edges, residual_of, adj, totals.get, pk, put)
    block_of = lambda v, x: planes[x][v * W : (v + 1) * W]
    pack_stream(d, block_of, None, s_a, s_b)
    pack_span(d, d.edges, block_of, None, z_in, z_out)
    pack_walls(d, d.edges, new_adj, None, w_a, w_b)


def later_stream_kernel(
    d, edge, adj, rs_full, rates, s0, s1, mk, pk, inner_adj, inner_residual,
    new_adj, residual, edge_adj, edge_residual, sems,
):
    X, W, Z, n = d.X, d.W, d.Z, d.n
    copies = []

    def store(source, target, part, here):
        copy = pltpu.make_async_copy(source.at[here], target.at[part], sems.at[len(copies)])
        copy.start()
        copies.append(copy)

    if len(d.inner):
        part = d.planes_at(1, len(d.inner))
        store(inner_residual, residual, part, part)
        store(inner_adj, new_adj, part, part)
    products, _ = stream_terms(d, s0, s1, mk)

    def residual_of(x):
        k = d.edges.index(x)
        result = edge[k * n : (k + 1) * n, :]
        for side, at in enumerate((0, X - 1)):
            if x == at:
                result = result - d.each(rates[side * W : (side + 1) * W, :]) * products[side]
        return result

    def put(x, new, res):
        here = d.planes_at(d.edges.index(x), 1)
        for value, held, target in (
            (res, edge_residual, residual),
            (new, edge_adj, new_adj),
        ):
            held[here] = value.reshape(d.V, W, Z)
            store(held, target, d.planes_at(x, 1), here)

    rs_of = lambda x: rs_full[d.block(0, x), :]
    update_planes(d, d.edges, residual_of, adj, rs_of, pk, put)
    for copy in copies:
        copy.wait()


def exchange_pairs(sizes, axis, odd, spare):
    ids = np.arange(int(np.prod(sizes))).reshape(sizes)
    pairs = []
    for at in np.ndindex(*sizes):
        to = list(at)
        step = 1 if (at[axis] - odd) % 2 == 0 else -1
        if at[axis] >= odd and 0 <= at[axis] + step < sizes[axis]:
            to[axis] += step
        elif (at[spare] ^ 1) < sizes[spare]:
            to[spare] ^= 1
        else:
            continue
        pairs.append((int(ids[at]), int(ids[tuple(to)])))
    return pairs


def swap_lines(sizes, s_a, s_b, w_a, w_b, z):
    move = lambda value, pairs: lax.ppermute(value, AXES, pairs)
    s0 = move(s_a, exchange_pairs(sizes, 0, 0, 2))
    s1 = move(s_b, exchange_pairs(sizes, 0, 1, 2))
    w1 = move(w_b, exchange_pairs(sizes, 2, 1, 1))
    w0 = move(w_a, exchange_pairs(sizes, 2, 0, 1))
    peers = sizes[1]
    if peers == 1:
        zl = zr = z
    elif peers == 2:
        zl = zr = lax.ppermute(z, "span", [(0, 1), (1, 0)])
    else:
        up = [(i, (i + 1) % peers) for i in range(peers)]
        zl = lax.ppermute(z, "span", up)
        zr = lax.ppermute(z, "span", [(j, i) for i, j in up])
    return s0, s1, w0, w1, zl, zr


def call(kernel, d, outs, flops, args, held=(), scratch=(), out_held=False, aliases=None):
    space = lambda k: pltpu.HBM if k in held else pltpu.VMEM
    out_space = pltpu.HBM if out_held else pltpu.VMEM
    args = [pltpu.with_memory_space_constraint(a, space(k)) for k, a in enumerate(args)]
    moved = sum(int(np.prod(a.shape)) * a.dtype.itemsize for a in args)
    return pl.pallas_call(
        functools.partial(kernel, d),
        out_shape=tuple(out_space(s, t) for s, t in outs),
        in_specs=[pl.BlockSpec(memory_space=space(k)) for k in range(len(args))],
        out_specs=tuple(pl.BlockSpec(memory_space=out_space) for _ in outs),
        scratch_shapes=scratch,
        input_output_aliases=aliases or {},
        compiler_params=pltpu.CompilerParams(vmem_limit_bytes=24 * 2**20),
        cost_estimate=pl.CostEstimate(flops=flops, bytes_accessed=moved, transcendentals=0),
        name=kernel.__name__,
    )(*args)


def on_device(sizes, adj, source, velocity, sound, couple, precond, codes, mask, table, gain):
    shape = adj.shape
    d = Dims(shape)
    V, X, W, Z, B, n = d.V, d.X, d.W, d.Z, d.B, d.n
    inputs = [
        adj.reshape(d.rows, Z),
        velocity.reshape(3 * X * W, Z),
        sound.reshape(X * W, Z),
        couple.transpose(0, 2, 1, 3),
        precond,
        codes,
        mask,
        table,
        gain.reshape(1, -1),
    ]
    source = source.reshape(V, X * W, Z)
    faces = [((B, Z), F32)] * 2 + [((d.wall_rows, Z), F32)] * 2 + [((d.span_groups * W, Z), F32)]
    field, scalar = ((d.rows, Z), F32), ((X * W, Z), F32)
    planes = ((V, X * W, Z), F32)
    sems = lambda *counts: pltpu.SemaphoreType.DMA(counts)
    *kept, s_a, s_b, w_a, w_b, z = call(
        pack_kernel,
        d,
        [(a.shape, a.dtype) for a in inputs] + faces,
        0,
        inputs,
        held=range(len(inputs)),
        scratch=[sems(len(inputs))],
    )
    adj, velocity, sound = kept[:3]
    made = [
        ((6 * n, 3 * B), BF16),
        ((n, 6 * d.wall_k), BF16),
        ((n, 3 * B), BF16),
        ((X * d.stack, Z), F32),
    ]
    room = [pltpu.VMEM((7 * d.stack, 3 * B), F32), pltpu.VMEM((2 * d.stack, 6 * d.wall_k), F32)]
    params = kept[3:]
    *matrices, s_a, s_b, w_a, w_b, z = call(
        early_kernel,
        d,
        made + faces,
        0,
        params + [s_a, s_b, w_a, w_b, z],
        scratch=room,
        aliases={len(params) + k: len(made) + k for k in range(5)},
    )
    got = swap_lines(sizes, s_a, s_b, w_a, w_b, z)
    partial, rs, mk, mw, pk, wall_coef = call(
        first_local_kernel,
        d,
        [field, scalar] + made,
        10**9,
        [adj, source, velocity, sound] + params + matrices,
        scratch=room,
        aliases={4 + len(params) + k: 2 + k for k in range(len(made))},
    )
    s0, s1, w0, w1, zl, zr = got
    edge = ((len(d.edges) * n, Z), F32)
    inner, rs, rates, held, w_a, w_b, z = call(
        first_inner_kernel,
        d,
        [field, scalar, ((2 * X * W, Z), F32), edge] + faces[2:],
        10**8,
        [partial, adj, rs, velocity, sound, w0, w1, zl, zr, mk, mw, pk],
    )
    adj1, rs, w_a, w_b, z, stream_rates, s_a, s_b = call(
        first_stream_kernel,
        d,
        [field, scalar] + faces[2:] + [((2 * W, Z), F32)] + faces[:2],
        10**7,
        [held, adj, rs, velocity, sound, s0, s1, mk, pk, inner, w_a, w_b, z],
        aliases={9: 0, 2: 1, 10: 2, 11: 3, 12: 4},
    )
    s0, s1, w0, w1, zl, zr = swap_lines(sizes, s_a, s_b, w_a, w_b, z)
    (partial,) = call(
        later_local_kernel,
        d,
        [field],
        10**9,
        [adj1, source, velocity, sound, rs, mk, wall_coef],
    )
    inner, inner_residual, held = call(
        later_inner_kernel,
        d,
        [planes, planes, edge],
        10**8,
        [partial, adj1, rs, rates, w0, w1, zl, zr, mk, mw, pk],
    )
    edge = ((V, len(d.edges) * W, Z), F32)
    adj2, residual = call(
        later_stream_kernel,
        d,
        [planes, planes],
        10**7,
        [held, adj1, rs, stream_rates, s0, s1, mk, pk, inner, inner_residual],
        scratch=[pltpu.VMEM(*edge), pltpu.VMEM(*edge), sems(2 + 2 * len(d.edges))],
        out_held=True,
    )
    return adj2.reshape(shape), residual.reshape(shape)


def solution(mesh):
    sizes = tuple(mesh.shape[a] for a in AXES)
    field = P(None, "stream", "wall", "span")
    return jax.shard_map(
        functools.partial(on_device, sizes),
        mesh=mesh,
        in_specs=(field, field, field, P("stream", "wall", "span")) + (P(),) * 6,
        out_specs=(field, field),
        check_vma=False,
    )
```

```python
import functools

import jax
import jax.numpy as jnp
import numpy as np
from jax import lax
from jax.experimental import pallas as pl
from jax.experimental.pallas import tpu as pltpu
from jax.sharding import PartitionSpec as P

AXES = ("stream", "span", "wall")
F32 = jnp.float32
BF16 = jnp.bfloat16


class Dims:
    def __init__(self, shape):
        self.V, self.X, self.W, self.Z = shape
        self.G = self.V + 1
        while self.G * self.W % 16:
            self.G += 1
        self.B = self.G * self.W
        self.n = self.V * self.W
        self.rows = self.n * self.X
        self.edges = sorted({0, self.X - 1})
        self.inner = range(1, self.X - 1)
        self.wall_rows = self.X * self.G + 8
        self.wall_k = -(-self.G // 8) * 8
        self.stack = -(-self.V // 8) * 8
        self.per = self.Z // (2 * self.X)
        self.span_groups = -(-(self.V + 1) // self.per)

    def block(self, group, x):
        return pl.ds((group * self.X + x) * self.W, self.W)

    def rows_at(self, x, w):
        return pl.ds(x * self.W + w, self.V, stride=self.X * self.W)

    def plane(self, ref, x):
        return jnp.concatenate([ref[self.block(v, x), :] for v in range(self.V)], axis=0)

    def store_plane(self, ref, x, value):
        for v in range(self.V):
            ref[self.block(v, x), :] = value[v * self.W : (v + 1) * self.W]

    def plane3(self, ref, x):
        return ref[:, x * self.W : (x + 1) * self.W, :].reshape(self.n, self.Z)

    def planes_at(self, start, count):
        return (slice(None), pl.ds(start * self.W, count * self.W), slice(None))

    def each(self, factor):
        return jnp.concatenate([factor] * self.V, axis=0)


def lanes(d, rows):
    return lax.broadcasted_iota(jnp.int32, (rows, d.Z), 1)


def row_ids(d):
    return lax.broadcasted_iota(jnp.int32, (d.W, d.Z), 0)


def radius_at(d, vel, snd, direction, x):
    return jnp.abs(vel[d.block(direction, x), :]) + snd[d.block(0, x), :]


def split3(value):
    high = value.astype(BF16)
    low = (value - high.astype(F32)).astype(BF16)
    return jnp.concatenate([high, low, high], axis=0)


def padded_plane(d, value):
    extra = d.B - value.shape[0]
    if not extra:
        return value
    return jnp.concatenate([value, jnp.zeros((extra, value.shape[1]), F32)], axis=0)


def dot(a, b):
    return jnp.dot(a, b, preferred_element_type=F32)


def pack_stream(d, block_of, radius_of, s_a, s_b):
    W, even = d.W, parity("stream")
    for g in range(d.G):
        if g < d.V:
            first, last = block_of(g, 0), block_of(g, d.X - 1)
        elif g == d.V and radius_of is not None:
            first, last = radius_of(0, 0), radius_of(0, d.X - 1)
        else:
            first = last = jnp.zeros((W, d.Z), F32)
        s_a[g * W : (g + 1) * W, :] = jnp.where(even, last, first)
        s_b[g * W : (g + 1) * W, :] = jnp.where(even, first, last)


def pack_span(d, planes, block_of, radius_of, given, z_out):
    V, X, W, Z = d.V, d.X, d.W, d.Z
    pair = lanes(d, W) // 2
    for q in range(d.span_groups):
        rows = pl.ds(q * W, W)
        group = jnp.zeros((W, Z), F32) if given is None else given[rows, :]
        for v in range(q * d.per, min(V + 1, (q + 1) * d.per)):
            if v == V and radius_of is None:
                continue
            for x in planes:
                value = block_of(v, x) if v < V else radius_of(2, x)
                spot = X * (v % d.per) + x
                group = jnp.where(pair == spot, pltpu.roll(value, (2 * spot + 1) % Z, 1), group)
        z_out[rows, :] = group


def pack_walls(d, planes, adj, radius_of, w_a, w_b):
    V, X, W, Z, G = d.V, d.X, d.W, d.Z, d.G
    even = parity("wall")
    tail = jnp.zeros((G - V, Z), F32)
    for x in planes:
        first, last = adj[d.rows_at(x, 0), :], adj[d.rows_at(x, W - 1), :]
        w_a[x * G : x * G + V, :] = jnp.where(even, last, first)
        w_b[x * G : x * G + V, :] = jnp.where(even, first, last)
        if radius_of is None or G - V > 1:
            w_a[x * G + V : (x + 1) * G, :] = tail
            w_b[x * G + V : (x + 1) * G, :] = tail
        if radius_of is not None:
            radius = radius_of(1, x)
            first, last = radius[:1], radius[W - 1 :]
            w_a[x * G + V : x * G + V + 1, :] = jnp.where(even, last, first)
            w_b[x * G + V : x * G + V + 1, :] = jnp.where(even, first, last)
    if X - 1 in planes:
        w_a[X * G :, :] = jnp.zeros((8, Z), F32)
        w_b[X * G :, :] = jnp.zeros((8, Z), F32)


def parity(axis):
    return lax.rem(lax.axis_index(axis), 2) == 0


def pack_kernel(d, *refs):
    count = (len(refs) - 6) // 2
    held, kept = refs[:count], refs[count : 2 * count]
    s_a, s_b, w_a, w_b, z_out, sems = refs[2 * count :]
    adj, vel, snd = kept[:3]
    copies = [pltpu.make_async_copy(held[k], kept[k], sems.at[k]) for k in range(count)]
    for copy in copies:
        copy.start()
    for copy in copies:
        copy.wait()
    block_of = lambda v, x: adj[d.block(v, x), :]
    radius_of = functools.partial(radius_at, d, vel, snd)
    pack_stream(d, block_of, radius_of, s_a, s_b)
    pack_span(d, range(d.X), block_of, radius_of, None, z_out)
    pack_walls(d, range(d.X), adj, radius_of, w_a, w_b)


def make_matrices(d, couple, precond, mk, mw, pk, wide, wide_wall):
    V, W, B, n, K, S = d.V, d.W, d.B, d.n, d.wall_k, d.stack
    gap = jnp.zeros((V, S - V), F32)
    blocks = [couple[k // 2, :, k % 2, :] for k in range(6)] + [precond[...].T]
    blocks = [piece for m in blocks for piece in ((m, gap) if S > V else (m,))]
    blocks = jnp.concatenate(blocks, axis=1)
    high = blocks.astype(BF16).astype(F32)
    gap = jnp.zeros((S - V, 7 * S), F32)
    pieces = (high, gap, blocks - high, gap) if S > V else (high, blocks - high)
    blocks = jnp.concatenate(pieces, axis=0).astype(BF16)
    dims = (((0,), (0,)), ((), ()))

    def spread(some, width, keep):
        row = lax.broadcasted_iota(jnp.int32, (2 * S, 3 * width), 0)
        col = lax.broadcasted_iota(jnp.int32, (2 * S, 3 * width), 1)
        part = keep(lax.rem(col, width), jnp.where(row < S, row, row - S))
        part = part & ((row < S) == (col < 2 * width))
        return lax.dot_general(some, part.astype(BF16), dims, preferred_element_type=F32)

    wide[...] = spread(blocks, B, lambda col, v: col // W == v)
    sides = []
    for side in range(2):
        some = blocks[:, (2 + side) * S : (3 + side) * S]
        sides.append(spread(some, 2 * K, lambda col, v: col - side * K == v))
    wide_wall[...] = jnp.concatenate(sides, axis=0)
    row = lax.broadcasted_iota(jnp.int32, (W, 3 * B), 0)
    col = lax.rem(lax.broadcasted_iota(jnp.int32, (W, 3 * B), 1), W)
    same, lower, upper = [(col - row == k).astype(F32) for k in (0, -1, 1)]

    def rows(k):
        mask = {2: lower, 3: upper}.get(k, same)
        return [wide[pl.ds(k * S + v, 1), :] * mask for v in range(V)]

    for k in range(0, 6, 2):
        both = jnp.concatenate(rows(k) + rows(k + 1), axis=0)
        mk[k * n : (k + 2) * n, :] = both.astype(BF16)
    pk[...] = jnp.concatenate(rows(6), axis=0).astype(BF16)
    row = lax.broadcasted_iota(jnp.int32, (W, 6 * K), 0)
    first, last = (row == 0).astype(F32), (row == W - 1).astype(F32)
    pieces = [
        wide_wall[pl.ds(v, 1), :] * first + wide_wall[pl.ds(S + v, 1), :] * last for v in range(V)
    ]
    mw[...] = jnp.concatenate(pieces, axis=0).astype(BF16)


def make_wall(d, codes, mask, table, gain, wall_out):
    X, Z, V, S = d.X, d.Z, d.V, d.stack
    place = lax.axis_index("stream")
    lane0 = pl.multiple_of(lax.axis_index("span") * Z, Z)
    kinds = table.shape[0]

    def window(ref):
        value = ref[:X, pl.ds(lane0, Z)]
        for s in range(1, lax.axis_size("stream")):
            value = jnp.where(place == s, ref[s * X : (s + 1) * X, pl.ds(lane0, Z)], value)
        return value

    code, spall = window(codes), window(mask).astype(F32)
    column = lambda values: jnp.broadcast_to(values.T, (V, Z))
    columns = [column(table[k : k + 1, :]) for k in range(kinds)]
    gains = column(gain[...])
    for x in range(X):
        here = jnp.broadcast_to(code[x : x + 1], (V, Z))
        coef = columns[kinds - 1]
        for k in range(kinds - 1):
            coef = jnp.where(here == k, columns[k], coef)
        wall_out[x * S : x * S + V, :] = coef + gains * spall[x : x + 1]


def sweep_local(d, adj, src, vel, snd, mk, wall_coef, rates_of, out, rs_out):
    X, W, Z, n = d.X, d.W, d.Z, d.n
    lane, row = lanes(d, W), row_ids(d)
    wall_flag = (lax.axis_index("wall") == 0).astype(F32)
    half = [[0.5 * radius_at(d, vel, snd, k, x) for x in range(X)] for k in range(3)]
    sums = {}

    def begin(x):
        total = 1.0
        for neighbour in (x - 1, x + 1):
            total = total + half[0][x]
            if 0 <= neighbour < X:
                total = total + half[0][neighbour]
        rates = []
        for edge, turn in ((0, 1), (W - 1, W - 1)):
            near = jnp.where(row == edge, 0.0, pltpu.roll(half[1][x], turn, 0))
            rates.append(half[1][x] + near)
            total = total + rates[-1]
        for edge, turn in ((0, 1), (Z - 1, Z - 1)):
            near = jnp.where(lane == edge, 0.0, pltpu.roll(half[2][x], turn, 1))
            total = total + half[2][x] + near
            rates.append(jnp.where(lane == edge, 0.0, half[2][x] + near))
        if rates_of is None:
            rs_out[d.block(0, x), :] = total
        else:
            total = rates_of[d.block(0, x), :]
        sums[x] = d.plane3(src, x) - d.each(total) * d.plane(adj, x)
        return rates

    def subtract(x, rate, value):
        sums[x] = sums[x] - d.each(rate) * value

    done = 0
    step = 2
    begun = {}
    for start in range(0, X, step):
        here = list(range(start, min(X, start + step)))
        for x in range(max(0, start - 1), min(X, start + step + 1)):
            if x not in begun:
                begun[x] = begin(x)
        right = split3(jnp.concatenate([padded_plane(d, d.plane(adj, x)) for x in here], axis=1))
        for k in (0, 2, 4):
            both = dot(mk[k * n : (k + 2) * n, :], right)
            for side in range(2):
                for offset, x in enumerate(here):
                    value = both[side * n : (side + 1) * n, offset * Z : (offset + 1) * Z]
                    if k == 0:
                        to = x + 1 - 2 * side
                        if 0 <= to < X:
                            subtract(to, half[0][x] + half[0][to], value)
                    elif k == 2:
                        subtract(x, begun[x][side], value)
                    else:
                        turn = (1, Z - 1)[side]
                        subtract(x, begun[x][2 + side], pltpu.roll(value, turn, 1))
        while done < X and (done < here[-1] or here[-1] == X - 1):
            d.store_plane(out, done, sums.pop(done))
            done += 1
    for x in range(X):
        spot = d.rows_at(x, 0)
        factor = wall_flag * (2.0 * half[1][x][:1])
        coef = wall_coef[x * d.stack : x * d.stack + d.V, :]
        out[spot, :] = out[spot, :] - factor * coef * adj[spot, :]


def early():
    return 2 * lax.axis_index("stream") < lax.axis_size("stream")


def early_kernel(d, couple, precond, codes, mask, table, gain, *refs):
    mk, mw, pk, wall_coef = refs[5:9]
    wide, wide_wall = refs[-2:]

    @pl.when(early())
    def _():
        make_matrices(d, couple, precond, mk, mw, pk, wide, wide_wall)
        make_wall(d, codes, mask, table, gain, wall_coef)


def first_local_kernel(
    d, adj, src, vel, snd, couple, precond, codes, mask, table, gain, _mk, _mw, _pk, _wall_coef,
    out, rs, mk, mw, pk, wall_coef, wide, wide_wall,
):
    @pl.when(jnp.logical_not(early()))
    def _():
        make_matrices(d, couple, precond, mk, mw, pk, wide, wide_wall)
        make_wall(d, codes, mask, table, gain, wall_coef)

    sweep_local(d, adj, src, vel, snd, mk, wall_coef, None, out, rs)


def later_local_kernel(d, adj, src, vel, snd, rs, mk, wall_coef, out):
    sweep_local(d, adj, src, vel, snd, mk, wall_coef, rs, out, None)


def neighbours(axis):
    index = lax.axis_index(axis)
    return (index > 0).astype(F32), (index < lax.axis_size(axis) - 1).astype(F32)


def wall_terms(d, w0, w1, mw):
    X, W, Z, G = d.X, d.W, d.Z, d.G
    even = parity("wall")
    has_low, has_high = neighbours("wall")
    row = row_ids(d)

    def received(start, count):
        a, b = w0[pl.ds(start, count), :], w1[pl.ds(start, count), :]
        return jnp.where(even, b, a) * has_low, jnp.where(even, a, b) * has_high

    products = {}
    for start in range(0, X, 2):
        here = list(range(start, min(X, start + 2)))
        right = [jnp.concatenate(received(x * G, d.wall_k), axis=0) for x in here]
        value = dot(mw[...], split3(jnp.concatenate(right, axis=1)))
        for k, x in enumerate(here):
            products[x] = value[:, k * Z : (k + 1) * Z]

    def radius(x):
        first, last = received(x * G + d.V, 1)
        return jnp.where(row == 0, first, jnp.where(row == W - 1, last, 0.0))

    return products.get, radius


def span_terms(d, zl, zr, mk):
    V, X, W, Z, n = d.V, d.X, d.W, d.Z, d.n
    even = lax.rem(lanes(d, W), 2) == 0
    pieces = []
    for v in range(V + 1):
        q = pl.ds((v // d.per) * W, W)
        value = jnp.where(even, zl[q, :], zr[q, :])
        turn = (Z - 2 * X * (v % d.per)) % Z
        pieces.append(pltpu.roll(value, turn, 1) if turn else value)
    radius = jnp.where(even, pieces[V], pltpu.roll(pieces[V], Z - 2, 1))
    pieces += [jnp.zeros((W, Z), F32)] * (d.G - V - 1)
    both = dot(mk[4 * n :], split3(jnp.concatenate(pieces, axis=0)))
    even = lax.rem(lanes(d, n), 2) == 0
    span = jnp.where(even, both[:n], pltpu.roll(both[n:], Z - 2, 1))
    at = lambda value, x: pltpu.roll(value, (Z - 2 * x) % Z, 1) if x else value
    return lambda x: at(span, x), lambda x: at(radius, x)


def update_planes(d, planes, residual_of, adj, rs_of, pk, put):
    Z = d.Z

    def finish(here, residuals, update):
        for k, x in enumerate(here):
            inverse = 1.0 / rs_of(x)
            new = d.plane(adj, x) + update[:, k * Z : (k + 1) * Z] * d.each(inverse)
            put(x, new, residuals[k])

    waiting = None
    for start in range(0, len(planes), 2):
        here = planes[start : start + 2]
        residuals = [residual_of(x) for x in here]
        right = jnp.concatenate([padded_plane(d, r) for r in residuals], axis=1)
        update = dot(pk[...], split3(right))
        if waiting:
            finish(*waiting)
        waiting = here, residuals, update
    if waiting:
        finish(*waiting)


def first_inner_kernel(
    d, partial, adj, rs, vel, snd, w0, w1, zl, zr, mk, mw, pk,
    new_adj, rs_full, rates, edge, w_a, w_b, z_out,
):
    V, X, W, Z, n = d.V, d.X, d.W, d.Z, d.n
    span, span_radius = span_terms(d, zl, zr, mk)
    wall, wall_radius = wall_terms(d, w0, w1, mw)
    lane, row = lanes(d, W), row_ids(d)
    edge_lane = (lane == 0) | (lane == Z - 1)
    edge_row = (row == 0) | (row == W - 1)
    totals = {}

    def residual_of(x):
        from_wall = 0.5 * wall_radius(x)
        from_span = jnp.where(edge_lane, 0.5 * span_radius(x), 0.0)
        rate_wall = jnp.where(edge_row, 0.5 * radius_at(d, vel, snd, 1, x) + from_wall, 0.0)
        rate_span = jnp.where(edge_lane, 0.5 * radius_at(d, vel, snd, 2, x) + from_span, 0.0)
        correction = from_wall + from_span
        totals[x] = rs[d.block(0, x), :] + correction
        rates[d.block(0, x), :] = rate_wall
        rates[d.block(1, x), :] = rate_span
        rs_full[d.block(0, x), :] = totals[x]
        result = d.plane(partial, x) - d.each(correction) * d.plane(adj, x)
        return result - d.each(rate_wall) * wall(x) - d.each(rate_span) * span(x)

    for k, x in enumerate(d.edges):
        edge[k * n : (k + 1) * n, :] = residual_of(x)
    put = lambda x, new, _: d.store_plane(new_adj, x, new)
    update_planes(d, list(d.inner), residual_of, adj, totals.get, pk, put)
    pack_walls(d, d.inner, new_adj, None, w_a, w_b)
    pack_span(d, d.inner, lambda v, x: new_adj[d.block(v, x), :], None, None, z_out)


def later_inner_kernel(
    d, partial, adj, rs_full, rates, w0, w1, zl, zr, mk, mw, pk, new_adj, residual, edge
):
    W, n = d.W, d.n
    span, _ = span_terms(d, zl, zr, mk)
    wall, _ = wall_terms(d, w0, w1, mw)

    def residual_of(x):
        result = d.plane(partial, x) - d.each(rates[d.block(0, x), :]) * wall(x)
        return result - d.each(rates[d.block(1, x), :]) * span(x)

    def put(x, new, res):
        new_adj[d.planes_at(x, 1)] = new.reshape(d.V, W, d.Z)
        residual[d.planes_at(x, 1)] = res.reshape(d.V, W, d.Z)

    for k, x in enumerate(d.edges):
        edge[k * n : (k + 1) * n, :] = residual_of(x)
    rs_of = lambda x: rs_full[d.block(0, x), :]
    update_planes(d, list(d.inner), residual_of, adj, rs_of, pk, put)


def stream_terms(d, s0, s1, mk):
    n, Z = d.n, d.Z
    even = parity("stream")
    has_low, has_high = neighbours("stream")
    low = jnp.where(even, s1[...], s0[...]) * has_low
    high = jnp.where(even, s0[...], s1[...]) * has_high
    both = dot(mk[: 2 * n], split3(jnp.concatenate([low, high], axis=1)))
    return (both[:n, :Z], both[n:, Z:]), (low[n : n + d.W], high[n : n + d.W])


def first_stream_kernel(
    d, edge, adj, rs, vel, snd, s0, s1, mk, pk, inner, w_in0, w_in1, z_in,
    new_adj, rs_full, w_a, w_b, z_out, rates, s_a, s_b,
):
    X, W, n = d.X, d.W, d.n
    products, received = stream_terms(d, s0, s1, mk)
    totals = {}

    def residual_of(x):
        k = d.edges.index(x)
        result = edge[k * n : (k + 1) * n, :]
        totals[x] = rs[d.block(0, x), :]
        for side, at in enumerate((0, X - 1)):
            if x == at:
                rate = 0.5 * (radius_at(d, vel, snd, 0, x) + received[side])
                rates[side * W : (side + 1) * W, :] = rate
                totals[x] = totals[x] + 0.5 * received[side]
                result = result - d.each(0.5 * received[side]) * d.plane(adj, x)
                result = result - d.each(rate) * products[side]
        rs_full[d.block(0, x), :] = totals[x]
        return result

    planes = {}

    def put(x, new, _):
        d.store_plane(new_adj, x, new)
        planes[x] = new

    update_planes(d, d.edges, residual_of, adj, totals.get, pk, put)
    block_of = lambda v, x: planes[x][v * W : (v + 1) * W]
    pack_stream(d, block_of, None, s_a, s_b)
    pack_span(d, d.edges, block_of, None, z_in, z_out)
    pack_walls(d, d.edges, new_adj, None, w_a, w_b)


def later_stream_kernel(
    d, edge, adj, rs_full, rates, s0, s1, mk, pk, inner_adj, inner_residual,
    new_adj, residual, edge_adj, edge_residual, sems,
):
    X, W, Z, n = d.X, d.W, d.Z, d.n
    copies = []

    def store(source, target, part, here):
        copy = pltpu.make_async_copy(source.at[here], target.at[part], sems.at[len(copies)])
        copy.start()
        copies.append(copy)

    if len(d.inner):
        part = d.planes_at(1, len(d.inner))
        store(inner_residual, residual, part, part)
        store(inner_adj, new_adj, part, part)
    products, _ = stream_terms(d, s0, s1, mk)

    def residual_of(x):
        k = d.edges.index(x)
        result = edge[k * n : (k + 1) * n, :]
        for side, at in enumerate((0, X - 1)):
            if x == at:
                result = result - d.each(rates[side * W : (side + 1) * W, :]) * products[side]
        return result

    def put(x, new, res):
        here = d.planes_at(d.edges.index(x), 1)
        for value, held, target in (
            (res, edge_residual, residual),
            (new, edge_adj, new_adj),
        ):
            held[here] = value.reshape(d.V, W, Z)
            store(held, target, d.planes_at(x, 1), here)

    rs_of = lambda x: rs_full[d.block(0, x), :]
    update_planes(d, d.edges, residual_of, adj, rs_of, pk, put)
    for copy in copies:
        copy.wait()


def exchange_pairs(sizes, axis, odd, spare):
    ids = np.arange(int(np.prod(sizes))).reshape(sizes)
    pairs = []
    for at in np.ndindex(*sizes):
        to = list(at)
        step = 1 if (at[axis] - odd) % 2 == 0 else -1
        if at[axis] >= odd and 0 <= at[axis] + step < sizes[axis]:
            to[axis] += step
        elif (at[spare] ^ 1) < sizes[spare]:
            to[spare] ^= 1
        else:
            continue
        pairs.append((int(ids[at]), int(ids[tuple(to)])))
    return pairs


def swap_lines(sizes, s_a, s_b, w_a, w_b, z):
    move = lambda value, pairs: lax.ppermute(value, AXES, pairs)
    s0 = move(s_a, exchange_pairs(sizes, 0, 0, 2))
    s1 = move(s_b, exchange_pairs(sizes, 0, 1, 2))
    w1 = move(w_b, exchange_pairs(sizes, 2, 1, 1))
    w0 = move(w_a, exchange_pairs(sizes, 2, 0, 1))
    peers = sizes[1]
    if peers == 1:
        zl = zr = z
    elif peers == 2:
        zl = zr = lax.ppermute(z, "span", [(0, 1), (1, 0)])
    else:
        up = [(i, (i + 1) % peers) for i in range(peers)]
        zl = lax.ppermute(z, "span", up)
        zr = lax.ppermute(z, "span", [(j, i) for i, j in up])
    return s0, s1, w0, w1, zl, zr


def call(kernel, d, outs, flops, args, held=(), scratch=(), out_held=False, aliases=None):
    space = lambda k: pltpu.HBM if k in held else pltpu.VMEM
    out_space = pltpu.HBM if out_held else pltpu.VMEM
    args = [pltpu.with_memory_space_constraint(a, space(k)) for k, a in enumerate(args)]
    moved = sum(int(np.prod(a.shape)) * a.dtype.itemsize for a in args)
    return pl.pallas_call(
        functools.partial(kernel, d),
        out_shape=tuple(out_space(s, t) for s, t in outs),
        in_specs=[pl.BlockSpec(memory_space=space(k)) for k in range(len(args))],
        out_specs=tuple(pl.BlockSpec(memory_space=out_space) for _ in outs),
        scratch_shapes=scratch,
        input_output_aliases=aliases or {},
        compiler_params=pltpu.CompilerParams(vmem_limit_bytes=24 * 2**20),
        cost_estimate=pl.CostEstimate(flops=flops, bytes_accessed=moved, transcendentals=0),
        name=kernel.__name__,
    )(*args)


def on_device(sizes, adj, source, velocity, sound, couple, precond, codes, mask, table, gain):
    shape = adj.shape
    d = Dims(shape)
    V, X, W, Z, B, n = d.V, d.X, d.W, d.Z, d.B, d.n
    inputs = [
        adj.reshape(d.rows, Z),
        velocity.reshape(3 * X * W, Z),
        sound.reshape(X * W, Z),
        couple.transpose(0, 2, 1, 3),
        precond,
        codes,
        mask,
        table,
        gain.reshape(1, -1),
    ]
    source = source.reshape(V, X * W, Z)
    faces = [((B, Z), F32)] * 2 + [((d.wall_rows, Z), F32)] * 2 + [((d.span_groups * W, Z), F32)]
    field, scalar = ((d.rows, Z), F32), ((X * W, Z), F32)
    planes = ((V, X * W, Z), F32)
    sems = lambda *counts: pltpu.SemaphoreType.DMA(counts)
    *kept, s_a, s_b, w_a, w_b, z = call(
        pack_kernel,
        d,
        [(a.shape, a.dtype) for a in inputs] + faces,
        0,
        inputs,
        held=range(len(inputs)),
        scratch=[sems(len(inputs))],
    )
    adj, velocity, sound = kept[:3]
    made = [
        ((6 * n, 3 * B), BF16),
        ((n, 6 * d.wall_k), BF16),
        ((n, 3 * B), BF16),
        ((X * d.stack, Z), F32),
    ]
    room = [pltpu.VMEM((7 * d.stack, 3 * B), F32), pltpu.VMEM((2 * d.stack, 6 * d.wall_k), F32)]
    params = kept[3:]
    *matrices, s_a, s_b, w_a, w_b, z = call(
        early_kernel,
        d,
        made + faces,
        0,
        params + [s_a, s_b, w_a, w_b, z],
        scratch=room,
        aliases={len(params) + k: len(made) + k for k in range(5)},
    )
    got = swap_lines(sizes, s_a, s_b, w_a, w_b, z)
    partial, rs, mk, mw, pk, wall_coef = call(
        first_local_kernel,
        d,
        [field, scalar] + made,
        10**9,
        [adj, source, velocity, sound] + params + matrices,
        scratch=room,
        aliases={4 + len(params) + k: 2 + k for k in range(len(made))},
    )
    s0, s1, w0, w1, zl, zr = got
    edge = ((len(d.edges) * n, Z), F32)
    inner, rs, rates, held, w_a, w_b, z = call(
        first_inner_kernel,
        d,
        [field, scalar, ((2 * X * W, Z), F32), edge] + faces[2:],
        10**8,
        [partial, adj, rs, velocity, sound, w0, w1, zl, zr, mk, mw, pk],
    )
    adj1, rs, w_a, w_b, z, stream_rates, s_a, s_b = call(
        first_stream_kernel,
        d,
        [field, scalar] + faces[2:] + [((2 * W, Z), F32)] + faces[:2],
        10**7,
        [held, adj, rs, velocity, sound, s0, s1, mk, pk, inner, w_a, w_b, z],
        aliases={9: 0, 2: 1, 10: 2, 11: 3, 12: 4},
    )
    s0, s1, w0, w1, zl, zr = swap_lines(sizes, s_a, s_b, w_a, w_b, z)
    (partial,) = call(
        later_local_kernel,
        d,
        [field],
        10**9,
        [adj1, source, velocity, sound, rs, mk, wall_coef],
    )
    inner, inner_residual, held = call(
        later_inner_kernel,
        d,
        [planes, planes, edge],
        10**8,
        [partial, adj1, rs, rates, w0, w1, zl, zr, mk, mw, pk],
    )
    edge = ((V, len(d.edges) * W, Z), F32)
    adj2, residual = call(
        later_stream_kernel,
        d,
        [planes, planes],
        10**7,
        [held, adj1, rs, stream_rates, s0, s1, mk, pk, inner, inner_residual],
        scratch=[pltpu.VMEM(*edge), pltpu.VMEM(*edge), sems(2 + 2 * len(d.edges))],
        out_held=True,
    )
    return adj2.reshape(shape), residual.reshape(shape)


def solution(mesh):
    sizes = tuple(mesh.shape[a] for a in AXES)
    field = P(None, "stream", "wall", "span")
    return jax.shard_map(
        functools.partial(on_device, sizes),
        mesh=mesh,
        in_specs=(field, field, field, P("stream", "wall", "span")) + (P(),) * 6,
        out_specs=(field, field),
        check_vma=False,
    )
```

```python
import functools

import jax
import jax.numpy as jnp
import numpy as np
from jax import lax
from jax.experimental import pallas as pl
from jax.experimental.pallas import tpu as pltpu
from jax.sharding import PartitionSpec as P

AXES = ("stream", "span", "wall")
F32 = jnp.float32
BF16 = jnp.bfloat16


class Dims:
    def __init__(self, shape):
        self.V, self.X, self.W, self.Z = shape
        self.G = self.V + 1
        while self.G * self.W % 16:
            self.G += 1
        self.B = self.G * self.W
        self.n = self.V * self.W
        self.rows = self.n * self.X
        self.edges = sorted({0, self.X - 1})
        self.inner = range(1, self.X - 1)
        self.wall_rows = self.X * self.G + 8
        self.wall_k = -(-self.G // 8) * 8
        self.stack = -(-self.V // 8) * 8
        self.per = self.Z // (2 * self.X)
        self.span_groups = -(-(self.V + 1) // self.per)

    def block(self, group, x):
        return pl.ds((group * self.X + x) * self.W, self.W)

    def rows_at(self, x, w):
        return pl.ds(x * self.W + w, self.V, stride=self.X * self.W)

    def plane(self, ref, x):
        return jnp.concatenate([ref[self.block(v, x), :] for v in range(self.V)], axis=0)

    def store_plane(self, ref, x, value):
        for v in range(self.V):
            ref[self.block(v, x), :] = value[v * self.W : (v + 1) * self.W]

    def plane3(self, ref, x):
        return ref[:, x * self.W : (x + 1) * self.W, :].reshape(self.n, self.Z)

    def planes_at(self, start, count):
        return (slice(None), pl.ds(start * self.W, count * self.W), slice(None))

    def each(self, factor):
        return jnp.concatenate([factor] * self.V, axis=0)


def lanes(d, rows):
    return lax.broadcasted_iota(jnp.int32, (rows, d.Z), 1)


def row_ids(d):
    return lax.broadcasted_iota(jnp.int32, (d.W, d.Z), 0)


def radius_at(d, vel, snd, direction, x):
    return jnp.abs(vel[d.block(direction, x), :]) + snd[d.block(0, x), :]


def split3(value):
    high = value.astype(BF16)
    low = (value - high.astype(F32)).astype(BF16)
    return jnp.concatenate([high, low, high], axis=0)


def padded_plane(d, value):
    extra = d.B - value.shape[0]
    if not extra:
        return value
    return jnp.concatenate([value, jnp.zeros((extra, value.shape[1]), F32)], axis=0)


def dot(a, b):
    return jnp.dot(a, b, preferred_element_type=F32)


def pack_stream(d, block_of, radius_of, s_a, s_b):
    W, even = d.W, parity("stream")
    for g in range(d.G):
        if g < d.V:
            first, last = block_of(g, 0), block_of(g, d.X - 1)
        elif g == d.V and radius_of is not None:
            first, last = radius_of(0, 0), radius_of(0, d.X - 1)
        else:
            first = last = jnp.zeros((W, d.Z), F32)
        s_a[g * W : (g + 1) * W, :] = jnp.where(even, last, first)
        s_b[g * W : (g + 1) * W, :] = jnp.where(even, first, last)


def pack_span(d, planes, block_of, radius_of, given, z_out, groups=None):
    V, X, W, Z = d.V, d.X, d.W, d.Z
    pair = lanes(d, W) // 2
    for q in range(d.span_groups) if groups is None else groups:
        rows = pl.ds(q * W, W)
        group = jnp.zeros((W, Z), F32) if given is None else given[rows, :]
        for v in range(q * d.per, min(V + 1, (q + 1) * d.per)):
            if v == V and radius_of is None:
                continue
            for x in planes:
                value = block_of(v, x) if v < V else radius_of(2, x)
                spot = X * (v % d.per) + x
                group = jnp.where(pair == spot, pltpu.roll(value, (2 * spot + 1) % Z, 1), group)
        z_out[rows, :] = group


def pack_walls(d, planes, adj, radius_of, w_a, w_b):
    V, X, W, Z, G = d.V, d.X, d.W, d.Z, d.G
    even = parity("wall")
    tail = jnp.zeros((G - V, Z), F32)
    for x in planes:
        first, last = adj[d.rows_at(x, 0), :], adj[d.rows_at(x, W - 1), :]
        w_a[x * G : x * G + V, :] = jnp.where(even, last, first)
        w_b[x * G : x * G + V, :] = jnp.where(even, first, last)
        if radius_of is None or G - V > 1:
            w_a[x * G + V : (x + 1) * G, :] = tail
            w_b[x * G + V : (x + 1) * G, :] = tail
        if radius_of is not None:
            radius = radius_of(1, x)
            first, last = radius[:1], radius[W - 1 :]
            w_a[x * G + V : x * G + V + 1, :] = jnp.where(even, last, first)
            w_b[x * G + V : x * G + V + 1, :] = jnp.where(even, first, last)
    if X - 1 in planes:
        w_a[X * G :, :] = jnp.zeros((8, Z), F32)
        w_b[X * G :, :] = jnp.zeros((8, Z), F32)


def parity(axis):
    return lax.rem(lax.axis_index(axis), 2) == 0


def pack_kernel(d, *refs):
    count = (len(refs) - 6) // 2
    held, kept = refs[:count], refs[count : 2 * count]
    s_a, s_b, w_a, w_b, z_out, sems = refs[2 * count :]
    adj, vel, snd = kept[:3]
    groups = -(-d.span_groups // 2)
    size = d.X * d.W
    front = min(d.V, groups * d.per) * size
    parts = [pl.ds(0, front), pl.ds(front, d.rows - front)] if front < d.rows else [pl.ds(0, front)]
    copies = [
        pltpu.make_async_copy(held[0].at[part], adj.at[part], sems.at[count + k])
        for k, part in enumerate(parts)
    ]
    copies += [pltpu.make_async_copy(held[k], kept[k], sems.at[k]) for k in range(1, count)]
    for copy in copies:
        copy.start()
    copies[0].wait()
    block_of = lambda v, x: adj[d.block(v, x), :]
    radius_of = functools.partial(radius_at, d, vel, snd)
    pack_span(d, range(d.X), block_of, radius_of, None, z_out, range(groups))
    for copy in copies[1:]:
        copy.wait()
    pack_span(d, range(d.X), block_of, radius_of, None, z_out, range(groups, d.span_groups))
    pack_stream(d, block_of, radius_of, s_a, s_b)
    pack_walls(d, range(d.X), adj, radius_of, w_a, w_b)


def make_matrices(d, couple, precond, mk, mw, pk, wide, wide_wall):
    V, W, B, n, K, S = d.V, d.W, d.B, d.n, d.wall_k, d.stack
    gap = jnp.zeros((V, S - V), F32)
    blocks = [couple[k // 2, :, k % 2, :] for k in range(6)] + [precond[...].T]
    blocks = [piece for m in blocks for piece in ((m, gap) if S > V else (m,))]
    blocks = jnp.concatenate(blocks, axis=1)
    high = blocks.astype(BF16).astype(F32)
    gap = jnp.zeros((S - V, 7 * S), F32)
    pieces = (high, gap, blocks - high, gap) if S > V else (high, blocks - high)
    blocks = jnp.concatenate(pieces, axis=0).astype(BF16)
    dims = (((0,), (0,)), ((), ()))

    def spread(some, width, keep):
        row = lax.broadcasted_iota(jnp.int32, (2 * S, 3 * width), 0)
        col = lax.broadcasted_iota(jnp.int32, (2 * S, 3 * width), 1)
        part = keep(lax.rem(col, width), jnp.where(row < S, row, row - S))
        part = part & ((row < S) == (col < 2 * width))
        return lax.dot_general(some, part.astype(BF16), dims, preferred_element_type=F32)

    wide[...] = spread(blocks, B, lambda col, v: col // W == v)
    sides = []
    for side in range(2):
        some = blocks[:, (2 + side) * S : (3 + side) * S]
        sides.append(spread(some, 2 * K, lambda col, v: col - side * K == v))
    wide_wall[...] = jnp.concatenate(sides, axis=0)
    row = lax.broadcasted_iota(jnp.int32, (W, 3 * B), 0)
    col = lax.rem(lax.broadcasted_iota(jnp.int32, (W, 3 * B), 1), W)
    same, lower, upper = [(col - row == k).astype(F32) for k in (0, -1, 1)]

    def rows(k):
        mask = {2: lower, 3: upper}.get(k, same)
        return [wide[pl.ds(k * S + v, 1), :] * mask for v in range(V)]

    for k in range(0, 6, 2):
        both = jnp.concatenate(rows(k) + rows(k + 1), axis=0)
        mk[k * n : (k + 2) * n, :] = both.astype(BF16)
    pk[...] = jnp.concatenate(rows(6), axis=0).astype(BF16)
    row = lax.broadcasted_iota(jnp.int32, (W, 6 * K), 0)
    first, last = (row == 0).astype(F32), (row == W - 1).astype(F32)
    pieces = [
        wide_wall[pl.ds(v, 1), :] * first + wide_wall[pl.ds(S + v, 1), :] * last for v in range(V)
    ]
    mw[...] = jnp.concatenate(pieces, axis=0).astype(BF16)


def make_wall(d, codes, mask, table, gain, wall_out):
    X, Z, V, S = d.X, d.Z, d.V, d.stack
    place = lax.axis_index("stream")
    lane0 = pl.multiple_of(lax.axis_index("span") * Z, Z)
    kinds = table.shape[0]

    def window(ref):
        value = ref[:X, pl.ds(lane0, Z)]
        for s in range(1, lax.axis_size("stream")):
            value = jnp.where(place == s, ref[s * X : (s + 1) * X, pl.ds(lane0, Z)], value)
        return value

    code, spall = window(codes), window(mask).astype(F32)
    column = lambda values: jnp.broadcast_to(values.T, (V, Z))
    columns = [column(table[k : k + 1, :]) for k in range(kinds)]
    gains = column(gain[...])
    for x in range(X):
        here = jnp.broadcast_to(code[x : x + 1], (V, Z))
        coef = columns[kinds - 1]
        for k in range(kinds - 1):
            coef = jnp.where(here == k, columns[k], coef)
        wall_out[x * S : x * S + V, :] = coef + gains * spall[x : x + 1]


def sweep_local(d, adj, src, vel, snd, mk, wall_coef, rates_of, out, rs_out):
    X, W, Z, n = d.X, d.W, d.Z, d.n
    lane, row = lanes(d, W), row_ids(d)
    wall_flag = (lax.axis_index("wall") == 0).astype(F32)
    half = [[0.5 * radius_at(d, vel, snd, k, x) for x in range(X)] for k in range(3)]
    sums = {}

    def begin(x):
        total = 1.0
        for neighbour in (x - 1, x + 1):
            total = total + half[0][x]
            if 0 <= neighbour < X:
                total = total + half[0][neighbour]
        rates = []
        for edge, turn in ((0, 1), (W - 1, W - 1)):
            near = jnp.where(row == edge, 0.0, pltpu.roll(half[1][x], turn, 0))
            rates.append(half[1][x] + near)
            total = total + rates[-1]
        for edge, turn in ((0, 1), (Z - 1, Z - 1)):
            near = jnp.where(lane == edge, 0.0, pltpu.roll(half[2][x], turn, 1))
            total = total + half[2][x] + near
            rates.append(jnp.where(lane == edge, 0.0, half[2][x] + near))
        if rates_of is None:
            rs_out[d.block(0, x), :] = total
        else:
            total = rates_of[d.block(0, x), :]
        sums[x] = d.plane3(src, x) - d.each(total) * d.plane(adj, x)
        return rates

    def subtract(x, rate, value):
        sums[x] = sums[x] - d.each(rate) * value

    done = 0
    step = 2
    begun = {}
    for start in range(0, X, step):
        here = list(range(start, min(X, start + step)))
        for x in range(max(0, start - 1), min(X, start + step + 1)):
            if x not in begun:
                begun[x] = begin(x)
        right = split3(jnp.concatenate([padded_plane(d, d.plane(adj, x)) for x in here], axis=1))
        for k in (0, 2, 4):
            both = dot(mk[k * n : (k + 2) * n, :], right)
            for side in range(2):
                for offset, x in enumerate(here):
                    value = both[side * n : (side + 1) * n, offset * Z : (offset + 1) * Z]
                    if k == 0:
                        to = x + 1 - 2 * side
                        if 0 <= to < X:
                            subtract(to, half[0][x] + half[0][to], value)
                    elif k == 2:
                        subtract(x, begun[x][side], value)
                    else:
                        turn = (1, Z - 1)[side]
                        subtract(x, begun[x][2 + side], pltpu.roll(value, turn, 1))
        while done < X and (done < here[-1] or here[-1] == X - 1):
            d.store_plane(out, done, sums.pop(done))
            done += 1
    for x in range(X):
        spot = d.rows_at(x, 0)
        factor = wall_flag * (2.0 * half[1][x][:1])
        coef = wall_coef[x * d.stack : x * d.stack + d.V, :]
        out[spot, :] = out[spot, :] - factor * coef * adj[spot, :]


def early():
    return 2 * lax.axis_index("stream") < lax.axis_size("stream")


def early_kernel(d, couple, precond, codes, mask, table, gain, *refs):
    mk, mw, pk, wall_coef = refs[5:9]
    wide, wide_wall = refs[-2:]

    @pl.when(early())
    def _():
        make_matrices(d, couple, precond, mk, mw, pk, wide, wide_wall)
        make_wall(d, codes, mask, table, gain, wall_coef)


def first_local_kernel(
    d, adj, src, vel, snd, couple, precond, codes, mask, table, gain, _mk, _mw, _pk, _wall_coef,
    out, rs, mk, mw, pk, wall_coef, wide, wide_wall,
):
    @pl.when(jnp.logical_not(early()))
    def _():
        make_matrices(d, couple, precond, mk, mw, pk, wide, wide_wall)
        make_wall(d, codes, mask, table, gain, wall_coef)

    sweep_local(d, adj, src, vel, snd, mk, wall_coef, None, out, rs)


def later_local_kernel(d, adj, src, vel, snd, rs, mk, wall_coef, out):
    sweep_local(d, adj, src, vel, snd, mk, wall_coef, rs, out, None)


def neighbours(axis):
    index = lax.axis_index(axis)
    return (index > 0).astype(F32), (index < lax.axis_size(axis) - 1).astype(F32)


def wall_terms(d, w0, w1, mw):
    X, W, Z, G = d.X, d.W, d.Z, d.G
    even = parity("wall")
    has_low, has_high = neighbours("wall")
    row = row_ids(d)

    def received(start, count):
        a, b = w0[pl.ds(start, count), :], w1[pl.ds(start, count), :]
        return jnp.where(even, b, a) * has_low, jnp.where(even, a, b) * has_high

    products = {}
    for start in range(0, X, 2):
        here = list(range(start, min(X, start + 2)))
        right = [jnp.concatenate(received(x * G, d.wall_k), axis=0) for x in here]
        value = dot(mw[...], split3(jnp.concatenate(right, axis=1)))
        for k, x in enumerate(here):
            products[x] = value[:, k * Z : (k + 1) * Z]

    def radius(x):
        first, last = received(x * G + d.V, 1)
        return jnp.where(row == 0, first, jnp.where(row == W - 1, last, 0.0))

    return products.get, radius


def span_terms(d, zl, zr, mk):
    V, X, W, Z, n = d.V, d.X, d.W, d.Z, d.n
    even = lax.rem(lanes(d, W), 2) == 0
    pieces = []
    for v in range(V + 1):
        q = pl.ds((v // d.per) * W, W)
        value = jnp.where(even, zl[q, :], zr[q, :])
        turn = (Z - 2 * X * (v % d.per)) % Z
        pieces.append(pltpu.roll(value, turn, 1) if turn else value)
    radius = jnp.where(even, pieces[V], pltpu.roll(pieces[V], Z - 2, 1))
    pieces += [jnp.zeros((W, Z), F32)] * (d.G - V - 1)
    both = dot(mk[4 * n :], split3(jnp.concatenate(pieces, axis=0)))
    even = lax.rem(lanes(d, n), 2) == 0
    span = jnp.where(even, both[:n], pltpu.roll(both[n:], Z - 2, 1))
    at = lambda value, x: pltpu.roll(value, (Z - 2 * x) % Z, 1) if x else value
    return lambda x: at(span, x), lambda x: at(radius, x)


def update_planes(d, planes, residual_of, adj, rs_of, pk, put):
    Z = d.Z

    def finish(here, residuals, update):
        for k, x in enumerate(here):
            inverse = 1.0 / rs_of(x)
            new = d.plane(adj, x) + update[:, k * Z : (k + 1) * Z] * d.each(inverse)
            put(x, new, residuals[k])

    waiting = None
    for start in range(0, len(planes), 2):
        here = planes[start : start + 2]
        residuals = [residual_of(x) for x in here]
        right = jnp.concatenate([padded_plane(d, r) for r in residuals], axis=1)
        update = dot(pk[...], split3(right))
        if waiting:
            finish(*waiting)
        waiting = here, residuals, update
    if waiting:
        finish(*waiting)


def first_inner_kernel(
    d, partial, adj, rs, vel, snd, w0, w1, zl, zr, mk, mw, pk,
    new_adj, rs_full, rates, edge, w_a, w_b, z_out,
):
    V, X, W, Z, n = d.V, d.X, d.W, d.Z, d.n
    span, span_radius = span_terms(d, zl, zr, mk)
    wall, wall_radius = wall_terms(d, w0, w1, mw)
    lane, row = lanes(d, W), row_ids(d)
    edge_lane = (lane == 0) | (lane == Z - 1)
    edge_row = (row == 0) | (row == W - 1)
    totals = {}

    def residual_of(x):
        from_wall = 0.5 * wall_radius(x)
        from_span = jnp.where(edge_lane, 0.5 * span_radius(x), 0.0)
        rate_wall = jnp.where(edge_row, 0.5 * radius_at(d, vel, snd, 1, x) + from_wall, 0.0)
        rate_span = jnp.where(edge_lane, 0.5 * radius_at(d, vel, snd, 2, x) + from_span, 0.0)
        correction = from_wall + from_span
        totals[x] = rs[d.block(0, x), :] + correction
        rates[d.block(0, x), :] = rate_wall
        rates[d.block(1, x), :] = rate_span
        rs_full[d.block(0, x), :] = totals[x]
        result = d.plane(partial, x) - d.each(correction) * d.plane(adj, x)
        return result - d.each(rate_wall) * wall(x) - d.each(rate_span) * span(x)

    for k, x in enumerate(d.edges):
        edge[k * n : (k + 1) * n, :] = residual_of(x)
    put = lambda x, new, _: d.store_plane(new_adj, x, new)
    update_planes(d, list(d.inner), residual_of, adj, totals.get, pk, put)
    pack_walls(d, d.inner, new_adj, None, w_a, w_b)
    pack_span(d, d.inner, lambda v, x: new_adj[d.block(v, x), :], None, None, z_out)


def later_inner_kernel(
    d, partial, adj, rs_full, rates, w1, w0, zl, zr, mk, mw, pk, new_adj, residual, edge
):
    W, n = d.W, d.n
    span, _ = span_terms(d, zl, zr, mk)
    wall, _ = wall_terms(d, w0, w1, mw)

    def residual_of(x):
        result = d.plane(partial, x) - d.each(rates[d.block(0, x), :]) * wall(x)
        return result - d.each(rates[d.block(1, x), :]) * span(x)

    def put(x, new, res):
        new_adj[d.planes_at(x, 1)] = new.reshape(d.V, W, d.Z)
        residual[d.planes_at(x, 1)] = res.reshape(d.V, W, d.Z)

    for k, x in enumerate(d.edges):
        edge[k * n : (k + 1) * n, :] = residual_of(x)
    rs_of = lambda x: rs_full[d.block(0, x), :]
    update_planes(d, list(d.inner), residual_of, adj, rs_of, pk, put)


def stream_terms(d, s0, s1, mk):
    n, Z = d.n, d.Z
    even = parity("stream")
    has_low, has_high = neighbours("stream")
    low = jnp.where(even, s1[...], s0[...]) * has_low
    high = jnp.where(even, s0[...], s1[...]) * has_high
    both = dot(mk[: 2 * n], split3(jnp.concatenate([low, high], axis=1)))
    return (both[:n, :Z], both[n:, Z:]), (low[n : n + d.W], high[n : n + d.W])


def first_stream_kernel(
    d, edge, adj, rs, vel, snd, s0, s1, mk, pk, inner, w_in0, w_in1, z_in,
    new_adj, rs_full, w_a, w_b, z_out, rates, s_a, s_b,
):
    X, W, n = d.X, d.W, d.n
    products, received = stream_terms(d, s0, s1, mk)
    totals = {}

    def residual_of(x):
        k = d.edges.index(x)
        result = edge[k * n : (k + 1) * n, :]
        totals[x] = rs[d.block(0, x), :]
        for side, at in enumerate((0, X - 1)):
            if x == at:
                rate = 0.5 * (radius_at(d, vel, snd, 0, x) + received[side])
                rates[side * W : (side + 1) * W, :] = rate
                totals[x] = totals[x] + 0.5 * received[side]
                result = result - d.each(0.5 * received[side]) * d.plane(adj, x)
                result = result - d.each(rate) * products[side]
        rs_full[d.block(0, x), :] = totals[x]
        return result

    planes = {}

    def put(x, new, _):
        d.store_plane(new_adj, x, new)
        planes[x] = new

    update_planes(d, d.edges, residual_of, adj, totals.get, pk, put)
    block_of = lambda v, x: planes[x][v * W : (v + 1) * W]
    pack_stream(d, block_of, None, s_a, s_b)
    pack_span(d, d.edges, block_of, None, z_in, z_out)
    pack_walls(d, d.edges, new_adj, None, w_a, w_b)


def later_stream_kernel(
    d, edge, adj, rs_full, rates, s0, s1, mk, pk, inner_adj, inner_residual,
    new_adj, residual, edge_adj, edge_residual, sems,
):
    X, W, Z, n = d.X, d.W, d.Z, d.n
    copies = []

    def store(source, target, part, here):
        copy = pltpu.make_async_copy(source.at[here], target.at[part], sems.at[len(copies)])
        copy.start()
        copies.append(copy)

    if len(d.inner):
        part = d.planes_at(1, len(d.inner))
        store(inner_residual, residual, part, part)
        store(inner_adj, new_adj, part, part)
    products, _ = stream_terms(d, s0, s1, mk)

    def residual_of(x):
        k = d.edges.index(x)
        result = edge[k * n : (k + 1) * n, :]
        for side, at in enumerate((0, X - 1)):
            if x == at:
                result = result - d.each(rates[side * W : (side + 1) * W, :]) * products[side]
        return result

    def put(x, new, res):
        here = d.planes_at(d.edges.index(x), 1)
        for value, held, target in (
            (res, edge_residual, residual),
            (new, edge_adj, new_adj),
        ):
            held[here] = value.reshape(d.V, W, Z)
            store(held, target, d.planes_at(x, 1), here)

    rs_of = lambda x: rs_full[d.block(0, x), :]
    update_planes(d, d.edges, residual_of, adj, rs_of, pk, put)
    for copy in copies:
        copy.wait()


def exchange_pairs(sizes, axis, odd, spare):
    ids = np.arange(int(np.prod(sizes))).reshape(sizes)
    pairs = []
    for at in np.ndindex(*sizes):
        to = list(at)
        step = 1 if (at[axis] - odd) % 2 == 0 else -1
        if at[axis] >= odd and 0 <= at[axis] + step < sizes[axis]:
            to[axis] += step
        elif spare == axis and sizes[axis] % 2 == 0:
            to[axis] = sizes[axis] - 1 - at[axis]
        elif spare != axis and (at[spare] ^ 1) < sizes[spare]:
            to[spare] ^= 1
        else:
            continue
        pairs.append((int(ids[at]), int(ids[tuple(to)])))
    return pairs


def swap_lines(sizes, s_a, s_b, w_a, w_b, z):
    move = lambda value, pairs: lax.ppermute(value, AXES, pairs)
    s0 = move(s_a, exchange_pairs(sizes, 0, 0, 2))
    s1 = move(s_b, exchange_pairs(sizes, 0, 1, 2))
    w1 = move(w_b, exchange_pairs(sizes, 2, 1, 2))
    w0 = move(w_a, exchange_pairs(sizes, 2, 0, 1))
    peers = sizes[1]
    if peers == 1:
        zl = zr = z
    elif peers == 2:
        zl = zr = lax.ppermute(z, "span", [(0, 1), (1, 0)])
    else:
        up = [(i, (i + 1) % peers) for i in range(peers)]
        zl = lax.ppermute(z, "span", up)
        zr = lax.ppermute(z, "span", [(j, i) for i, j in up])
    return s0, s1, w0, w1, zl, zr


def call(kernel, d, outs, flops, args, held=(), scratch=(), out_held=False, aliases=None):
    space = lambda k: pltpu.HBM if k in held else pltpu.VMEM
    out_space = pltpu.HBM if out_held else pltpu.VMEM
    args = [pltpu.with_memory_space_constraint(a, space(k)) for k, a in enumerate(args)]
    moved = sum(int(np.prod(a.shape)) * a.dtype.itemsize for a in args)
    return pl.pallas_call(
        functools.partial(kernel, d),
        out_shape=tuple(out_space(s, t) for s, t in outs),
        in_specs=[pl.BlockSpec(memory_space=space(k)) for k in range(len(args))],
        out_specs=tuple(pl.BlockSpec(memory_space=out_space) for _ in outs),
        scratch_shapes=scratch,
        input_output_aliases=aliases or {},
        compiler_params=pltpu.CompilerParams(vmem_limit_bytes=24 * 2**20),
        cost_estimate=pl.CostEstimate(flops=flops, bytes_accessed=moved, transcendentals=0),
        name=kernel.__name__,
    )(*args)


def on_device(sizes, adj, source, velocity, sound, couple, precond, codes, mask, table, gain):
    shape = adj.shape
    d = Dims(shape)
    V, X, W, Z, B, n = d.V, d.X, d.W, d.Z, d.B, d.n
    inputs = [
        adj.reshape(d.rows, Z),
        velocity.reshape(3 * X * W, Z),
        sound.reshape(X * W, Z),
        couple.transpose(0, 2, 1, 3),
        precond,
        codes,
        mask,
        table,
        gain.reshape(1, -1),
    ]
    source = source.reshape(V, X * W, Z)
    faces = [((B, Z), F32)] * 2 + [((d.wall_rows, Z), F32)] * 2 + [((d.span_groups * W, Z), F32)]
    field, scalar = ((d.rows, Z), F32), ((X * W, Z), F32)
    planes = ((V, X * W, Z), F32)
    sems = lambda *counts: pltpu.SemaphoreType.DMA(counts)
    *kept, s_a, s_b, w_a, w_b, z = call(
        pack_kernel,
        d,
        [(a.shape, a.dtype) for a in inputs] + faces,
        0,
        inputs,
        held=range(len(inputs)),
        scratch=[sems(len(inputs) + 2)],
    )
    adj, velocity, sound = kept[:3]
    made = [
        ((6 * n, 3 * B), BF16),
        ((n, 6 * d.wall_k), BF16),
        ((n, 3 * B), BF16),
        ((X * d.stack, Z), F32),
    ]
    room = [pltpu.VMEM((7 * d.stack, 3 * B), F32), pltpu.VMEM((2 * d.stack, 6 * d.wall_k), F32)]
    params = kept[3:]
    *matrices, s_a, s_b, w_a, w_b, z = call(
        early_kernel,
        d,
        made + faces,
        0,
        params + [s_a, s_b, w_a, w_b, z],
        scratch=room,
        aliases={len(params) + k: len(made) + k for k in range(5)},
    )
    got = swap_lines(sizes, s_a, s_b, w_a, w_b, z)
    partial, rs, mk, mw, pk, wall_coef = call(
        first_local_kernel,
        d,
        [field, scalar] + made,
        10**9,
        [adj, source, velocity, sound] + params + matrices,
        scratch=room,
        aliases={4 + len(params) + k: 2 + k for k in range(len(made))},
    )
    s0, s1, w0, w1, zl, zr = got
    edge = ((len(d.edges) * n, Z), F32)
    inner, rs, rates, held, w_a, w_b, z = call(
        first_inner_kernel,
        d,
        [field, scalar, ((2 * X * W, Z), F32), edge] + faces[2:],
        10**8,
        [partial, adj, rs, velocity, sound, w0, w1, zl, zr, mk, mw, pk],
    )
    adj1, rs, w_a, w_b, z, stream_rates, s_a, s_b = call(
        first_stream_kernel,
        d,
        [field, scalar] + faces[2:] + [((2 * W, Z), F32)] + faces[:2],
        10**7,
        [held, adj, rs, velocity, sound, s0, s1, mk, pk, inner, w_a, w_b, z],
        aliases={9: 0, 2: 1, 10: 2, 11: 3, 12: 4},
    )
    s0, s1, w0, w1, zl, zr = swap_lines(sizes, s_a, s_b, w_a, w_b, z)
    (partial,) = call(
        later_local_kernel,
        d,
        [field],
        10**9,
        [adj1, source, velocity, sound, rs, mk, wall_coef],
    )
    inner, inner_residual, held = call(
        later_inner_kernel,
        d,
        [planes, planes, edge],
        10**8,
        [partial, adj1, rs, rates, w1, w0, zl, zr, mk, mw, pk],
    )
    edge = ((V, len(d.edges) * W, Z), F32)
    adj2, residual = call(
        later_stream_kernel,
        d,
        [planes, planes],
        10**7,
        [held, adj1, rs, stream_rates, s0, s1, mk, pk, inner, inner_residual],
        scratch=[pltpu.VMEM(*edge), pltpu.VMEM(*edge), sems(2 + 2 * len(d.edges))],
        out_held=True,
    )
    return adj2.reshape(shape), residual.reshape(shape)


def solution(mesh):
    sizes = tuple(mesh.shape[a] for a in AXES)
    field = P(None, "stream", "wall", "span")
    return jax.shard_map(
        functools.partial(on_device, sizes),
        mesh=mesh,
        in_specs=(field, field, field, P("stream", "wall", "span")) + (P(),) * 6,
        out_specs=(field, field),
        check_vma=False,
    )
```

```python
import functools

import jax
import jax.numpy as jnp
import numpy as np
from jax import lax
from jax.experimental import pallas as pl
from jax.experimental.pallas import tpu as pltpu
from jax.sharding import PartitionSpec as P

AXES = ("stream", "span", "wall")
F32 = jnp.float32
BF16 = jnp.bfloat16


class Dims:
    def __init__(self, shape):
        self.V, self.X, self.W, self.Z = shape
        self.G = self.V + 1
        while self.G * self.W % 16:
            self.G += 1
        self.B = self.G * self.W
        self.n = self.V * self.W
        self.rows = self.n * self.X
        self.edges = sorted({0, self.X - 1})
        self.inner = range(1, self.X - 1)
        self.wall_k = -(-self.G // 8) * 8
        self.wall_rows, self.later_wall_rows = [
            -(-((self.X - 1) * g + self.wall_k) // 8) * 8 for g in (self.G, self.V)
        ]
        self.stack = -(-self.V // 8) * 8
        self.per = self.Z // (2 * self.X)
        self.span_groups = -(-(self.V + 1) // self.per)

    def block(self, group, x):
        return pl.ds((group * self.X + x) * self.W, self.W)

    def rows_at(self, x, w):
        return pl.ds(x * self.W + w, self.V, stride=self.X * self.W)

    def plane(self, ref, x):
        return jnp.concatenate([ref[self.block(v, x), :] for v in range(self.V)], axis=0)

    def store_plane(self, ref, x, value):
        for v in range(self.V):
            ref[self.block(v, x), :] = value[v * self.W : (v + 1) * self.W]

    def plane3(self, ref, x):
        return ref[:, x * self.W : (x + 1) * self.W, :].reshape(self.n, self.Z)

    def planes_at(self, start, count):
        return (slice(None), pl.ds(start * self.W, count * self.W), slice(None))

    def each(self, factor):
        return jnp.concatenate([factor] * self.V, axis=0)


def lanes(d, rows):
    return lax.broadcasted_iota(jnp.int32, (rows, d.Z), 1)


def row_ids(d):
    return lax.broadcasted_iota(jnp.int32, (d.W, d.Z), 0)


def radius_at(d, vel, snd, direction, x):
    return jnp.abs(vel[d.block(direction, x), :]) + snd[d.block(0, x), :]


def split3(value):
    high = value.astype(BF16)
    low = (value - high.astype(F32)).astype(BF16)
    return jnp.concatenate([high, low, high], axis=0)


def padded_plane(d, value):
    extra = d.B - value.shape[0]
    if not extra:
        return value
    return jnp.concatenate([value, jnp.zeros((extra, value.shape[1]), F32)], axis=0)


def dot(a, b):
    return jnp.dot(a, b, preferred_element_type=F32)


def pack_stream(d, block_of, radius_of, s_a, s_b):
    W, even = d.W, parity("stream")
    for g in range(d.V if radius_of is None else d.G):
        if g < d.V:
            first, last = block_of(g, 0), block_of(g, d.X - 1)
        elif g == d.V and radius_of is not None:
            first, last = radius_of(0, 0), radius_of(0, d.X - 1)
        else:
            first = last = jnp.zeros((W, d.Z), F32)
        s_a[g * W : (g + 1) * W, :] = jnp.where(even, last, first)
        s_b[g * W : (g + 1) * W, :] = jnp.where(even, first, last)


def pack_span(d, planes, block_of, radius_of, given, z_out, groups=None):
    V, X, W, Z = d.V, d.X, d.W, d.Z
    pair = lanes(d, W) // 2
    for q in range(d.span_groups) if groups is None else groups:
        rows = pl.ds(q * W, W)
        group = jnp.zeros((W, Z), F32) if given is None else given[rows, :]
        for v in range(q * d.per, min(V + 1, (q + 1) * d.per)):
            if v == V and radius_of is None:
                continue
            for x in planes:
                value = block_of(v, x) if v < V else radius_of(2, x)
                spot = X * (v % d.per) + x
                group = jnp.where(pair == spot, pltpu.roll(value, (2 * spot + 1) % Z, 1), group)
        z_out[rows, :] = group


def pack_walls(d, planes, adj, radius_of, w_a, w_b):
    V, X, W, Z = d.V, d.X, d.W, d.Z
    G = V if radius_of is None else d.G
    even = parity("wall")
    tail = jnp.zeros((max(G - V, 1), Z), F32)
    rest = w_a.shape[0] - X * G
    for x in planes:
        first, last = adj[d.rows_at(x, 0), :], adj[d.rows_at(x, W - 1), :]
        w_a[x * G : x * G + V, :] = jnp.where(even, last, first)
        w_b[x * G : x * G + V, :] = jnp.where(even, first, last)
        if G - V > 1:
            w_a[x * G + V : (x + 1) * G, :] = tail
            w_b[x * G + V : (x + 1) * G, :] = tail
        if radius_of is not None:
            radius = radius_of(1, x)
            first, last = radius[:1], radius[W - 1 :]
            w_a[x * G + V : x * G + V + 1, :] = jnp.where(even, last, first)
            w_b[x * G + V : x * G + V + 1, :] = jnp.where(even, first, last)
    if X - 1 in planes:
        w_a[X * G :, :] = jnp.zeros((rest, Z), F32)
        w_b[X * G :, :] = jnp.zeros((rest, Z), F32)


def parity(axis):
    return lax.rem(lax.axis_index(axis), 2) == 0


def pack_kernel(d, *refs):
    count = (len(refs) - 6) // 2
    held, kept = refs[:count], refs[count : 2 * count]
    s_a, s_b, w_a, w_b, z_out, sems = refs[2 * count :]
    adj, vel, snd = kept[:3]
    groups = -(-d.span_groups // 2)
    size = d.X * d.W
    front = min(d.V, groups * d.per) * size
    parts = [pl.ds(0, front), pl.ds(front, d.rows - front)] if front < d.rows else [pl.ds(0, front)]
    copies = [
        pltpu.make_async_copy(held[0].at[part], adj.at[part], sems.at[count + k])
        for k, part in enumerate(parts)
    ]
    copies += [pltpu.make_async_copy(held[k], kept[k], sems.at[k]) for k in range(1, count)]
    for copy in copies:
        copy.start()
    copies[0].wait()
    block_of = lambda v, x: adj[d.block(v, x), :]
    radius_of = functools.partial(radius_at, d, vel, snd)
    pack_span(d, range(d.X), block_of, radius_of, None, z_out, range(groups))
    for copy in copies[1:]:
        copy.wait()
    pack_span(d, range(d.X), block_of, radius_of, None, z_out, range(groups, d.span_groups))
    pack_stream(d, block_of, radius_of, s_a, s_b)
    pack_walls(d, range(d.X), adj, radius_of, w_a, w_b)


def make_matrices(d, couple, precond, mk, mw, pk, wide, wide_wall):
    V, W, B, n, K, S = d.V, d.W, d.B, d.n, d.wall_k, d.stack
    gap = jnp.zeros((V, S - V), F32)
    blocks = [couple[k // 2, :, k % 2, :] for k in range(6)] + [precond[...].T]
    blocks = [piece for m in blocks for piece in ((m, gap) if S > V else (m,))]
    blocks = jnp.concatenate(blocks, axis=1)
    high = blocks.astype(BF16).astype(F32)
    gap = jnp.zeros((S - V, 7 * S), F32)
    pieces = (high, gap, blocks - high, gap) if S > V else (high, blocks - high)
    blocks = jnp.concatenate(pieces, axis=0).astype(BF16)
    dims = (((0,), (0,)), ((), ()))

    def spread(some, width, keep):
        row = lax.broadcasted_iota(jnp.int32, (2 * S, 3 * width), 0)
        col = lax.broadcasted_iota(jnp.int32, (2 * S, 3 * width), 1)
        part = keep(lax.rem(col, width), jnp.where(row < S, row, row - S))
        part = part & ((row < S) == (col < 2 * width))
        return lax.dot_general(some, part.astype(BF16), dims, preferred_element_type=F32)

    wide[...] = spread(blocks, B, lambda col, v: col // W == v)
    sides = []
    for side in range(2):
        some = blocks[:, (2 + side) * S : (3 + side) * S]
        sides.append(spread(some, 2 * K, lambda col, v: col - side * K == v))
    wide_wall[...] = jnp.concatenate(sides, axis=0)
    row = lax.broadcasted_iota(jnp.int32, (W, 3 * B), 0)
    col = lax.rem(lax.broadcasted_iota(jnp.int32, (W, 3 * B), 1), W)
    same, lower, upper = [(col - row == k).astype(F32) for k in (0, -1, 1)]

    def rows(k):
        mask = {2: lower, 3: upper}.get(k, same)
        return [wide[pl.ds(k * S + v, 1), :] * mask for v in range(V)]

    for k in range(0, 6, 2):
        both = jnp.concatenate(rows(k) + rows(k + 1), axis=0)
        mk[k * n : (k + 2) * n, :] = both.astype(BF16)
    pk[...] = jnp.concatenate(rows(6), axis=0).astype(BF16)
    row = lax.broadcasted_iota(jnp.int32, (W, 6 * K), 0)
    first, last = (row == 0).astype(F32), (row == W - 1).astype(F32)
    pieces = [
        wide_wall[pl.ds(v, 1), :] * first + wide_wall[pl.ds(S + v, 1), :] * last for v in range(V)
    ]
    mw[...] = jnp.concatenate(pieces, axis=0).astype(BF16)


def make_wall(d, codes, mask, table, gain, wall_out):
    X, Z, V, S = d.X, d.Z, d.V, d.stack
    place = lax.axis_index("stream")
    lane0 = pl.multiple_of(lax.axis_index("span") * Z, Z)
    kinds = table.shape[0]

    def window(ref):
        value = ref[:X, pl.ds(lane0, Z)]
        for s in range(1, lax.axis_size("stream")):
            value = jnp.where(place == s, ref[s * X : (s + 1) * X, pl.ds(lane0, Z)], value)
        return value

    code, spall = window(codes), window(mask).astype(F32)
    column = lambda values: jnp.broadcast_to(values.T, (V, Z))
    columns = [column(table[k : k + 1, :]) for k in range(kinds)]
    gains = column(gain[...])
    for x in range(X):
        here = jnp.broadcast_to(code[x : x + 1], (V, Z))
        coef = columns[kinds - 1]
        for k in range(kinds - 1):
            coef = jnp.where(here == k, columns[k], coef)
        wall_out[x * S : x * S + V, :] = coef + gains * spall[x : x + 1]


def sweep_local(d, adj, src, vel, snd, mk, wall_coef, rates_of, out, rs_out):
    X, W, Z, n = d.X, d.W, d.Z, d.n
    lane, row = lanes(d, W), row_ids(d)
    wall_flag = (lax.axis_index("wall") == 0).astype(F32)
    half = [[0.5 * radius_at(d, vel, snd, k, x) for x in range(X)] for k in range(3)]
    sums = {}

    def begin(x):
        total = 1.0
        for neighbour in (x - 1, x + 1):
            total = total + half[0][x]
            if 0 <= neighbour < X:
                total = total + half[0][neighbour]
        rates = []
        for edge, turn in ((0, 1), (W - 1, W - 1)):
            near = jnp.where(row == edge, 0.0, pltpu.roll(half[1][x], turn, 0))
            rates.append(half[1][x] + near)
            total = total + rates[-1]
        for edge, turn in ((0, 1), (Z - 1, Z - 1)):
            near = jnp.where(lane == edge, 0.0, pltpu.roll(half[2][x], turn, 1))
            total = total + half[2][x] + near
            rates.append(jnp.where(lane == edge, 0.0, half[2][x] + near))
        if rates_of is None:
            rs_out[d.block(0, x), :] = total
        else:
            total = rates_of[d.block(0, x), :]
        sums[x] = d.plane3(src, x) - d.each(total) * d.plane(adj, x)
        return rates

    def subtract(x, rate, value):
        sums[x] = sums[x] - d.each(rate) * value

    done = 0
    step = 2
    begun = {}
    for start in range(0, X, step):
        here = list(range(start, min(X, start + step)))
        for x in range(max(0, start - 1), min(X, start + step + 1)):
            if x not in begun:
                begun[x] = begin(x)
        right = split3(jnp.concatenate([padded_plane(d, d.plane(adj, x)) for x in here], axis=1))
        for k in (0, 2, 4):
            both = dot(mk[k * n : (k + 2) * n, :], right)
            for side in range(2):
                for offset, x in enumerate(here):
                    value = both[side * n : (side + 1) * n, offset * Z : (offset + 1) * Z]
                    if k == 0:
                        to = x + 1 - 2 * side
                        if 0 <= to < X:
                            subtract(to, half[0][x] + half[0][to], value)
                    elif k == 2:
                        subtract(x, begun[x][side], value)
                    else:
                        turn = (1, Z - 1)[side]
                        subtract(x, begun[x][2 + side], pltpu.roll(value, turn, 1))
        while done < X and (done < here[-1] or here[-1] == X - 1):
            d.store_plane(out, done, sums.pop(done))
            done += 1
    for x in range(X):
        spot = d.rows_at(x, 0)
        factor = wall_flag * (2.0 * half[1][x][:1])
        coef = wall_coef[x * d.stack : x * d.stack + d.V, :]
        out[spot, :] = out[spot, :] - factor * coef * adj[spot, :]


def early():
    return 2 * lax.axis_index("stream") < lax.axis_size("stream")


def early_kernel(d, couple, precond, codes, mask, table, gain, *refs):
    mk, mw, pk, wall_coef = refs[5:9]
    wide, wide_wall = refs[-2:]

    @pl.when(early())
    def _():
        make_matrices(d, couple, precond, mk, mw, pk, wide, wide_wall)
        make_wall(d, codes, mask, table, gain, wall_coef)


def first_local_kernel(
    d, adj, src, vel, snd, couple, precond, codes, mask, table, gain, _mk, _mw, _pk, _wall_coef,
    out, rs, mk, mw, pk, wall_coef, wide, wide_wall,
):
    @pl.when(jnp.logical_not(early()))
    def _():
        make_matrices(d, couple, precond, mk, mw, pk, wide, wide_wall)
        make_wall(d, codes, mask, table, gain, wall_coef)

    sweep_local(d, adj, src, vel, snd, mk, wall_coef, None, out, rs)


def later_local_kernel(d, adj, src, vel, snd, rs, mk, wall_coef, out):
    sweep_local(d, adj, src, vel, snd, mk, wall_coef, rs, out, None)


def neighbours(axis):
    index = lax.axis_index(axis)
    return (index > 0).astype(F32), (index < lax.axis_size(axis) - 1).astype(F32)


def wall_terms(d, w0, w1, mw, G):
    X, W, Z = d.X, d.W, d.Z
    even = parity("wall")
    has_low, has_high = neighbours("wall")
    row = row_ids(d)

    def received(start, count):
        a, b = w0[pl.ds(start, count), :], w1[pl.ds(start, count), :]
        return jnp.where(even, b, a) * has_low, jnp.where(even, a, b) * has_high

    products = {}
    for start in range(0, X, 2):
        here = list(range(start, min(X, start + 2)))
        right = [jnp.concatenate(received(x * G, d.wall_k), axis=0) for x in here]
        value = dot(mw[...], split3(jnp.concatenate(right, axis=1)))
        for k, x in enumerate(here):
            products[x] = value[:, k * Z : (k + 1) * Z]

    def radius(x):
        first, last = received(x * G + d.V, 1)
        return jnp.where(row == 0, first, jnp.where(row == W - 1, last, 0.0))

    return products.get, radius


def span_terms(d, zl, zr, mk):
    V, X, W, Z, n = d.V, d.X, d.W, d.Z, d.n
    even = lax.rem(lanes(d, W), 2) == 0
    pieces = []
    for v in range(V + 1):
        q = pl.ds((v // d.per) * W, W)
        value = jnp.where(even, zl[q, :], zr[q, :])
        turn = (Z - 2 * X * (v % d.per)) % Z
        pieces.append(pltpu.roll(value, turn, 1) if turn else value)
    radius = jnp.where(even, pieces[V], pltpu.roll(pieces[V], Z - 2, 1))
    pieces += [jnp.zeros((W, Z), F32)] * (d.G - V - 1)
    both = dot(mk[4 * n :], split3(jnp.concatenate(pieces, axis=0)))
    even = lax.rem(lanes(d, n), 2) == 0
    span = jnp.where(even, both[:n], pltpu.roll(both[n:], Z - 2, 1))
    at = lambda value, x: pltpu.roll(value, (Z - 2 * x) % Z, 1) if x else value
    return lambda x: at(span, x), lambda x: at(radius, x)


def update_planes(d, planes, residual_of, adj, rs_of, pk, put):
    Z = d.Z

    def finish(here, residuals, update):
        for k, x in enumerate(here):
            inverse = 1.0 / rs_of(x)
            new = d.plane(adj, x) + update[:, k * Z : (k + 1) * Z] * d.each(inverse)
            put(x, new, residuals[k])

    waiting = None
    for start in range(0, len(planes), 2):
        here = planes[start : start + 2]
        residuals = [residual_of(x) for x in here]
        right = jnp.concatenate([padded_plane(d, r) for r in residuals], axis=1)
        update = dot(pk[...], split3(right))
        if waiting:
            finish(*waiting)
        waiting = here, residuals, update
    if waiting:
        finish(*waiting)


def first_inner_kernel(
    d, partial, adj, rs, vel, snd, w0, w1, zl, zr, mk, mw, pk,
    new_adj, rs_full, rates, edge, w_a, w_b, z_out,
):
    V, X, W, Z, n = d.V, d.X, d.W, d.Z, d.n
    span, span_radius = span_terms(d, zl, zr, mk)
    wall, wall_radius = wall_terms(d, w0, w1, mw, d.G)
    lane, row = lanes(d, W), row_ids(d)
    edge_lane = (lane == 0) | (lane == Z - 1)
    edge_row = (row == 0) | (row == W - 1)
    totals = {}

    def residual_of(x):
        from_wall = 0.5 * wall_radius(x)
        from_span = jnp.where(edge_lane, 0.5 * span_radius(x), 0.0)
        rate_wall = jnp.where(edge_row, 0.5 * radius_at(d, vel, snd, 1, x) + from_wall, 0.0)
        rate_span = jnp.where(edge_lane, 0.5 * radius_at(d, vel, snd, 2, x) + from_span, 0.0)
        correction = from_wall + from_span
        totals[x] = rs[d.block(0, x), :] + correction
        rates[d.block(0, x), :] = rate_wall
        rates[d.block(1, x), :] = rate_span
        rs_full[d.block(0, x), :] = totals[x]
        result = d.plane(partial, x) - d.each(correction) * d.plane(adj, x)
        return result - d.each(rate_wall) * wall(x) - d.each(rate_span) * span(x)

    for k, x in enumerate(d.edges):
        edge[k * n : (k + 1) * n, :] = residual_of(x)
    put = lambda x, new, _: d.store_plane(new_adj, x, new)
    update_planes(d, list(d.inner), residual_of, adj, totals.get, pk, put)
    pack_walls(d, d.inner, new_adj, None, w_a, w_b)
    pack_span(d, d.inner, lambda v, x: new_adj[d.block(v, x), :], None, None, z_out)


def later_inner_kernel(
    d, partial, adj, rs_full, rates, w1, w0, zl, zr, mk, mw, pk, new_adj, residual, edge
):
    W, n = d.W, d.n
    span, _ = span_terms(d, zl, zr, mk)
    wall, _ = wall_terms(d, w0, w1, mw, d.V)

    def residual_of(x):
        result = d.plane(partial, x) - d.each(rates[d.block(0, x), :]) * wall(x)
        return result - d.each(rates[d.block(1, x), :]) * span(x)

    def put(x, new, res):
        new_adj[d.planes_at(x, 1)] = new.reshape(d.V, W, d.Z)
        residual[d.planes_at(x, 1)] = res.reshape(d.V, W, d.Z)

    for k, x in enumerate(d.edges):
        edge[k * n : (k + 1) * n, :] = residual_of(x)
    rs_of = lambda x: rs_full[d.block(0, x), :]
    update_planes(d, list(d.inner), residual_of, adj, rs_of, pk, put)


def stream_terms(d, s0, s1, mk):
    n, Z = d.n, d.Z
    even = parity("stream")
    has_low, has_high = neighbours("stream")
    low = jnp.where(even, s1[...], s0[...]) * has_low
    high = jnp.where(even, s0[...], s1[...]) * has_high
    both = dot(mk[: 2 * n], split3(padded_plane(d, jnp.concatenate([low, high], axis=1))))
    return (both[:n, :Z], both[n:, Z:]), [v[n : n + d.W] if v.shape[0] > n else None for v in (low, high)]


def first_stream_kernel(
    d, edge, adj, rs, vel, snd, s0, s1, mk, pk, inner, w_in0, w_in1, z_in,
    new_adj, rs_full, w_a, w_b, z_out, rates, s_a, s_b,
):
    X, W, n = d.X, d.W, d.n
    products, received = stream_terms(d, s0, s1, mk)
    totals = {}

    def residual_of(x):
        k = d.edges.index(x)
        result = edge[k * n : (k + 1) * n, :]
        totals[x] = rs[d.block(0, x), :]
        for side, at in enumerate((0, X - 1)):
            if x == at:
                rate = 0.5 * (radius_at(d, vel, snd, 0, x) + received[side])
                rates[side * W : (side + 1) * W, :] = rate
                totals[x] = totals[x] + 0.5 * received[side]
                result = result - d.each(0.5 * received[side]) * d.plane(adj, x)
                result = result - d.each(rate) * products[side]
        rs_full[d.block(0, x), :] = totals[x]
        return result

    planes = {}

    def put(x, new, _):
        d.store_plane(new_adj, x, new)
        planes[x] = new

    update_planes(d, d.edges, residual_of, adj, totals.get, pk, put)
    block_of = lambda v, x: planes[x][v * W : (v + 1) * W]
    pack_stream(d, block_of, None, s_a, s_b)
    pack_span(d, d.edges, block_of, None, z_in, z_out)
    pack_walls(d, d.edges, new_adj, None, w_a, w_b)


def later_stream_kernel(
    d, edge, adj, rs_full, rates, s0, s1, mk, pk, inner_adj, inner_residual,
    new_adj, residual, edge_adj, edge_residual, sems,
):
    X, W, Z, n = d.X, d.W, d.Z, d.n
    copies = []

    def store(source, target, part, here):
        copy = pltpu.make_async_copy(source.at[here], target.at[part], sems.at[len(copies)])
        copy.start()
        copies.append(copy)

    if len(d.inner):
        part = d.planes_at(1, len(d.inner))
        store(inner_residual, residual, part, part)
        store(inner_adj, new_adj, part, part)
    products, _ = stream_terms(d, s0, s1, mk)

    def residual_of(x):
        k = d.edges.index(x)
        result = edge[k * n : (k + 1) * n, :]
        for side, at in enumerate((0, X - 1)):
            if x == at:
                result = result - d.each(rates[side * W : (side + 1) * W, :]) * products[side]
        return result

    def put(x, new, res):
        here = d.planes_at(d.edges.index(x), 1)
        for value, held, target in (
            (res, edge_residual, residual),
            (new, edge_adj, new_adj),
        ):
            held[here] = value.reshape(d.V, W, Z)
            store(held, target, d.planes_at(x, 1), here)

    rs_of = lambda x: rs_full[d.block(0, x), :]
    update_planes(d, d.edges, residual_of, adj, rs_of, pk, put)
    for copy in copies:
        copy.wait()


def exchange_pairs(sizes, axis, odd, spare):
    ids = np.arange(int(np.prod(sizes))).reshape(sizes)
    pairs = []
    for at in np.ndindex(*sizes):
        to = list(at)
        step = 1 if (at[axis] - odd) % 2 == 0 else -1
        if at[axis] >= odd and 0 <= at[axis] + step < sizes[axis]:
            to[axis] += step
        elif spare == axis and sizes[axis] % 2 == 0:
            to[axis] = sizes[axis] - 1 - at[axis]
        elif spare != axis and (at[spare] ^ 1) < sizes[spare]:
            to[spare] ^= 1
        else:
            continue
        pairs.append((int(ids[at]), int(ids[tuple(to)])))
    return pairs


def swap_lines(sizes, s_a, s_b, w_a, w_b, z):
    move = lambda value, pairs: lax.ppermute(value, AXES, pairs)
    s0 = move(s_a, exchange_pairs(sizes, 0, 0, 2))
    s1 = move(s_b, exchange_pairs(sizes, 0, 1, 2))
    w1 = move(w_b, exchange_pairs(sizes, 2, 1, 2))
    w0 = move(w_a, exchange_pairs(sizes, 2, 0, 1))
    peers = sizes[1]
    if peers == 1:
        zl = zr = z
    elif peers == 2:
        zl = zr = lax.ppermute(z, "span", [(0, 1), (1, 0)])
    else:
        up = [(i, (i + 1) % peers) for i in range(peers)]
        zl = lax.ppermute(z, "span", up)
        zr = lax.ppermute(z, "span", [(j, i) for i, j in up])
    return s0, s1, w0, w1, zl, zr


def call(kernel, d, outs, flops, args, held=(), scratch=(), out_held=False, aliases=None):
    space = lambda k: pltpu.HBM if k in held else pltpu.VMEM
    out_space = pltpu.HBM if out_held else pltpu.VMEM
    args = [pltpu.with_memory_space_constraint(a, space(k)) for k, a in enumerate(args)]
    moved = sum(int(np.prod(a.shape)) * a.dtype.itemsize for a in args)
    return pl.pallas_call(
        functools.partial(kernel, d),
        out_shape=tuple(out_space(s, t) for s, t in outs),
        in_specs=[pl.BlockSpec(memory_space=space(k)) for k in range(len(args))],
        out_specs=tuple(pl.BlockSpec(memory_space=out_space) for _ in outs),
        scratch_shapes=scratch,
        input_output_aliases=aliases or {},
        compiler_params=pltpu.CompilerParams(vmem_limit_bytes=24 * 2**20),
        cost_estimate=pl.CostEstimate(flops=flops, bytes_accessed=moved, transcendentals=0),
        name=kernel.__name__,
    )(*args)


def on_device(sizes, adj, source, velocity, sound, couple, precond, codes, mask, table, gain):
    shape = adj.shape
    d = Dims(shape)
    V, X, W, Z, B, n = d.V, d.X, d.W, d.Z, d.B, d.n
    inputs = [
        adj.reshape(d.rows, Z),
        velocity.reshape(3 * X * W, Z),
        sound.reshape(X * W, Z),
        couple.transpose(0, 2, 1, 3),
        precond,
        codes,
        mask,
        table,
        gain.reshape(1, -1),
    ]
    source = source.reshape(V, X * W, Z)
    faces = [((B, Z), F32)] * 2 + [((d.wall_rows, Z), F32)] * 2 + [((d.span_groups * W, Z), F32)]
    later = [((n, Z), F32)] * 2 + [((d.later_wall_rows, Z), F32)] * 2 + faces[4:]
    field, scalar = ((d.rows, Z), F32), ((X * W, Z), F32)
    planes = ((V, X * W, Z), F32)
    sems = lambda *counts: pltpu.SemaphoreType.DMA(counts)
    *kept, s_a, s_b, w_a, w_b, z = call(
        pack_kernel,
        d,
        [(a.shape, a.dtype) for a in inputs] + faces,
        0,
        inputs,
        held=range(len(inputs)),
        scratch=[sems(len(inputs) + 2)],
    )
    adj, velocity, sound = kept[:3]
    made = [
        ((6 * n, 3 * B), BF16),
        ((n, 6 * d.wall_k), BF16),
        ((n, 3 * B), BF16),
        ((X * d.stack, Z), F32),
    ]
    room = [pltpu.VMEM((7 * d.stack, 3 * B), F32), pltpu.VMEM((2 * d.stack, 6 * d.wall_k), F32)]
    params = kept[3:]
    *matrices, s_a, s_b, w_a, w_b, z = call(
        early_kernel,
        d,
        made + faces,
        0,
        params + [s_a, s_b, w_a, w_b, z],
        scratch=room,
        aliases={len(params) + k: len(made) + k for k in range(5)},
    )
    got = swap_lines(sizes, s_a, s_b, w_a, w_b, z)
    partial, rs, mk, mw, pk, wall_coef = call(
        first_local_kernel,
        d,
        [field, scalar] + made,
        10**9,
        [adj, source, velocity, sound] + params + matrices,
        scratch=room,
        aliases={4 + len(params) + k: 2 + k for k in range(len(made))},
    )
    s0, s1, w0, w1, zl, zr = got
    edge = ((len(d.edges) * n, Z), F32)
    inner, rs, rates, held, w_a, w_b, z = call(
        first_inner_kernel,
        d,
        [field, scalar, ((2 * X * W, Z), F32), edge] + later[2:],
        10**8,
        [partial, adj, rs, velocity, sound, w0, w1, zl, zr, mk, mw, pk],
    )
    adj1, rs, w_a, w_b, z, stream_rates, s_a, s_b = call(
        first_stream_kernel,
        d,
        [field, scalar] + later[2:] + [((2 * W, Z), F32)] + later[:2],
        10**7,
        [held, adj, rs, velocity, sound, s0, s1, mk, pk, inner, w_a, w_b, z],
        aliases={9: 0, 2: 1, 10: 2, 11: 3, 12: 4},
    )
    s0, s1, w0, w1, zl, zr = swap_lines(sizes, s_a, s_b, w_a, w_b, z)
    (partial,) = call(
        later_local_kernel,
        d,
        [field],
        10**9,
        [adj1, source, velocity, sound, rs, mk, wall_coef],
    )
    inner, inner_residual, held = call(
        later_inner_kernel,
        d,
        [planes, planes, edge],
        10**8,
        [partial, adj1, rs, rates, w1, w0, zl, zr, mk, mw, pk],
    )
    edge = ((V, len(d.edges) * W, Z), F32)
    adj2, residual = call(
        later_stream_kernel,
        d,
        [planes, planes],
        10**7,
        [held, adj1, rs, stream_rates, s0, s1, mk, pk, inner, inner_residual],
        scratch=[pltpu.VMEM(*edge), pltpu.VMEM(*edge), sems(2 + 2 * len(d.edges))],
        out_held=True,
    )
    return adj2.reshape(shape), residual.reshape(shape)


def solution(mesh):
    sizes = tuple(mesh.shape[a] for a in AXES)
    field = P(None, "stream", "wall", "span")
    return jax.shard_map(
        functools.partial(on_device, sizes),
        mesh=mesh,
        in_specs=(field, field, field, P("stream", "wall", "span")) + (P(),) * 6,
        out_specs=(field, field),
        check_vma=False,
    )
```
